32 devices in a mesh: gx: 4 (over x, core), gy: 8 (over z, y).
Axes of the slice: x: 2, y: 2, z: 4, core: 2. Of those that a mesh axis runs over, the one named last changes fastest.
Arguments:
- positions: float32 [4, 8, 3, 32], P('gx', 'gy'), may hold values from 0 to 12, as said below
- features: float32 [4, 8, 32, 128], P('gx', 'gy'), may hold values from -6 to 6
- cotangent: float32 [4, 8, 32, 1152], P('gx', 'gy'), may hold values from -6 to 6
- nbr_src: int32 [4, 8, 5, 5, 32], P('gx', 'gy'), may hold values from 0 to 31
- nbr_tgt: int32 [4, 8, 5, 5, 32], P('gx', 'gy'), may hold values from 0 to 31
- pair_mask: int32 [4, 8, 5, 5, 32], P('gx', 'gy'), may hold values 0 or 1
- pair_species: int32 [4, 8, 5, 5, 32], P('gx', 'gy'), may hold values from 0 to 9
- w_in: float32 [8, 32], replicated, may hold values from -2 to 2
- species_emb: float32 [10, 32], replicated, may hold values from -6 to 6
- w_out: float32 [32, 384], replicated, may hold values from -1 to 1
Outputs:
- pos_grad: float32 [4, 8, 3, 32], P('gx', 'gy')
- feat_grad: float32 [4, 8, 32, 128], P('gx', 'gy')
The draws below stay inside these ranges and needn't reach their ends.
Inputs may be any that keep to these rules, and one draw needn't show every extreme that they name: `positions`: the first two coordinates lie in 0 to 5, the third in 0 to 12.
All inputs are finite; a program needn't handle non-finite values. No bound on the sum of `pair_mask` on one device may be relied on, other than what follows from the above.
Results may differ from the reference program's by a relative error of at most 0.0003.
Values sent between devices are 32-bit elements; how exact they have to be, the bound alone decides.
No kernel may reach another device: no remote copies, remote signals or barrier semaphores. Data moves between devices by JAX's collectives and lax.ppermute only.
A program may use at most 64 MiB of HBM per device.

```python
import math
import jax
import jax.numpy as jnp
from jax import lax

ATOMS = 32
CHANNELS = 128
RBASIS = 8
RHIDDEN = 32
NSPEC = 10
PAIRS = 32
NGX = 4
NGY = 8


def draw_positions(key, part):
    key_plane = jax.random.fold_in(key, 11)
    key_depth = jax.random.fold_in(key, 23)
    plane = jax.random.uniform(key_plane, (NGX, NGY, 2, ATOMS), jnp.float32, 0.0, 5.0)
    depth_extent = float(2 * ATOMS // 5)
    depth = jax.random.uniform(key_depth, (NGX, NGY, 1, ATOMS), jnp.float32, 0.0, depth_extent)
    return jnp.concatenate([plane, depth], axis=2)


def plant(entries, rng, smallest, high):
    place = [jax.random.randint(jax.random.fold_in(rng, axis), (), 0, length) for axis, length in enumerate(entries.shape)]
    longest = entries.shape.index(max(entries.shape))
    neighbour = place[:longest] + [(place[longest] + 1) % entries.shape[longest]] + place[longest + 1:]
    return entries.at[tuple(place)].set(smallest).at[tuple(neighbour)].set(high)


def shard_levels(own_key, dims, cuts, smallest, top_value):
    def one(position, blocks):
        draws = jax.random.uniform(jax.random.fold_in(jax.random.fold_in(own_key, 6), position), (blocks,), jnp.float32, smallest / len(cuts), top_value / len(cuts))
        return jnp.repeat(jnp.exp(draws), dims[position] // blocks).reshape((-1,) + (1,) * (len(dims) - position - 1))

    level = one(*cuts[0])
    for cut in cuts[1:]:
        level = level * one(*cut)
    return level


def centred(rng, shape, width, most, shards=(), kind=jnp.bfloat16):
    entries = width * jax.random.normal(rng, shape, jnp.float32)
    if shards:
        entries = entries * shard_levels(rng, shape, shards, -0.22, 0.18)
    return jnp.clip(entries, -most, most).astype(kind)


def setup_inputs(seed: int = 0) -> dict:
    seeds = jax.random.split(jax.random.key(seed), 11)
    positions = draw_positions(jax.random.fold_in(seeds[10], 71), 0)
    features = centred(seeds[1], (NGX, NGY, ATOMS, CHANNELS), 1.0, 6.0, ((0, 4), (1, 8)), jnp.float32)
    cotangent = centred(seeds[2], (NGX, NGY, ATOMS, 9 * CHANNELS), 1.0, 6.0, ((0, 4), (1, 8)), jnp.float32)
    nbr_src = plant(jax.random.randint(seeds[3], (NGX, NGY, 5, 5, PAIRS), 0, ATOMS), jax.random.fold_in(seeds[3], 1), 0, ATOMS - 1).astype(jnp.int32)
    nbr_tgt = plant(jax.random.randint(seeds[4], (NGX, NGY, 5, 5, PAIRS), 0, ATOMS), jax.random.fold_in(seeds[4], 1), 0, ATOMS - 1).astype(jnp.int32)
    pair_mask = plant((jax.random.randint(seeds[5], (NGX, NGY, 5, 5, PAIRS), 0, 4) < 3).astype(jnp.int32), jax.random.fold_in(seeds[5], 1), 0, 1)
    pair_species = plant(jax.random.randint(seeds[6], (NGX, NGY, 5, 5, PAIRS), 0, NSPEC), jax.random.fold_in(seeds[6], 1), 0, NSPEC - 1).astype(jnp.int32)
    w_in = centred(seeds[7], (RBASIS, RHIDDEN), RBASIS ** -0.5, 2.0, (), jnp.float32)
    species_emb = centred(seeds[8], (NSPEC, RHIDDEN), 1.0, 6.0, (), jnp.float32)
    w_out = centred(seeds[9], (RHIDDEN, 3 * CHANNELS), RHIDDEN ** -0.5, 1.0, (), jnp.float32)
    return dict(positions=positions, features=features, cotangent=cotangent, nbr_src=nbr_src, nbr_tgt=nbr_tgt, pair_mask=pair_mask, pair_species=pair_species, w_in=w_in, species_emb=species_emb, w_out=w_out)


domain_side = 5.0
cutoff = 12.0
soften = 0.25
highest = lax.Precision.HIGHEST

def harmonics(unit):
    unit_x, unit_y, unit_z = (unit[0], unit[1], unit[2])
    root_three = math.sqrt(3.0)
    root_five = math.sqrt(5.0)
    root_fifteen = math.sqrt(15.0)
    return jnp.stack([jnp.ones_like(unit_x), root_three * unit_x, root_three * unit_y, root_three * unit_z, root_fifteen * unit_x * unit_y, root_fifteen * unit_y * unit_z, 0.5 * root_five * (2.0 * unit_z * unit_z - unit_x * unit_x - unit_y * unit_y), root_fifteen * unit_x * unit_z, 0.5 * root_fifteen * (unit_x * unit_x - unit_y * unit_y)], axis=0)

def tile_messages(tgt_pos, src_pos, src_feats, offset, source_index, target_index, live_pair, species, w_in, species_emb, w_out):
    atom_count = tgt_pos.shape[1]
    channels = src_feats.shape[1]
    pair_count = source_index.shape[0]
    relative = jnp.take(src_pos, source_index, axis=1) + offset[:, None] - jnp.take(tgt_pos, target_index, axis=1)
    distance = jnp.sqrt(lax.optimization_barrier(jnp.sum(relative * relative, axis=0)) + soften)
    scaled = distance / cutoff
    envelope = jnp.where(scaled < 1.0, (1.0 - scaled * scaled) ** 2, 0.0) * live_pair.astype(jnp.float32)
    orders = jnp.arange(1, w_in.shape[0] + 1, dtype=jnp.int32).astype(jnp.float32)
    radial_basis = math.sqrt(2.0 / cutoff) * jnp.sin(orders[None, :] * math.pi * scaled[:, None]) / distance[:, None]
    picked = (species[:, None] == jnp.arange(species_emb.shape[0], dtype=jnp.int32)[None, :]).astype(jnp.float32)
    hidden = jax.nn.silu(jnp.dot(radial_basis, w_in, precision=highest) + jnp.dot(picked, species_emb, precision=highest))
    radial = jnp.dot(hidden, w_out, precision=highest).reshape(pair_count, 3, channels) * envelope[:, None, None]
    radial_full = jnp.concatenate([radial[:, 0:1], jnp.repeat(radial[:, 1:2], 3, axis=1), jnp.repeat(radial[:, 2:3], 5, axis=1)], axis=1)
    shapes = harmonics(relative / distance[None, :])
    gathered = jnp.take(src_feats, source_index, axis=0)
    message = radial_full * shapes.T[:, :, None] * gathered[:, None, :]
    return jax.ops.segment_sum(message.reshape(pair_count, 9 * channels), target_index, num_segments=atom_count)

def tile_grads(tgt_pos, src_pos, src_feats, offset, source_index, target_index, live_pair, species, w_in, species_emb, w_out, cot_block):

    def forward(target_xyz, source_xyz, source_vals):
        return tile_messages(target_xyz, source_xyz, source_vals, offset, source_index, target_index, live_pair, species, w_in, species_emb, w_out)
    pullback = jax.vjp(forward, tgt_pos, src_pos, src_feats)[1]
    return pullback(cot_block)

def reference(positions, features, cotangent, nbr_src, nbr_tgt, pair_mask, pair_species, w_in, species_emb, w_out):
    grid_x = positions.shape[0]
    grid_y = positions.shape[1]

    def visit(running, flat_index):
        pos_total, feat_total = running
        cell_a = flat_index // grid_y
        cell_b = flat_index % grid_y
        for row_step in range(-2, 3):
            for col_step in range(-2, 3):
                src_a = (cell_a + row_step) % grid_x
                tgt_b = (cell_b + col_step) % grid_y
                offset = jnp.array([row_step * domain_side, -col_step * domain_side, 0.0], dtype=jnp.float32)
                grads = tile_grads(positions[cell_a, tgt_b], positions[src_a, cell_b], features[src_a, cell_b], offset, nbr_src[cell_a, cell_b, row_step + 2, col_step + 2], nbr_tgt[cell_a, cell_b, row_step + 2, col_step + 2], pair_mask[cell_a, cell_b, row_step + 2, col_step + 2], pair_species[cell_a, cell_b, row_step + 2, col_step + 2], w_in, species_emb, w_out, cotangent[cell_a, tgt_b])
                pos_total = pos_total.at[cell_a, tgt_b].add(grads[0])
                pos_total = pos_total.at[src_a, cell_b].add(grads[1])
                feat_total = feat_total.at[src_a, cell_b].add(grads[2])
        return ((pos_total, feat_total), None)
    start = (jnp.zeros(positions.shape, jnp.float32), jnp.zeros(features.shape, jnp.float32))
    finals = lax.scan(visit, start, jnp.arange(grid_x * grid_y, dtype=jnp.int32))[0]
    return (finals[0], finals[1])
```

```python
import functools
import math

import jax
import jax.numpy as jnp
from jax import lax
from jax.experimental import pallas as pl
from jax.experimental.pallas import tpu as pltpu
from jax.sharding import PartitionSpec as P

domain_side = 5.0
cutoff = 12.0
soften = 0.25
reach = 2
sublanes = 8
f32 = jnp.float32
bf16 = jnp.bfloat16


class Link:
    def __init__(self, step, bit, peers):
        self.step, self.bit, self.peers = step, bit, peers

    def delta(self, i):
        return self.step if self.bit is None else self.step * (1 - 2 * ((i >> self.bit) & 1))

    def fetch(self, value, axis):
        n = self.peers
        return lax.ppermute(value, axis, [((i + self.delta(i)) % n, i) for i in range(n)])

    def give(self, value, axis):
        n = self.peers
        return lax.ppermute(value, axis, [(i, (i + self.delta(i)) % n) for i in range(n)])


def links_of(peers):
    if peers % 4 == 0:
        steps = [(1, 0), (-1, 0), (2, 1)] + ([(-2, 1)] if peers > 4 else [])
    else:
        steps = [(1, None), (-1, None), (2, None), (-2, None)]
    return [Link(step, bit, peers) for step, bit in steps]


def spots_of(links):
    spots = [(0, None, 0)]
    for table, link in enumerate(links):
        spots.append((table + 1, link, 1))
        if link.peers == 4 and abs(link.step) == 2:
            spots.append((table + 1, link, -1))
    return spots


def pieces(x, count):
    out = []
    for _ in range(count):
        out.append(x.astype(bf16).astype(f32))
        x = x - out[-1]
    return out


def dot(a, b):
    return jnp.dot(a, b, preferred_element_type=f32)


def dot_rows(a, b):
    return lax.dot_general(a, b, (((1,), (1,)), ((), ())), preferred_element_type=f32)


def dot_cols(a, b):
    return lax.dot_general(a, b, (((0,), (0,)), ((), ())), preferred_element_type=f32)


def pack_kernel(pos_ref, feat_ref, cot_ref, gx_ref, gy_ref):
    atoms, channels = feat_ref.shape[2:]
    gx_ref[0:atoms] = feat_ref[0, 0]
    gy_ref[0:atoms] = cot_ref[0, 0]
    zero = jnp.zeros((sublanes, channels), f32)
    gx_ref[atoms:] = zero
    gy_ref[atoms:, 0:channels] = zero
    gx_ref[atoms : atoms + 3, 0:atoms] = pos_ref[0, 0]
    gy_ref[atoms : atoms + 3, 0:atoms] = pos_ref[0, 0]


def prep_kernel(
    gx_spots, gy_spots, place_ref, src_ref, tgt_ref, mask_ref, spec_ref, in_ref, emb_ref, out_ref,
    rows_ref, wide_ref, back_ref, first_ref,
):
    atoms = pairs = src_ref.shape[4]
    at_x, at_y = place_ref[0], place_ref[1]
    rows_ref[...] = jnp.zeros(rows_ref.shape, jnp.int32)
    for spot, (_, gy_link, gy_sign) in enumerate(gy_spots):
        step_y = 0 if gy_link is None else gy_sign * gy_link.delta(at_y)
        for slot, (table, gx_link, gx_sign) in enumerate(gx_spots):
            step_x = 0 if gx_link is None else gx_sign * gx_link.delta(at_x)
            lanes = slice(slot * pairs, (slot + 1) * pairs)
            tile = (0, 0, pl.ds(reach + step_x, 1), pl.ds(reach + step_y, 1))
            rows_ref[spot, 0:1, lanes] = src_ref[tile][0, 0:1] + table * atoms
            rows_ref[spot, 1:2, lanes] = tgt_ref[tile][0, 0:1]
            rows_ref[spot, 2:3, lanes] = mask_ref[tile][0, 0:1]
            rows_ref[spot, 3:4, lanes] = spec_ref[tile][0, 0:1]
            rows_ref[spot, 4:5, lanes] = jnp.full((1, pairs), step_x, jnp.int32)
            rows_ref[spot, 5:6, lanes] = jnp.full((1, pairs), -step_y, jnp.int32)
    high, low = pieces(out_ref[...], 2)
    back_ref[...] = jnp.concatenate([high, high, low], axis=1).astype(bf16)
    wide_ref[...] = jnp.concatenate([high, high, low], axis=0).T.astype(bf16)
    orders, hidden = in_ref.shape
    kinds = emb_ref.shape[0]
    spare = first_ref.shape[0] - orders - kinds
    parts = [in_ref[...], emb_ref[...], jnp.zeros((spare, hidden), f32)]
    first_ref[...] = jnp.concatenate(parts, axis=0)


def radial_waves(dist, orders):
    order = (lax.broadcasted_iota(jnp.int32, (orders, 1), 0) + 1).astype(f32)
    turn = order * (dist * (1.0 / cutoff))
    whole = jnp.floor(turn + 0.5)
    part = turn - whole
    sign = 1.0 - 2.0 * (whole - 2.0 * jnp.floor(0.5 * whole))
    square = part * part
    sine = jnp.zeros_like(square)
    for k in (11, 9, 7, 5, 3, 1):
        sine = sine * square + (-1.0) ** (k // 2) * math.pi**k / math.factorial(k)
    cosine = jnp.zeros_like(square)
    for k in (12, 10, 8, 6, 4, 2, 0):
        cosine = cosine * square + (-1.0) ** (k // 2) * math.pi**k / math.factorial(k)
    return order, sign * part * sine, sign * cosine


def spot_grads(rows, cot_ref, src_pos, feats, first, wide, back, orders):
    slots = rows.shape[1]
    sources = feats[0].shape[1]
    atoms = cot_ref.shape[0] - sublanes
    channels = feats[0].shape[0]
    hidden = first.shape[1]

    def onehot(ids, count):
        return jnp.where(lax.broadcasted_iota(jnp.int32, (count, slots), 0) == ids, 1.0, 0.0)

    src_hot = onehot(rows[0:1], sources).astype(bf16)
    tgt_hot32 = onehot(rows[1:2], atoms)
    tgt_hot = tgt_hot32.astype(bf16)
    mask = rows[2:3].astype(f32)
    offset = rows[4:6].astype(f32) * domain_side

    tgt_pos = jnp.concatenate(pieces(cot_ref[atoms:, 0:atoms], 3), axis=0).astype(bf16)
    from_src = dot(src_pos, src_hot)
    from_tgt = dot(tgt_pos, tgt_hot)
    from_src = from_src[0:8] + from_src[8:16] + from_src[16:24]
    from_tgt = from_tgt[0:8] + from_tgt[8:16] + from_tgt[16:24]
    rel = [
        from_src[0:1] + offset[0:1] - from_tgt[0:1],
        from_src[1:2] + offset[1:2] - from_tgt[1:2],
        from_src[2:3] - from_tgt[2:3],
    ]
    dist = jnp.sqrt(rel[0] * rel[0] + rel[1] * rel[1] + rel[2] * rel[2] + soften)
    near = 1.0 / dist
    x, y, z = (r * near for r in rel)
    scaled = dist * (1.0 / cutoff)
    room = jnp.where(scaled < 1.0, 1.0 - scaled * scaled, 0.0)
    env = room * room * mask
    d_env = (-4.0 / cutoff) * scaled * room * mask

    order, sine, cosine = radial_waves(dist, orders)
    norm = math.sqrt(2.0 / cutoff)
    basis = norm * near * sine
    d_basis = norm * near * ((math.pi / cutoff) * order * cosine - sine * near)
    species = onehot(rows[3:4], first.shape[0] - orders)
    before = lax.dot_general(
        first, jnp.concatenate([basis, species], axis=0), (((0,), (0,)), ((), ())),
        precision=lax.Precision.HIGHEST, preferred_element_type=f32,
    )
    gate = 1.0 / (1.0 + jnp.exp(-before))
    act = before * gate
    d_act = gate * (1.0 + before * (1.0 - gate))
    act_high, act_low = pieces(act, 2)
    radial = dot(wide, jnp.concatenate([act_high, act_low, act_high], axis=0).astype(bf16))

    gathered = dot(feats[0], src_hot) + dot(feats[1], src_hot)

    root3, root5, root15 = math.sqrt(3.0), math.sqrt(5.0), math.sqrt(15.0)
    shapes = [
        None, root3 * x, root3 * y, root3 * z, root15 * x * y, root15 * y * z,
        0.5 * root5 * (2.0 * z * z - x * x - y * y), root15 * x * z, 0.5 * root15 * (x * x - y * y),
    ]
    tgt_twice = jnp.concatenate([tgt_hot32, tgt_hot32], axis=0).astype(bf16)
    d_shapes = [None] * 9
    d_radial = []
    through = None
    for low, high in ((0, 1), (1, 4), (4, 9)):
        l = len(d_radial)
        own = radial[l * channels : (l + 1) * channels]
        with_feats = own * gathered
        total = None
        for m in range(low, high):
            block = cot_ref[0:atoms, m * channels : (m + 1) * channels]
            cot = dot_cols(jnp.concatenate(pieces(block, 2), axis=0).astype(bf16), tgt_twice)
            if m:
                d_shapes[m] = jnp.sum(with_feats * cot, axis=0, keepdims=True) * env
                cot = cot * shapes[m]
            total = cot if total is None else total + cot
        d_radial.append(total * gathered)
        own = own * total
        through = own if through is None else through + own
    to_env = jnp.sum(through * gathered, axis=0, keepdims=True)
    through = through * env
    d_radial = jnp.concatenate(d_radial, axis=0) * env
    d_high, d_low = pieces(d_radial, 2)
    d_hidden = dot(back, jnp.concatenate([d_high, d_low, d_high], axis=0).astype(bf16))
    d_before = d_hidden * d_act
    to_basis = lax.dot_general(
        first[0:orders], d_before, (((1,), (0,)), ((), ())),
        precision=lax.Precision.HIGHEST, preferred_element_type=f32,
    )
    d_dist = jnp.sum(to_basis * d_basis, axis=0, keepdims=True) + to_env * d_env

    s = d_shapes
    d_x = root3 * s[1] + root15 * (y * s[4] + z * s[7] + x * s[8]) - root5 * x * s[6]
    d_y = root3 * s[2] + root15 * (x * s[4] + z * s[5] - y * s[8]) - root5 * y * s[6]
    d_z = root3 * s[3] + root15 * (y * s[5] + x * s[7]) + 2.0 * root5 * z * s[6]
    d_dist = d_dist - near * (x * d_x + y * d_y + z * d_z)
    grad = jnp.concatenate(
        [near * d_x + x * d_dist, near * d_y + y * d_dist, near * d_z + z * d_dist,
         jnp.zeros((sublanes - 3, slots), f32)], axis=0,
    )
    grad = jnp.concatenate(pieces(grad, 2), axis=0).astype(bf16)
    pos_src = dot_rows(grad, src_hot)
    pos_tgt = dot_rows(grad, tgt_hot)
    through_high, through_low = (p.astype(bf16) for p in pieces(through, 2))
    feat_src = dot_rows(src_hot, through_high) + dot_rows(src_hot, through_low)
    return pos_src[0:8] + pos_src[8:16], -(pos_tgt[0:8] + pos_tgt[8:16]), feat_src


def main_kernel(gy_spots, gx_count, gy_count, orders, *refs):
    rows_ref, wide_ref, back_ref, first_ref = refs[:4]
    gx_refs = refs[4 : 4 + gx_count]
    gy_refs = refs[4 + gx_count : 4 + gx_count + gy_count]
    outs = refs[4 + gx_count + gy_count :]
    gx_outs, gy_outs, place = outs[:gx_count], outs[gx_count : gx_count + gy_count], outs[-1]
    atoms = gx_refs[0].shape[0] - sublanes
    for table, ref in enumerate(gx_refs):
        place[:, table * atoms : (table + 1) * atoms] = ref[atoms:, 0:atoms]
    src_pos = jnp.concatenate(pieces(place[...], 3), axis=0).astype(bf16)
    feats = jnp.concatenate([ref[0:atoms] for ref in gx_refs], axis=0).T
    feats = [p.astype(bf16) for p in pieces(feats, 2)]
    first, wide, back = first_ref[...], wide_ref[...], back_ref[...]
    pos_sum = feat_sum = None
    tgt_sums = [None] * gy_count
    for spot, (table, _, _) in enumerate(gy_spots):
        pos_src, pos_tgt, feat_src = spot_grads(
            rows_ref[spot], gy_refs[table], src_pos, feats, first, wide, back, orders
        )
        pos_sum = pos_src if pos_sum is None else pos_sum + pos_src
        feat_sum = feat_src if feat_sum is None else feat_sum + feat_src
        held = tgt_sums[table]
        tgt_sums[table] = pos_tgt if held is None else held + pos_tgt
    for table, ref in enumerate(gx_outs):
        part = slice(table * atoms, (table + 1) * atoms)
        ref[0:atoms] = feat_sum[part]
        ref[atoms:] = jnp.zeros((sublanes, ref.shape[1]), f32)
        ref[atoms:, 0:atoms] = pos_sum[:, part]
    for total, ref in zip(tgt_sums, gy_outs):
        ref[...] = jnp.zeros(ref.shape, f32)
        ref[:, 0:atoms] = total


def sum_kernel(gx_count, *refs):
    gx_refs, gy_refs = refs[:gx_count], refs[gx_count:-2]
    pos_ref, feat_ref = refs[-2:]
    atoms = pos_ref.shape[3]
    feat = gx_refs[0][...]
    for ref in gx_refs[1:]:
        feat = feat + ref[...]
    pos = feat[atoms : atoms + 3, 0:atoms]
    for ref in gy_refs:
        pos = pos + ref[0:3, 0:atoms]
    pos_ref[0, 0] = pos
    feat_ref[0, 0] = feat[0:atoms]


vmem = pl.BlockSpec(memory_space=pltpu.VMEM)
smem = pl.BlockSpec(memory_space=pltpu.SMEM)


def local(
    gx_size, gy_size, positions, features, cotangent, nbr_src, nbr_tgt, pair_mask, pair_species,
    w_in, species_emb, w_out,
):
    atoms, channels = features.shape[2:]
    wide = cotangent.shape[3]
    steps, _, pairs = nbr_src.shape[2:]
    orders, hidden = w_in.shape
    kinds = species_emb.shape[0]
    slots = steps * pairs
    gx_links, gy_links = links_of(gx_size), links_of(gy_size)
    gx_spots, gy_spots = spots_of(gx_links), spots_of(gy_links)
    gx_count, gy_count = len(gx_links) + 1, len(gy_links) + 1
    sds = jax.ShapeDtypeStruct

    gx_own, gy_own = pl.pallas_call(
        pack_kernel,
        out_shape=(sds((atoms + sublanes, channels), f32), sds((atoms + sublanes, wide), f32)),
        in_specs=[vmem] * 3,
        out_specs=(vmem, vmem),
        name="pack",
    )(positions, features, cotangent)
    gy_packs = [gy_own] + [link.fetch(gy_own, "gy") for link in gy_links]
    gx_packs = [gx_own] + [link.fetch(gx_own, "gx") for link in gx_links]

    place = jnp.stack([lax.axis_index("gx"), lax.axis_index("gy")]).astype(jnp.int32)
    padded = -(-(orders + kinds) // sublanes) * sublanes
    prepared = pl.pallas_call(
        functools.partial(prep_kernel, gx_spots, gy_spots),
        out_shape=(
            sds((len(gy_spots), sublanes, slots), jnp.int32),
            sds((w_out.shape[1], 3 * hidden), bf16),
            sds((hidden, 3 * w_out.shape[1]), bf16),
            sds((padded, hidden), f32),
        ),
        in_specs=[smem] + [vmem] * 7,
        out_specs=(vmem,) * 4,
        name="prepare",
    )(place, nbr_src, nbr_tgt, pair_mask, pair_species, w_in, species_emb, w_out)

    outs = pl.pallas_call(
        functools.partial(main_kernel, gy_spots, gx_count, gy_count, orders),
        out_shape=(sds((atoms + sublanes, channels), f32),) * gx_count
        + (sds((sublanes, channels), f32),) * gy_count,
        in_specs=[vmem] * (4 + gx_count + gy_count),
        out_specs=(vmem,) * (gx_count + gy_count),
        scratch_shapes=[pltpu.VMEM((sublanes, gx_count * atoms), f32)],
        compiler_params=pltpu.CompilerParams(vmem_limit_bytes=32 * 1024 * 1024),
        name="tiles",
    )(*prepared, *gx_packs, *gy_packs)
    gx_outs, gy_outs = list(outs[:gx_count]), list(outs[gx_count:])
    gx_back = gx_outs[:1] + [l.give(o, "gx") for l, o in zip(gx_links, gx_outs[1:])]
    gy_back = gy_outs[:1] + [l.give(o, "gy") for l, o in zip(gy_links, gy_outs[1:])]
    return pl.pallas_call(
        functools.partial(sum_kernel, gx_count),
        out_shape=(sds(positions.shape, f32), sds(features.shape, f32)),
        in_specs=[vmem] * (gx_count + gy_count),
        out_specs=(vmem, vmem),
        name="sums",
    )(*gx_back, *gy_back)


def solution(mesh):
    split = [P("gx", "gy")] * 7 + [P()] * 3
    return jax.shard_map(
        functools.partial(local, mesh.shape["gx"], mesh.shape["gy"]),
        mesh=mesh,
        in_specs=tuple(split),
        out_specs=(P("gx", "gy"), P("gx", "gy")),
        check_vma=False,
    )
```

```python
import functools
import math

import jax
import jax.numpy as jnp
from jax import lax
from jax.experimental import pallas as pl
from jax.experimental.pallas import tpu as pltpu
from jax.sharding import PartitionSpec as P

domain_side = 5.0
cutoff = 12.0
soften = 0.25
reach = 2
sublanes = 8
degree = (0, 1, 1, 1, 2, 2, 2, 2, 2)
megabyte = 1024 * 1024
f32 = jnp.float32
bf16 = jnp.bfloat16


class Link:
    def __init__(self, step, bit, peers):
        self.step, self.bit, self.peers = step, bit, peers

    def delta(self, i):
        return self.step * (1 - 2 * ((i >> self.bit) & 1))

    def swap(self, value, axis):
        n = self.peers
        return lax.ppermute(value, axis, [(i, (i + self.delta(i)) % n) for i in range(n)])


def links_of(peers):
    assert peers % 4 == 0, peers
    steps = [(1, 0), (-1, 0), (2, 1)] + ([(-2, 1)] if peers > 4 else [])
    return [Link(step, bit, peers) for step, bit in steps]


def spots_of(links):
    spots = [(0, None, 0)]
    for table, link in enumerate(links):
        spots.append((table + 1, link, 1))
        if link.peers == 4 and abs(link.step) == 2:
            spots.append((table + 1, link, -1))
    return spots


def pieces(x, count):
    out = []
    for _ in range(count):
        out.append(x.astype(bf16).astype(f32))
        x = x - out[-1]
    return out


def dot(a, b):
    return jnp.dot(a, b, preferred_element_type=f32)


def dot_rows(a, b):
    return lax.dot_general(a, b, (((1,), (1,)), ((), ())), preferred_element_type=f32)


def dot_cols(a, b):
    return lax.dot_general(a, b, (((0,), (0,)), ((), ())), preferred_element_type=f32)


def pack_targets_kernel(pos_ref, cot_ref, out_ref):
    atoms = cot_ref.shape[2]
    parts = len(degree)
    channels = out_ref.shape[1]
    for m in range(parts):
        out_ref[m * atoms : (m + 1) * atoms] = cot_ref[0, 0, :, m * channels : (m + 1) * channels]
    out_ref[parts * atoms :] = jnp.zeros((sublanes, channels), f32)
    for axis in range(3):
        out_ref[parts * atoms + axis : parts * atoms + axis + 1, 0:atoms] = pos_ref[0, axis]


def pack_sources_kernel(pos_ref, feat_ref, out_ref):
    atoms, channels = feat_ref.shape[2:]
    out_ref[0:atoms] = feat_ref[0, 0]
    out_ref[atoms:] = jnp.zeros((sublanes, channels), f32)
    for axis in range(3):
        out_ref[atoms + axis : atoms + axis + 1, 0:atoms] = pos_ref[0, axis]


def stack_kernel(upper_ref, lower_ref, out_ref):
    rows = upper_ref.shape[0]
    out_ref[0:rows] = upper_ref[...]
    out_ref[rows:] = lower_ref[...]


def prep_kernel(
    gx_spots, gy_spots, groups, src_ref, tgt_ref, mask_ref, spec_ref, in_ref, emb_ref, out_ref,
    *outs,
):
    atoms = pairs = src_ref.shape[4]
    at_x, at_y = lax.axis_index("gx"), lax.axis_index("gy")
    wide_ref, back_ref, first_ref, last_ref = outs[len(groups) :]
    for group, rows_ref in zip(groups, outs):
        slot = 0
        for place, spot in enumerate(group):
            _, link, sign = gy_spots[spot]
            step_y = 0 if link is None else sign * link.delta(at_y)
            for table, link, sign in gx_spots:
                step_x = 0 if link is None else sign * link.delta(at_x)
                lanes = slice(slot * pairs, (slot + 1) * pairs)
                row, col = reach + step_x, reach + step_y
                rows_ref[0:1, lanes] = src_ref[0, row, col] + table * atoms
                rows_ref[1:2, lanes] = tgt_ref[0, row, col] + place * atoms
                rows_ref[2:3, lanes] = mask_ref[0, row, col]
                rows_ref[3:4, lanes] = spec_ref[0, row, col]
                rows_ref[4:5, lanes] = jnp.full((1, pairs), step_x, jnp.int32)
                rows_ref[5:6, lanes] = jnp.full((1, pairs), -step_y, jnp.int32)
                slot += 1
        rows_ref[6:8] = jnp.zeros((2, rows_ref.shape[1]), jnp.int32)
    high, low = pieces(out_ref[...], 2)
    wide_ref[...] = jnp.concatenate([high, high, low], axis=0).T.astype(bf16)
    upper = jnp.concatenate([high, high], axis=1)
    lower = jnp.concatenate([low, jnp.zeros_like(low)], axis=1)
    back_ref[...] = jnp.concatenate([upper, lower], axis=0).astype(bf16)
    orders, hidden = in_ref.shape
    spare = jnp.zeros((sublanes * 2 - emb_ref.shape[0], hidden), f32)
    high, low = pieces(jnp.concatenate([in_ref[...], emb_ref[...], spare], axis=0), 2)
    first_ref[...] = jnp.concatenate([high, high, low], axis=0).T.astype(bf16)
    last_ref[...] = jnp.concatenate([high[0:orders], high[0:orders], low[0:orders]], axis=1).astype(bf16)


def radial_waves(dist, orders):
    order = (lax.broadcasted_iota(jnp.int32, (orders, 1), 0) + 1).astype(f32)
    turn = order * (dist * (1.0 / cutoff))
    whole = jnp.floor(turn + 0.5)
    part = turn - whole
    sign = 1.0 - 2.0 * (whole - 2.0 * jnp.floor(0.5 * whole))
    square = part * part
    sine = jnp.zeros_like(square)
    for k in (11, 9, 7, 5, 3, 1):
        sine = sine * square + (-1.0) ** (k // 2) * math.pi**k / math.factorial(k)
    cosine = jnp.zeros_like(square)
    for k in (12, 10, 8, 6, 4, 2, 0):
        cosine = cosine * square + (-1.0) ** (k // 2) * math.pi**k / math.factorial(k)
    return order, sign * part * sine, sign * cosine


def thrice(x):
    high, low = pieces(x, 2)
    return jnp.concatenate([high, low, high], axis=0).astype(bf16)


def onehot(ids, count):
    return jnp.where(lax.broadcasted_iota(jnp.int32, (count, ids.shape[1]), 0) == ids, 1.0, 0.0)


def slot_grads(rows, cot_refs, src_pos, feats, weights, orders):
    wide, back, first, last = weights
    slots = rows.shape[1]
    sources = src_pos.shape[1]
    channels = feats.shape[0]
    hidden = last.shape[1] // 3
    parts = len(degree)
    atoms = (cot_refs[0].shape[0] - sublanes) // parts
    targets = atoms * len(cot_refs)

    src_hot = onehot(rows[0:1], sources).astype(bf16)
    tgt_hot = onehot(rows[1:2], targets).astype(bf16)
    mask = rows[2:3].astype(f32)
    offset = rows[4:6].astype(f32) * domain_side

    tgt_pos = [jnp.concatenate(pieces(ref[parts * atoms :, 0:atoms], 3), axis=0) for ref in cot_refs]
    from_src = dot(src_pos, src_hot)
    from_tgt = dot(jnp.concatenate(tgt_pos, axis=1).astype(bf16), tgt_hot)
    from_src = from_src[0:8] + from_src[8:16] + from_src[16:24]
    from_tgt = from_tgt[0:8] + from_tgt[8:16] + from_tgt[16:24]
    rel = [
        from_src[0:1] + offset[0:1] - from_tgt[0:1],
        from_src[1:2] + offset[1:2] - from_tgt[1:2],
        from_src[2:3] - from_tgt[2:3],
    ]
    dist = jnp.sqrt(rel[0] * rel[0] + rel[1] * rel[1] + rel[2] * rel[2] + soften)
    near = 1.0 / dist
    x, y, z = (r * near for r in rel)
    scaled = dist * (1.0 / cutoff)
    room = jnp.where(scaled < 1.0, 1.0 - scaled * scaled, 0.0)
    env = room * room * mask
    d_env = (-4.0 / cutoff) * scaled * room * mask

    order, sine, cosine = radial_waves(dist, orders)
    norm = math.sqrt(2.0 / cutoff)
    basis = norm * near * sine
    d_basis = norm * near * ((math.pi / cutoff) * order * cosine - sine * near)
    species = onehot(rows[3:4], 2 * sublanes)
    before = dot(first, thrice(jnp.concatenate([basis, species], axis=0)))
    gate = 1.0 / (1.0 + jnp.exp(-before))
    act = before * gate
    d_act = gate * (1.0 + before * (1.0 - gate))
    radial = dot(wide, thrice(act))
    gathered = dot(feats, jnp.concatenate([src_hot, src_hot], axis=0))

    root3, root5, root15 = math.sqrt(3.0), math.sqrt(5.0), math.sqrt(15.0)
    shapes = [
        None, root3 * x, root3 * y, root3 * z, root15 * x * y, root15 * y * z,
        0.5 * root5 * (2.0 * z * z - x * x - y * y), root15 * x * z, 0.5 * root15 * (x * x - y * y),
    ]
    twice = lax.broadcasted_iota(jnp.int32, (2 * targets, slots), 0)
    twice = (twice // (2 * atoms)) * atoms + lax.rem(twice, atoms)
    twice = jnp.where(twice == rows[1:2], 1.0, 0.0).astype(bf16)
    d_shapes = [None] * parts
    d_radial = []
    through = None
    for low, high in ((0, 1), (1, 4), (4, 9)):
        l = len(d_radial)
        own = radial[l * channels : (l + 1) * channels]
        with_feats = own * gathered
        total = None
        for m in range(low, high):
            blocks = []
            for ref in cot_refs:
                blocks += pieces(ref[m * atoms : (m + 1) * atoms], 2)
            cot = dot_cols(jnp.concatenate(blocks, axis=0).astype(bf16), twice)
            if m:
                d_shapes[m] = jnp.sum(with_feats * cot, axis=0, keepdims=True) * env
                cot = cot * shapes[m]
            total = cot if total is None else total + cot
        d_radial.append(total * gathered)
        own = own * total
        through = own if through is None else through + own
    to_env = jnp.sum(through * gathered, axis=0, keepdims=True)
    through = through * env
    d_hidden = dot(back, jnp.concatenate(
        [p.astype(bf16) for p in pieces(jnp.concatenate(d_radial, axis=0), 2)], axis=0
    ))
    d_before = (d_hidden[0:hidden] + d_hidden[hidden:]) * (d_act * env)
    to_basis = dot(last, thrice(d_before))
    d_dist = jnp.sum(to_basis * d_basis, axis=0, keepdims=True) + to_env * d_env

    s = d_shapes
    d_x = root3 * s[1] + root15 * (y * s[4] + z * s[7] + x * s[8]) - root5 * x * s[6]
    d_y = root3 * s[2] + root15 * (x * s[4] + z * s[5] - y * s[8]) - root5 * y * s[6]
    d_z = root3 * s[3] + root15 * (y * s[5] + x * s[7]) + 2.0 * root5 * z * s[6]
    d_dist = d_dist - near * (x * d_x + y * d_y + z * d_z)
    grad = jnp.concatenate(
        [near * d_x + x * d_dist, near * d_y + y * d_dist, near * d_z + z * d_dist,
         jnp.zeros((sublanes - 3, slots), f32)], axis=0,
    )
    grad = jnp.concatenate(pieces(grad, 2), axis=0).astype(bf16)
    pos_src = dot_rows(grad, src_hot)
    pos_tgt = dot_rows(grad, tgt_hot)
    feat_src = sum(dot_rows(src_hot, p.astype(bf16)) for p in pieces(through, 2))
    return pos_src[0:8] + pos_src[8:16], -(pos_tgt[0:8] + pos_tgt[8:16]), feat_src


def blocks_of(refs, rows):
    return [
        ref.at[start : start + rows] for ref in refs for start in range(0, ref.shape[0], rows)
    ]


def first_kernel(orders, group, gx_count, rows_ref, *refs):
    refs = list(refs)
    weights = [refs.pop(0)[...] for _ in range(4)]
    gx_refs = [refs.pop(0) for _ in range(gx_count)]
    gy_refs = [refs.pop(0) for _ in group]
    atoms = (gy_refs[0].shape[0] - sublanes) // len(degree)
    gx_refs = blocks_of(gx_refs, atoms + sublanes)
    src_pos_ref, feats_ref, feat_ref, pos_ref, tgt_ref, place = refs
    for table, ref in enumerate(gx_refs):
        place[:, table * atoms : (table + 1) * atoms] = ref[atoms:, 0:atoms]
    src_pos = jnp.concatenate(pieces(place[...], 3), axis=0).astype(bf16)
    feats = pieces(jnp.concatenate([ref[0:atoms] for ref in gx_refs], axis=0), 2)
    feats = jnp.concatenate(feats, axis=0).T.astype(bf16)
    src_pos_ref[...] = src_pos
    feats_ref[...] = feats
    pos_src, pos_tgt, feat_src = slot_grads(
        rows_ref[...], gy_refs, src_pos, feats, weights, orders
    )
    feat_ref[...] = feat_src
    pos_ref[...] = pos_src
    pos_ref[:, 0:atoms] = pos_src[:, 0:atoms] + pos_tgt[:, 0:atoms]
    tgt_ref[...] = jnp.zeros(tgt_ref.shape, f32)
    for place_in, table in enumerate(group):
        if table:
            tgt_ref[:, (table - 1) * atoms : table * atoms] = pos_tgt[
                :, place_in * atoms : (place_in + 1) * atoms
            ]


def last_kernel(orders, group, gx_count, rows_ref, *refs):
    refs = list(refs)
    weights = [refs.pop(0)[...] for _ in range(4)]
    src_pos, feats = (refs.pop(0)[...] for _ in range(2))
    held_feat, held_pos = (refs.pop(0) for _ in range(2))
    gy_refs = [refs.pop(0) for _ in group]
    gx_outs, (near_ref, far_ref) = refs[:gx_count], refs[gx_count:]
    pos_src, pos_tgt, feat_src = slot_grads(
        rows_ref[...], gy_refs, src_pos, feats, weights, orders
    )
    atoms = pos_tgt.shape[1] // len(group)
    feat = held_feat[...] + feat_src
    pos = held_pos[...] + pos_src
    tables = (0, 2, 1, 3) if len(gx_outs) == 3 else range(len(gx_outs))
    for table, ref in zip(tables, blocks_of(gx_outs, atoms + sublanes)):
        part = slice(table * atoms, (table + 1) * atoms)
        ref[0:atoms] = feat[part]
        ref[atoms:] = jnp.zeros((sublanes, ref.shape[1]), f32)
        ref[atoms:, 0:atoms] = pos[:, part]
    near_ref[...] = jnp.zeros(near_ref.shape, f32)
    far_ref[...] = jnp.zeros(far_ref.shape, f32)
    near_ref[:, 0:atoms] = pos_tgt[:, group.index(3) * atoms :][:, 0:atoms]
    far_ref[:, 0:atoms] = pos_tgt[:, group.index(4) * atoms :][:, 0:atoms]


def join_kernel(atoms, relay_ref, near_ref, far_ref, near_out, far_out):
    at_y = lax.axis_index("gy")
    to_far = ((at_y + (at_y >> 1)) & 1).astype(f32)
    relay = relay_ref[:, atoms : 2 * atoms]
    near_out[...] = near_ref[...]
    far_out[...] = far_ref[...]
    near_out[:, 0:atoms] = near_ref[:, 0:atoms] + relay * (1.0 - to_far)
    far_out[:, 0:atoms] = far_ref[:, 0:atoms] + relay * to_far


def sum_kernel(gx_count, *refs):
    gx_refs, gy_refs = refs[:gx_count], refs[gx_count:-2]
    pos_ref, feat_ref = refs[-2:]
    atoms = pos_ref.shape[3]
    feat = gx_refs[0][...]
    for ref in gx_refs[1:]:
        feat = feat + ref[ref.shape[0] - atoms - sublanes :]
    pos = feat[atoms : atoms + 3, 0:atoms]
    for ref in gy_refs:
        pos = pos + ref[0:3, 0:atoms]
    for axis in range(3):
        pos_ref[0, axis] = pos[axis : axis + 1]
    feat_ref[0, 0] = feat[0:atoms]


vmem = pl.BlockSpec(memory_space=pltpu.VMEM)
hbm = pl.BlockSpec(memory_space=pltpu.HBM)


def call(kernel, name, out_shape, operands, scratch=(), room=4, space=vmem):
    return pl.pallas_call(
        kernel,
        out_shape=out_shape,
        in_specs=[space] * len(operands),
        out_specs=(vmem,) * len(out_shape),
        scratch_shapes=list(scratch),
        compiler_params=pltpu.CompilerParams(vmem_limit_bytes=room and room * megabyte),
        name=name,
    )(*operands)


def gather(links, own):
    if links[0].peers > 4:
        return [own] + [link.swap(own, "gx") for link in links]
    one = links[0].swap(own, "gx")
    rows, columns = own.shape
    (both,) = call(
        stack_kernel, "stack", (jax.ShapeDtypeStruct((2 * rows, columns), own.dtype),), (one, own)
    )
    return [own, one, links[2].swap(both, "gx")]


def gx_shapes(links, block):
    if links[0].peers > 4:
        return (block,) * (len(links) + 1)
    rows, columns = block.shape
    return (block, jax.ShapeDtypeStruct((2 * rows, columns), block.dtype), block)


def scatter(links, outs):
    if links[0].peers > 4:
        return outs[:1] + [link.swap(out, "gx") for link, out in zip(links, outs[1:])]
    own, pair, far = outs
    rows = own.shape[0]
    pair = links[0].swap(pair, "gx")
    far = links[2].swap(far + pair[0:rows], "gx")
    return [own, pair, far]


def local(
    gx_size, gy_size, positions, features, cotangent, nbr_src, nbr_tgt, pair_mask, pair_species,
    w_in, species_emb, w_out,
):
    atoms, channels = features.shape[2:]
    steps, _, pairs = nbr_src.shape[2:]
    orders, hidden = w_in.shape
    slots = steps * pairs
    gx_links, gy_links = links_of(gx_size), links_of(gy_size)
    gx_spots, gy_spots = spots_of(gx_links), spots_of(gy_links)
    gx_count = len(gx_links) + 1
    sources = gx_count * atoms
    sds = jax.ShapeDtypeStruct
    groups = ((0, 2, 1), (4, 3))

    by_axis = jnp.transpose(positions, (0, 2, 1, 3))
    lists = [jnp.transpose(x, (0, 2, 3, 1, 4)) for x in (nbr_src, nbr_tgt, pair_mask, pair_species)]
    gx_pack = sds((atoms + sublanes, channels), f32)
    gy_pack = sds((len(degree) * atoms + sublanes, channels), f32)
    (gy_own,) = call(
        pack_targets_kernel, "pack_targets", (gy_pack,), (by_axis, cotangent), room=None
    )
    (gx_own,) = call(pack_sources_kernel, "pack_sources", (gx_pack,), (by_axis, features))
    gy_packs = [gy_own] + [link.swap(gy_own, "gy") for link in gy_links]
    gx_packs = gather(gx_links, gx_own)

    *rows, wide, back, first, last = call(
        functools.partial(prep_kernel, gx_spots, gy_spots, groups),
        "prepare",
        (
            *(sds((sublanes, len(group) * slots), jnp.int32) for group in groups),
            sds((w_out.shape[1], 3 * hidden), bf16),
            sds((2 * hidden, 2 * w_out.shape[1]), bf16),
            sds((hidden, 3 * (orders + 2 * sublanes)), bf16),
            sds((orders, 3 * hidden), bf16),
        ),
        (*lists, w_in, species_emb, w_out),
    )
    weights = (wide, back, first, last)
    packs = [[gy_packs[table] for table in group] for group in groups]
    tgt_pack = sds((sublanes, channels), f32)
    src_pos, feats, feat, pos, tgt = call(
        functools.partial(first_kernel, orders, groups[0], len(gx_packs)), "tiles",
        (
            sds((3 * sublanes, sources), bf16), sds((channels, 2 * sources), bf16),
            sds((sources, channels), f32), sds((sublanes, sources), f32), tgt_pack,
        ),
        (rows[0], *weights, *gx_packs, *packs[0]),
        [pltpu.VMEM((sublanes, sources), f32)], 16,
    )
    relay = gy_links[0].swap(tgt, "gy")
    *gx_outs, near, far = call(
        functools.partial(last_kernel, orders, groups[1], len(gx_packs)), "tiles",
        gx_shapes(gx_links, gx_pack) + (tgt_pack,) * 2,
        (rows[1], *weights, src_pos, feats, feat, pos, *packs[1]), room=16,
    )
    near, far = call(functools.partial(join_kernel, atoms), "join", (tgt_pack,) * 2, (relay, near, far))
    *gx_outs, near, far = lax.optimization_barrier((*gx_outs, near, far))
    back_gy = [gy_links[3].swap(far, "gy"), gy_links[2].swap(near, "gy"), relay]
    back_gx = scatter(gx_links, gx_outs)
    pos, feat = call(
        functools.partial(sum_kernel, len(back_gx)), "sums",
        (sds(by_axis.shape, f32), sds(features.shape, f32)),
        (*back_gx, *back_gy),
    )
    return jnp.transpose(pos, (0, 2, 1, 3)), feat


def solution(mesh):
    split = [P("gx", "gy")] * 7 + [P()] * 3
    return jax.shard_map(
        functools.partial(local, mesh.shape["gx"], mesh.shape["gy"]),
        mesh=mesh,
        in_specs=tuple(split),
        out_specs=(P("gx", "gy"), P("gx", "gy")),
        check_vma=False,
    )
```

```python
import functools
import math

import jax
import jax.numpy as jnp
from jax import lax
from jax.experimental import pallas as pl
from jax.experimental.pallas import tpu as pltpu
from jax.sharding import PartitionSpec as P

domain_side = 5.0
cutoff = 12.0
soften = 0.25
reach = 2
sublanes = 8
degree = (0, 1, 1, 1, 2, 2, 2, 2, 2)
megabyte = 1024 * 1024
f32 = jnp.float32
bf16 = jnp.bfloat16


class Link:
    def __init__(self, step, bit, peers):
        self.step, self.bit, self.peers = step, bit, peers

    def delta(self, i):
        return self.step * (1 - 2 * ((i >> self.bit) & 1))

    def swap(self, value, axis):
        n = self.peers
        return lax.ppermute(value, axis, [(i, (i + self.delta(i)) % n) for i in range(n)])


def links_of(peers):
    assert peers % 4 == 0, peers
    steps = [(1, 0), (-1, 0), (2, 1)] + ([(-2, 1)] if peers > 4 else [])
    return [Link(step, bit, peers) for step, bit in steps]


def spots_of(links):
    spots = [(0, None, 0)]
    for table, link in enumerate(links):
        spots.append((table + 1, link, 1))
        if link.peers == 4 and abs(link.step) == 2:
            spots.append((table + 1, link, -1))
    return spots


def pieces(x, count):
    out = []
    for _ in range(count):
        out.append(x.astype(bf16).astype(f32))
        x = x - out[-1]
    return out


def dot(a, b):
    return jnp.dot(a, b, preferred_element_type=f32)


def dot_rows(a, b):
    return lax.dot_general(a, b, (((1,), (1,)), ((), ())), preferred_element_type=f32)


def dot_cols(a, b):
    return lax.dot_general(a, b, (((0,), (0,)), ((), ())), preferred_element_type=f32)


def pack_kernel(pos_ref, feat_ref, cot_ref, gx_ref, gy_ref):
    atoms, channels = feat_ref.shape[2:]
    parts = len(degree)
    gx_ref[0:atoms] = feat_ref[0, 0]
    for m in range(parts):
        gy_ref[m * atoms : (m + 1) * atoms] = cot_ref[0, 0, :, m * channels : (m + 1) * channels]
    zero = jnp.zeros((sublanes, channels), f32)
    gx_ref[atoms:] = zero
    gy_ref[parts * atoms :] = zero
    for axis in range(3):
        gx_ref[atoms + axis : atoms + axis + 1, 0:atoms] = pos_ref[0, axis]
        gy_ref[parts * atoms + axis : parts * atoms + axis + 1, 0:atoms] = pos_ref[0, axis]


def stack_kernel(upper_ref, lower_ref, out_ref):
    rows = upper_ref.shape[0]
    out_ref[0:rows] = upper_ref[...]
    out_ref[rows:] = lower_ref[...]


def prep_kernel(
    gx_spots, gy_spots, groups, src_ref, tgt_ref, mask_ref, spec_ref, in_ref, emb_ref, out_ref,
    *outs,
):
    atoms = pairs = src_ref.shape[4]
    at_x, at_y = lax.axis_index("gx"), lax.axis_index("gy")
    wide_ref, back_ref, first_ref, last_ref = outs[len(groups) :]
    for group, rows_ref in zip(groups, outs):
        slot = 0
        for place, spot in enumerate(group):
            _, link, sign = gy_spots[spot]
            step_y = 0 if link is None else sign * link.delta(at_y)
            for table, link, sign in gx_spots:
                step_x = 0 if link is None else sign * link.delta(at_x)
                lanes = slice(slot * pairs, (slot + 1) * pairs)
                row, col = reach + step_x, reach + step_y
                rows_ref[0:1, lanes] = src_ref[0, row, col] + table * atoms
                rows_ref[1:2, lanes] = tgt_ref[0, row, col] + place * atoms
                rows_ref[2:3, lanes] = mask_ref[0, row, col]
                rows_ref[3:4, lanes] = spec_ref[0, row, col]
                rows_ref[4:5, lanes] = jnp.full((1, pairs), step_x, jnp.int32)
                rows_ref[5:6, lanes] = jnp.full((1, pairs), -step_y, jnp.int32)
                slot += 1
        rows_ref[6:8] = jnp.zeros((2, rows_ref.shape[1]), jnp.int32)
    high, low = pieces(out_ref[...], 2)
    wide_ref[...] = jnp.concatenate([high, high, low], axis=0).T.astype(bf16)
    upper = jnp.concatenate([high, high], axis=1)
    lower = jnp.concatenate([low, jnp.zeros_like(low)], axis=1)
    back_ref[...] = jnp.concatenate([upper, lower], axis=0).astype(bf16)
    orders, hidden = in_ref.shape
    spare = jnp.zeros((sublanes * 2 - emb_ref.shape[0], hidden), f32)
    high, low = pieces(jnp.concatenate([in_ref[...], emb_ref[...], spare], axis=0), 2)
    first_ref[...] = jnp.concatenate([high, high, low], axis=0).T.astype(bf16)
    last_ref[...] = jnp.concatenate([high[0:orders], high[0:orders], low[0:orders]], axis=1).astype(bf16)


def radial_waves(dist, orders):
    order = (lax.broadcasted_iota(jnp.int32, (orders, 1), 0) + 1).astype(f32)
    turn = order * (dist * (1.0 / cutoff))
    whole = jnp.floor(turn + 0.5)
    part = turn - whole
    sign = 1.0 - 2.0 * (whole - 2.0 * jnp.floor(0.5 * whole))
    square = part * part
    sine = jnp.zeros_like(square)
    for k in (11, 9, 7, 5, 3, 1):
        sine = sine * square + (-1.0) ** (k // 2) * math.pi**k / math.factorial(k)
    cosine = jnp.zeros_like(square)
    for k in (12, 10, 8, 6, 4, 2, 0):
        cosine = cosine * square + (-1.0) ** (k // 2) * math.pi**k / math.factorial(k)
    return order, sign * part * sine, sign * cosine


def thrice(x):
    high, low = pieces(x, 2)
    return jnp.concatenate([high, low, high], axis=0).astype(bf16)


def onehot(ids, count):
    return jnp.where(lax.broadcasted_iota(jnp.int32, (count, ids.shape[1]), 0) == ids, 1.0, 0.0)


def slot_grads(rows, cot_refs, src_pos, feats, weights, orders):
    wide, back, first, last = weights
    slots = rows.shape[1]
    sources = src_pos.shape[1]
    channels = feats.shape[0]
    hidden = last.shape[1] // 3
    parts = len(degree)
    atoms = (cot_refs[0].shape[0] - sublanes) // parts
    targets = atoms * len(cot_refs)

    src_hot = onehot(rows[0:1], sources).astype(bf16)
    tgt_hot = onehot(rows[1:2], targets).astype(bf16)
    mask = rows[2:3].astype(f32)
    offset = rows[4:6].astype(f32) * domain_side

    tgt_pos = [jnp.concatenate(pieces(ref[parts * atoms :, 0:atoms], 3), axis=0) for ref in cot_refs]
    from_src = dot(src_pos, src_hot)
    from_tgt = dot(jnp.concatenate(tgt_pos, axis=1).astype(bf16), tgt_hot)
    from_src = from_src[0:8] + from_src[8:16] + from_src[16:24]
    from_tgt = from_tgt[0:8] + from_tgt[8:16] + from_tgt[16:24]
    rel = [
        from_src[0:1] + offset[0:1] - from_tgt[0:1],
        from_src[1:2] + offset[1:2] - from_tgt[1:2],
        from_src[2:3] - from_tgt[2:3],
    ]
    dist = jnp.sqrt(rel[0] * rel[0] + rel[1] * rel[1] + rel[2] * rel[2] + soften)
    near = 1.0 / dist
    x, y, z = (r * near for r in rel)
    scaled = dist * (1.0 / cutoff)
    room = jnp.where(scaled < 1.0, 1.0 - scaled * scaled, 0.0)
    env = room * room * mask
    d_env = (-4.0 / cutoff) * scaled * room * mask

    order, sine, cosine = radial_waves(dist, orders)
    norm = math.sqrt(2.0 / cutoff)
    basis = norm * near * sine
    d_basis = norm * near * ((math.pi / cutoff) * order * cosine - sine * near)
    species = onehot(rows[3:4], 2 * sublanes)
    before = dot(first, thrice(jnp.concatenate([basis, species], axis=0)))
    gate = 1.0 / (1.0 + jnp.exp(-before))
    act = before * gate
    d_act = gate * (1.0 + before * (1.0 - gate))
    radial = dot(wide, thrice(act))
    gathered = dot(feats, jnp.concatenate([src_hot, src_hot], axis=0))

    root3, root5, root15 = math.sqrt(3.0), math.sqrt(5.0), math.sqrt(15.0)
    shapes = [
        None, root3 * x, root3 * y, root3 * z, root15 * x * y, root15 * y * z,
        0.5 * root5 * (2.0 * z * z - x * x - y * y), root15 * x * z, 0.5 * root15 * (x * x - y * y),
    ]
    twice = lax.broadcasted_iota(jnp.int32, (2 * targets, slots), 0)
    twice = (twice // (2 * atoms)) * atoms + lax.rem(twice, atoms)
    twice = jnp.where(twice == rows[1:2], 1.0, 0.0).astype(bf16)
    d_shapes = [None] * parts
    d_radial = []
    through = None
    for low, high in ((0, 1), (1, 4), (4, 9)):
        l = len(d_radial)
        own = radial[l * channels : (l + 1) * channels]
        with_feats = own * gathered
        total = None
        for m in range(low, high):
            blocks = []
            for ref in cot_refs:
                blocks += pieces(ref[m * atoms : (m + 1) * atoms], 2)
            cot = dot_cols(jnp.concatenate(blocks, axis=0).astype(bf16), twice)
            if m:
                d_shapes[m] = jnp.sum(with_feats * cot, axis=0, keepdims=True) * env
                cot = cot * shapes[m]
            total = cot if total is None else total + cot
        d_radial.append(total * gathered)
        own = own * total
        through = own if through is None else through + own
    to_env = jnp.sum(through * gathered, axis=0, keepdims=True)
    through = through * env
    d_hidden = dot(back, jnp.concatenate(
        [p.astype(bf16) for p in pieces(jnp.concatenate(d_radial, axis=0), 2)], axis=0
    ))
    d_before = (d_hidden[0:hidden] + d_hidden[hidden:]) * (d_act * env)
    to_basis = dot(last, thrice(d_before))
    d_dist = jnp.sum(to_basis * d_basis, axis=0, keepdims=True) + to_env * d_env

    s = d_shapes
    d_x = root3 * s[1] + root15 * (y * s[4] + z * s[7] + x * s[8]) - root5 * x * s[6]
    d_y = root3 * s[2] + root15 * (x * s[4] + z * s[5] - y * s[8]) - root5 * y * s[6]
    d_z = root3 * s[3] + root15 * (y * s[5] + x * s[7]) + 2.0 * root5 * z * s[6]
    d_dist = d_dist - near * (x * d_x + y * d_y + z * d_z)
    grad = jnp.concatenate(
        [near * d_x + x * d_dist, near * d_y + y * d_dist, near * d_z + z * d_dist,
         jnp.zeros((sublanes - 3, slots), f32)], axis=0,
    )
    grad = jnp.concatenate(pieces(grad, 2), axis=0).astype(bf16)
    pos_src = dot_rows(grad, src_hot)
    pos_tgt = dot_rows(grad, tgt_hot)
    feat_src = sum(dot_rows(src_hot, p.astype(bf16)) for p in pieces(through, 2))
    return pos_src[0:8] + pos_src[8:16], -(pos_tgt[0:8] + pos_tgt[8:16]), feat_src


def blocks_of(refs, rows):
    return [
        ref.at[start : start + rows] for ref in refs for start in range(0, ref.shape[0], rows)
    ]


def first_kernel(orders, group, gx_count, rows_ref, *refs):
    refs = list(refs)
    weights = [refs.pop(0)[...] for _ in range(4)]
    gx_refs = [refs.pop(0) for _ in range(gx_count)]
    gy_refs = [refs.pop(0) for _ in group]
    atoms = (gy_refs[0].shape[0] - sublanes) // len(degree)
    gx_refs = blocks_of(gx_refs, atoms + sublanes)
    src_pos_ref, feats_ref, feat_ref, pos_ref, tgt_ref, place = refs
    for table, ref in enumerate(gx_refs):
        place[:, table * atoms : (table + 1) * atoms] = ref[atoms:, 0:atoms]
    src_pos = jnp.concatenate(pieces(place[...], 3), axis=0).astype(bf16)
    feats = pieces(jnp.concatenate([ref[0:atoms] for ref in gx_refs], axis=0), 2)
    feats = jnp.concatenate(feats, axis=0).T.astype(bf16)
    src_pos_ref[...] = src_pos
    feats_ref[...] = feats
    pos_src, pos_tgt, feat_src = slot_grads(
        rows_ref[...], gy_refs, src_pos, feats, weights, orders
    )
    feat_ref[...] = feat_src
    pos_ref[...] = pos_src
    pos_ref[:, 0:atoms] = pos_src[:, 0:atoms] + pos_tgt[:, 0:atoms]
    tgt_ref[...] = jnp.zeros(tgt_ref.shape, f32)
    for place_in, table in enumerate(group):
        if table:
            tgt_ref[:, (table - 1) * atoms : table * atoms] = pos_tgt[
                :, place_in * atoms : (place_in + 1) * atoms
            ]


def last_kernel(orders, group, gx_count, rows_ref, *refs):
    refs = list(refs)
    weights = [refs.pop(0)[...] for _ in range(4)]
    src_pos, feats = (refs.pop(0)[...] for _ in range(2))
    held_feat, held_pos = (refs.pop(0) for _ in range(2))
    gy_refs = [refs.pop(0) for _ in group]
    gx_outs, (near_ref, far_ref) = refs[:gx_count], refs[gx_count:]
    pos_src, pos_tgt, feat_src = slot_grads(
        rows_ref[...], gy_refs, src_pos, feats, weights, orders
    )
    atoms = pos_tgt.shape[1] // len(group)
    feat = held_feat[...] + feat_src
    pos = held_pos[...] + pos_src
    tables = (0, 2, 1, 3) if len(gx_outs) == 3 else range(len(gx_outs))
    for table, ref in zip(tables, blocks_of(gx_outs, atoms + sublanes)):
        part = slice(table * atoms, (table + 1) * atoms)
        ref[0:atoms] = feat[part]
        ref[atoms:] = jnp.zeros((sublanes, ref.shape[1]), f32)
        ref[atoms:, 0:atoms] = pos[:, part]
    near_ref[...] = jnp.zeros(near_ref.shape, f32)
    far_ref[...] = jnp.zeros(far_ref.shape, f32)
    near_ref[:, 0:atoms] = pos_tgt[:, group.index(3) * atoms :][:, 0:atoms]
    far_ref[:, 0:atoms] = pos_tgt[:, group.index(4) * atoms :][:, 0:atoms]


def join_kernel(atoms, relay_ref, near_ref, far_ref, near_out, far_out):
    at_y = lax.axis_index("gy")
    to_far = ((at_y + (at_y >> 1)) & 1).astype(f32)
    relay = relay_ref[:, atoms : 2 * atoms]
    near_out[...] = jnp.zeros(near_out.shape, f32)
    far_out[...] = jnp.zeros(far_out.shape, f32)
    near_out[0:sublanes] = near_ref[...]
    far_out[0:sublanes] = far_ref[...]
    near_out[0:sublanes, 0:atoms] = near_ref[:, 0:atoms] + relay * (1.0 - to_far)
    far_out[0:sublanes, 0:atoms] = far_ref[:, 0:atoms] + relay * to_far


def sum_kernel(gx_count, *refs):
    gx_refs, gy_refs = refs[:gx_count], refs[gx_count:-2]
    pos_ref, feat_ref = refs[-2:]
    atoms = pos_ref.shape[3]
    feat = gx_refs[0][...]
    for ref in gx_refs[1:]:
        feat = feat + ref[ref.shape[0] - atoms - sublanes :]
    pos = feat[atoms : atoms + 3, 0:atoms]
    for ref in gy_refs:
        pos = pos + ref[0:3, 0:atoms]
    for axis in range(3):
        pos_ref[0, axis] = pos[axis : axis + 1]
    feat_ref[0, 0] = feat[0:atoms]


vmem = pl.BlockSpec(memory_space=pltpu.VMEM)


def call(kernel, name, out_shape, operands, scratch=(), room=4, us=None):
    return pl.pallas_call(
        kernel,
        out_shape=out_shape,
        in_specs=[vmem] * len(operands),
        out_specs=(vmem,) * len(out_shape),
        scratch_shapes=list(scratch),
        compiler_params=pltpu.CompilerParams(vmem_limit_bytes=room and room * megabyte),
        name=name,
        cost_estimate=us and pl.CostEstimate(
            flops=int(us * 1e9), bytes_accessed=0, transcendentals=0
        ),
    )(*operands)


def gather(links, own):
    if links[0].peers > 4:
        return [own] + [link.swap(own, "gx") for link in links]
    one = links[0].swap(own, "gx")
    rows, columns = own.shape
    two = links[2].swap(own, "gx")
    (both,) = call(
        stack_kernel, "stack", (jax.ShapeDtypeStruct((2 * rows, columns), own.dtype),), (own, two),
        us=2,
    )
    return [own, links[0].swap(both, "gx"), two]


def gx_shapes(links, block):
    if links[0].peers > 4:
        return (block,) * (len(links) + 1)
    rows, columns = block.shape
    return (block, jax.ShapeDtypeStruct((2 * rows, columns), block.dtype), block)


def scatter(links, outs):
    if links[0].peers > 4:
        return outs[:1] + [link.swap(out, "gx") for link, out in zip(links, outs[1:])]
    own, pair, far = outs
    rows = own.shape[0]
    pair = links[0].swap(pair, "gx")
    far = links[2].swap(far + pair[0:rows], "gx")
    return [own, pair, far]


def local(
    gx_size, gy_size, positions, features, cotangent, nbr_src, nbr_tgt, pair_mask, pair_species,
    w_in, species_emb, w_out,
):
    atoms, channels = features.shape[2:]
    steps, _, pairs = nbr_src.shape[2:]
    orders, hidden = w_in.shape
    slots = steps * pairs
    gx_links, gy_links = links_of(gx_size), links_of(gy_size)
    gx_spots, gy_spots = spots_of(gx_links), spots_of(gy_links)
    gx_count = len(gx_links) + 1
    sources = gx_count * atoms
    sds = jax.ShapeDtypeStruct
    groups = ((0, 2, 1), (4, 3))

    by_axis = jnp.transpose(positions, (0, 2, 1, 3))
    lists = [jnp.transpose(x, (0, 2, 3, 1, 4)) for x in (nbr_src, nbr_tgt, pair_mask, pair_species)]
    gx_pack = sds((atoms + sublanes, channels), f32)
    gy_pack = sds((len(degree) * atoms + sublanes, channels), f32)
    gx_own, gy_own = call(
        pack_kernel, "pack", (gx_pack, gy_pack), (by_axis, features, cotangent), room=None
    )
    gy_packs = [gy_own] + [link.swap(gy_own, "gy") for link in gy_links]
    gx_packs = gather(gx_links, gx_own)

    *rows, wide, back, first, last = call(
        functools.partial(prep_kernel, gx_spots, gy_spots, groups),
        "prepare",
        (
            *(sds((sublanes, len(group) * slots), jnp.int32) for group in groups),
            sds((w_out.shape[1], 3 * hidden), bf16),
            sds((2 * hidden, 2 * w_out.shape[1]), bf16),
            sds((hidden, 3 * (orders + 2 * sublanes)), bf16),
            sds((orders, 3 * hidden), bf16),
        ),
        (*lists, w_in, species_emb, w_out),
    )
    weights = (wide, back, first, last)
    packs = [[gy_packs[table] for table in group] for group in groups]
    tgt_pack = sds((sublanes, channels), f32)
    far_pack = sds((2 * channels // 4, channels), f32)
    src_pos, feats, feat, pos, tgt = call(
        functools.partial(first_kernel, orders, groups[0], len(gx_packs)), "tiles",
        (
            sds((3 * sublanes, sources), bf16), sds((channels, 2 * sources), bf16),
            sds((sources, channels), f32), sds((sublanes, sources), f32), tgt_pack,
        ),
        (rows[0], *weights, *gx_packs, *packs[0]),
        [pltpu.VMEM((sublanes, sources), f32)], 16,
    )
    relay = gy_links[0].swap(tgt, "gy")
    *gx_outs, near, far = call(
        functools.partial(last_kernel, orders, groups[1], len(gx_packs)), "tiles",
        gx_shapes(gx_links, gx_pack) + (tgt_pack,) * 2,
        (rows[1], *weights, src_pos, feats, feat, pos, *packs[1]), room=16,
    )
    near, far = call(functools.partial(join_kernel, atoms), "join", (far_pack,) * 2, (relay, near, far))
    *gx_outs, near, far = lax.optimization_barrier((*gx_outs, near, far))
    back_gy = [gy_links[3].swap(far, "gy"), gy_links[2].swap(near, "gy"), relay]
    back_gx = scatter(gx_links, gx_outs)
    pos, feat = call(
        functools.partial(sum_kernel, len(back_gx)), "sums",
        (sds(by_axis.shape, f32), sds(features.shape, f32)),
        (*back_gx, *back_gy),
    )
    return jnp.transpose(pos, (0, 2, 1, 3)), feat


def solution(mesh):
    split = [P("gx", "gy")] * 7 + [P()] * 3
    return jax.shard_map(
        functools.partial(local, mesh.shape["gx"], mesh.shape["gy"]),
        mesh=mesh,
        in_specs=tuple(split),
        out_specs=(P("gx", "gy"), P("gx", "gy")),
        check_vma=False,
    )
```

```python
import functools
import math

import jax
import jax.numpy as jnp
from jax import lax
from jax.experimental import pallas as pl
from jax.experimental.pallas import tpu as pltpu
from jax.sharding import PartitionSpec as P

domain_side = 5.0
cutoff = 12.0
soften = 0.25
reach = 2
sublanes = 8
degree = (0, 1, 1, 1, 2, 2, 2, 2, 2)
megabyte = 1024 * 1024
f32 = jnp.float32
bf16 = jnp.bfloat16


class Link:
    def __init__(self, step, bit, peers):
        self.step, self.bit, self.peers = step, bit, peers

    def delta(self, i):
        return self.step * (1 - 2 * ((i >> self.bit) & 1))

    def swap(self, value, axis):
        n = self.peers
        return lax.ppermute(value, axis, [(i, (i + self.delta(i)) % n) for i in range(n)])


def links_of(peers):
    assert peers % 4 == 0, peers
    steps = [(1, 0), (-1, 0), (2, 1)] + ([(-2, 1)] if peers > 4 else [])
    return [Link(step, bit, peers) for step, bit in steps]


def gx_spots_of(links):
    spots = [(0, None, 0)]
    for table, link in enumerate(links):
        spots.append((table + 1, link, 1))
        if link.peers == 4 and abs(link.step) == 2:
            spots.append((table + 1, link, -1))
    return spots


def pieces(x, count):
    out = []
    for _ in range(count):
        out.append(x.astype(bf16).astype(f32))
        x = x - out[-1]
    return out


def dot(a, b):
    return jnp.dot(a, b, preferred_element_type=f32)


def dot_rows(a, b):
    return lax.dot_general(a, b, (((1,), (1,)), ((), ())), preferred_element_type=f32)


def dot_cols(a, b):
    return lax.dot_general(a, b, (((0,), (0,)), ((), ())), preferred_element_type=f32)


def write_rows(store, gx_spots, at_x, lists, step_y, place, start):
    atoms = pairs = lists[0].shape[4]
    for slot, (table, link, sign) in enumerate(gx_spots):
        step_x = 0 if link is None else sign * link.delta(at_x)
        src, tgt, mask, spec = (ref[0, reach + step_x, reach + step_y] for ref in lists)
        store(0, start + slot * pairs, src + table * atoms)
        store(1, start + slot * pairs, tgt + place * atoms)
        store(2, start + slot * pairs, mask)
        store(3, start + slot * pairs, spec)
        store(4, start + slot * pairs, jnp.full((1, pairs), step_x, jnp.int32))
        store(5, start + slot * pairs, jnp.full((1, pairs), -step_y, jnp.int32))


def pack_kernel(
    gx_spots, gy_links, pos_ref, feat_ref, cot_ref, src_ref, tgt_ref, mask_ref, spec_ref,
    gx_ref, y_ref, gy_ref,
):
    atoms, channels = feat_ref.shape[2:]
    pairs = src_ref.shape[4]
    parts = len(degree)
    zero = jnp.zeros((sublanes, channels), f32)
    for ref in (gx_ref, y_ref):
        ref[0:atoms] = feat_ref[0, 0]
        ref[atoms : atoms + sublanes] = zero
    for m in range(parts):
        gy_ref[m * atoms : (m + 1) * atoms] = cot_ref[0, 0, :, m * channels : (m + 1) * channels]
    gy_ref[parts * atoms :] = zero
    for axis in range(3):
        row = pos_ref[0, axis]
        gx_ref[atoms + axis : atoms + axis + 1, 0:atoms] = row
        y_ref[atoms + axis : atoms + axis + 1, 0:atoms] = row
        gy_ref[parts * atoms + axis : parts * atoms + axis + 1, 0:atoms] = row

    base = atoms + sublanes
    for start in range(base, y_ref.shape[0], sublanes):
        y_ref[start : start + sublanes] = zero

    def store(row, lane, value):
        chunk, lane = divmod(lane, channels)
        at = base + chunk * sublanes + row
        y_ref[at : at + 1, lane : lane + pairs] = value.astype(f32)

    at_x, at_y = lax.axis_index("gx"), lax.axis_index("gy")
    lists = (src_ref, tgt_ref, mask_ref, spec_ref)
    near, other = gy_links[0].delta(at_y), gy_links[1].delta(at_y)
    partner = at_y + near
    to_far = (partner + (partner >> 1)) & 1
    write_rows(store, gx_spots, at_x, lists, near, 0, 0)
    write_rows(store, gx_spots, at_x, lists, other, 1 + to_far, len(gx_spots) * pairs)


def stack_kernel(rows, *refs):
    *refs, out_ref = refs
    for at, ref in enumerate(refs):
        out_ref[at * rows : (at + 1) * rows] = ref[0:rows]


def prep_kernel(
    gx_spots, gy_links, src_ref, tgt_ref, mask_ref, spec_ref, in_ref, emb_ref, out_ref,
    rows_ref, wide_ref, back_ref, first_ref, last_ref,
):
    pairs = src_ref.shape[4]
    rows_ref[...] = jnp.zeros(rows_ref.shape, jnp.int32)

    def store(row, lane, value):
        rows_ref[row : row + 1, lane : lane + pairs] = value

    at_x, at_y = lax.axis_index("gx"), lax.axis_index("gy")
    lists = (src_ref, tgt_ref, mask_ref, spec_ref)
    for place, link in enumerate((None, gy_links[2], gy_links[3])):
        step_y = 0 if link is None else link.delta(at_y)
        write_rows(store, gx_spots, at_x, lists, step_y, place, place * len(gx_spots) * pairs)
    high, low = pieces(out_ref[...], 2)
    wide_ref[...] = jnp.concatenate([high, high, low], axis=0).T.astype(bf16)
    upper = jnp.concatenate([high, high], axis=1)
    lower = jnp.concatenate([low, jnp.zeros_like(low)], axis=1)
    back_ref[...] = jnp.concatenate([upper, lower], axis=0).astype(bf16)
    orders, hidden = in_ref.shape
    spare = jnp.zeros((sublanes * 2 - emb_ref.shape[0], hidden), f32)
    high, low = pieces(jnp.concatenate([in_ref[...], emb_ref[...], spare], axis=0), 2)
    first_ref[...] = jnp.concatenate([high, high, low], axis=0).T.astype(bf16)
    last_ref[...] = jnp.concatenate([high[0:orders], high[0:orders], low[0:orders]], axis=1).astype(bf16)


def radial_waves(dist, orders):
    order = (lax.broadcasted_iota(jnp.int32, (orders, 1), 0) + 1).astype(f32)
    turn = order * (dist * (1.0 / cutoff))
    whole = jnp.floor(turn + 0.5)
    part = turn - whole
    sign = 1.0 - 2.0 * (whole - 2.0 * jnp.floor(0.5 * whole))
    square = part * part
    sine = jnp.zeros_like(square)
    for k in (11, 9, 7, 5, 3, 1):
        sine = sine * square + (-1.0) ** (k // 2) * math.pi**k / math.factorial(k)
    cosine = jnp.zeros_like(square)
    for k in (12, 10, 8, 6, 4, 2, 0):
        cosine = cosine * square + (-1.0) ** (k // 2) * math.pi**k / math.factorial(k)
    return order, sign * part * sine, sign * cosine


def thrice(x):
    high, low = pieces(x, 2)
    return jnp.concatenate([high, low, high], axis=0).astype(bf16)


def onehot(ids, count):
    return jnp.where(lax.broadcasted_iota(jnp.int32, (count, ids.shape[1]), 0) == ids, 1.0, 0.0)


def slot_grads(rows, cot_refs, columns, weights, orders):
    wide, back, first, last = weights
    slots = rows.shape[1]
    sources = columns[0][1].shape[1]
    channels = columns[0][2].shape[0]
    hidden = last.shape[1] // 3
    parts = len(degree)
    atoms = (cot_refs[0].shape[0] - sublanes) // parts
    targets = atoms * len(cot_refs)

    src_hot = onehot(rows[0:1], sources).astype(bf16)
    tgt_hot = onehot(rows[1:2], targets).astype(bf16)
    mask = rows[2:3].astype(f32)
    offset = rows[4:6].astype(f32) * domain_side

    tgt_pos = [jnp.concatenate(pieces(ref[parts * atoms :, 0:atoms], 3), axis=0) for ref in cot_refs]
    hots = [src_hot[:, lanes] for lanes, _, _ in columns]
    from_src = jnp.concatenate([dot(c[1], hot) for c, hot in zip(columns, hots)], axis=1)
    from_tgt = dot(jnp.concatenate(tgt_pos, axis=1).astype(bf16), tgt_hot)
    from_src = from_src[0:8] + from_src[8:16] + from_src[16:24]
    from_tgt = from_tgt[0:8] + from_tgt[8:16] + from_tgt[16:24]
    rel = [
        from_src[0:1] + offset[0:1] - from_tgt[0:1],
        from_src[1:2] + offset[1:2] - from_tgt[1:2],
        from_src[2:3] - from_tgt[2:3],
    ]
    dist = jnp.sqrt(rel[0] * rel[0] + rel[1] * rel[1] + rel[2] * rel[2] + soften)
    near = 1.0 / dist
    x, y, z = (r * near for r in rel)
    scaled = dist * (1.0 / cutoff)
    room = jnp.where(scaled < 1.0, 1.0 - scaled * scaled, 0.0)
    env = room * room * mask
    d_env = (-4.0 / cutoff) * scaled * room * mask

    order, sine, cosine = radial_waves(dist, orders)
    norm = math.sqrt(2.0 / cutoff)
    basis = norm * near * sine
    d_basis = norm * near * ((math.pi / cutoff) * order * cosine - sine * near)
    species = onehot(rows[3:4], 2 * sublanes)
    before = dot(first, thrice(jnp.concatenate([basis, species], axis=0)))
    gate = 1.0 / (1.0 + jnp.exp(-before))
    act = before * gate
    d_act = gate * (1.0 + before * (1.0 - gate))
    radial = dot(wide, thrice(act))
    gathered = jnp.concatenate(
        [dot(c[2], jnp.concatenate([hot, hot], axis=0)) for c, hot in zip(columns, hots)], axis=1
    )

    root3, root5, root15 = math.sqrt(3.0), math.sqrt(5.0), math.sqrt(15.0)
    shapes = [
        None, root3 * x, root3 * y, root3 * z, root15 * x * y, root15 * y * z,
        0.5 * root5 * (2.0 * z * z - x * x - y * y), root15 * x * z, 0.5 * root15 * (x * x - y * y),
    ]
    twice = lax.broadcasted_iota(jnp.int32, (2 * targets, slots), 0)
    twice = (twice // (2 * atoms)) * atoms + lax.rem(twice, atoms)
    twice = jnp.where(twice == rows[1:2], 1.0, 0.0).astype(bf16)
    d_shapes = [None] * parts
    d_radial = []
    through = None
    for low, high in ((0, 1), (1, 4), (4, 9)):
        l = len(d_radial)
        own = radial[l * channels : (l + 1) * channels]
        with_feats = own * gathered
        total = None
        for m in range(low, high):
            blocks = []
            for ref in cot_refs:
                blocks += pieces(ref[m * atoms : (m + 1) * atoms], 2)
            cot = dot_cols(jnp.concatenate(blocks, axis=0).astype(bf16), twice)
            if m:
                d_shapes[m] = jnp.sum(with_feats * cot, axis=0, keepdims=True) * env
                cot = cot * shapes[m]
            total = cot if total is None else total + cot
        d_radial.append(total * gathered)
        own = own * total
        through = own if through is None else through + own
    to_env = jnp.sum(through * gathered, axis=0, keepdims=True)
    through = through * env
    d_hidden = dot(back, jnp.concatenate(
        [p.astype(bf16) for p in pieces(jnp.concatenate(d_radial, axis=0), 2)], axis=0
    ))
    d_before = (d_hidden[0:hidden] + d_hidden[hidden:]) * (d_act * env)
    to_basis = dot(last, thrice(d_before))
    d_dist = jnp.sum(to_basis * d_basis, axis=0, keepdims=True) + to_env * d_env

    s = d_shapes
    d_x = root3 * s[1] + root15 * (y * s[4] + z * s[7] + x * s[8]) - root5 * x * s[6]
    d_y = root3 * s[2] + root15 * (x * s[4] + z * s[5] - y * s[8]) - root5 * y * s[6]
    d_z = root3 * s[3] + root15 * (y * s[5] + x * s[7]) + 2.0 * root5 * z * s[6]
    d_dist = d_dist - near * (x * d_x + y * d_y + z * d_z)
    grad = jnp.concatenate(
        [near * d_x + x * d_dist, near * d_y + y * d_dist, near * d_z + z * d_dist,
         jnp.zeros((sublanes - 3, slots), f32)], axis=0,
    )
    grad = jnp.concatenate(pieces(grad, 2), axis=0).astype(bf16)
    pos_tgt = dot_rows(grad, tgt_hot)
    through = [p.astype(bf16) for p in pieces(through, 2)]
    sums = []
    for (lanes, _, _), hot in zip(columns, hots):
        pos_src = dot_rows(grad[:, lanes], hot)
        feat_src = dot_rows(hot, through[0][:, lanes]) + dot_rows(hot, through[1][:, lanes])
        sums.append((pos_src[0:8] + pos_src[8:16], feat_src))
    return sums, -(pos_tgt[0:8] + pos_tgt[8:16])


def tiles_kernel(orders, tables, homes, rows_ref, *refs):
    refs = list(refs)
    weights = [refs.pop(0)[...] for _ in range(4)]
    y_ref = refs.pop(0)
    block_refs = [refs.pop(0) for _ in range(1 + max(ref for column in tables for ref, _ in column))]
    cot_refs = [refs.pop(0) for _ in range(3)]
    *outs, near_ref, far_ref, place = refs
    atoms = (cot_refs[0].shape[0] - sublanes) // len(degree)
    block = atoms + sublanes
    own_rows = rows_ref[...]
    chunks = [y_ref[at : at + sublanes] for at in range(block, y_ref.shape[0], sublanes)]
    rows = jnp.concatenate([own_rows, jnp.concatenate(chunks, axis=1).astype(jnp.int32)], axis=1)
    split = own_rows.shape[1]
    columns = []
    for at, column in enumerate(tables):
        views = [block_refs[ref].at[start * block : (start + 1) * block] for ref, start in column]
        for table, ref in enumerate(views):
            place[at, :, table * atoms : (table + 1) * atoms] = ref[atoms:, 0:atoms]
        src_pos = jnp.concatenate(pieces(place[at], 3), axis=0).astype(bf16)
        feats = pieces(jnp.concatenate([ref[0:atoms] for ref in views], axis=0), 2)
        lanes = slice(split, None) if at else slice(0, split)
        columns.append((lanes, src_pos, jnp.concatenate(feats, axis=0).T.astype(bf16)))
    sums, pos_tgt = slot_grads(rows, cot_refs, columns, weights, orders)
    for ref, home in zip(outs, homes):
        for at, (column, table) in enumerate(home):
            pos_src, feat_src = sums[column]
            part = slice(table * atoms, (table + 1) * atoms)
            pos = pos_src[:, part]
            if column == 0 and table == 0:
                pos = pos + pos_tgt[:, 0:atoms]
            ref[at * block : at * block + atoms] = feat_src[part]
            ref[at * block + atoms : (at + 1) * block] = jnp.zeros((sublanes, ref.shape[1]), f32)
            ref[at * block + atoms : (at + 1) * block, 0:atoms] = pos
    for at, ref in ((1, near_ref), (2, far_ref)):
        ref[...] = jnp.zeros(ref.shape, f32)
        ref[0:sublanes, 0:atoms] = pos_tgt[:, at * atoms : (at + 1) * atoms]


def add_kernel(count, *refs):
    total = refs[0][...]
    for ref in refs[1:count]:
        total = total + ref[...]
    rows = total.shape[0] // len(refs[count:])
    for at, ref in enumerate(refs[count:]):
        ref[...] = total[at * rows : (at + 1) * rows]


def sum_kernel(gx_count, *refs):
    gx_refs, gy_refs = refs[:gx_count], refs[gx_count:-2]
    pos_ref, feat_ref = refs[-2:]
    atoms = pos_ref.shape[3]
    feat = gx_refs[0][...]
    for ref in gx_refs[1:]:
        feat = feat + ref[...]
    pos = feat[atoms : atoms + 3, 0:atoms]
    for ref in gy_refs:
        pos = pos + ref[0:3, 0:atoms]
    for axis in range(3):
        pos_ref[0, axis] = pos[axis : axis + 1]
    feat_ref[0, 0] = feat[0:atoms]


vmem = pl.BlockSpec(memory_space=pltpu.VMEM)


def call(kernel, name, out_shape, operands, scratch=(), room=4, us=None):
    return pl.pallas_call(
        kernel,
        out_shape=out_shape,
        in_specs=[vmem] * len(operands),
        out_specs=(vmem,) * len(out_shape),
        scratch_shapes=list(scratch),
        compiler_params=pltpu.CompilerParams(vmem_limit_bytes=room and room * megabyte),
        name=name,
        cost_estimate=us and pl.CostEstimate(
            flops=int(us * 1e9), bytes_accessed=0, transcendentals=0
        ),
    )(*operands)


def local(
    gx_size, gy_size, positions, features, cotangent, nbr_src, nbr_tgt, pair_mask, pair_species,
    w_in, species_emb, w_out,
):
    atoms, channels = features.shape[2:]
    steps, _, pairs = nbr_src.shape[2:]
    orders, hidden = w_in.shape
    slots = steps * pairs
    gx_links, gy_links = links_of(gx_size), links_of(gy_size)
    gx_spots = gx_spots_of(gx_links)
    sources = (len(gx_links) + 1) * atoms
    block = atoms + sublanes
    sds = jax.ShapeDtypeStruct

    by_axis = jnp.transpose(positions, (0, 2, 1, 3))
    lists = [jnp.transpose(x, (0, 2, 3, 1, 4)) for x in (nbr_src, nbr_tgt, pair_mask, pair_species)]
    gx_pack = sds((block, channels), f32)
    y_pack = sds((block + -(-2 * slots // channels) * sublanes, channels), f32)
    gy_pack = sds((len(degree) * atoms + sublanes, channels), f32)
    own, y_own, cot_own = call(
        functools.partial(pack_kernel, gx_spots, gy_links), "pack", (gx_pack, y_pack, gy_pack),
        (by_axis, features, cotangent, *lists), room=None,
    )
    y = gy_links[0].swap(y_own, "gy")
    (two,) = call(
        functools.partial(stack_kernel, block), "stack", (sds((2 * block, channels), f32),),
        (own, y), us=2,
    )
    blocks = [own, y] + [link.swap(two, "gx") for link in gx_links]
    tables = tuple(
        ((at, 0),) + tuple((2 + l, at) for l in range(len(gx_links))) for at in range(2)
    )
    homes = tuple(((0, table), (1, table)) for table in range(len(gx_links) + 1))
    far_links = (gy_links[3], gy_links[2])
    cot_far, cot_near = (link.swap(cot_own, "gy") for link in far_links)

    own_lanes = -(-3 * slots // channels) * channels
    rows, *weights = call(
        functools.partial(prep_kernel, gx_spots, gy_links),
        "prepare",
        (
            sds((sublanes, own_lanes), jnp.int32),
            sds((w_out.shape[1], 3 * hidden), bf16),
            sds((2 * hidden, 2 * w_out.shape[1]), bf16),
            sds((hidden, 3 * (orders + 2 * sublanes)), bf16),
            sds((orders, 3 * hidden), bf16),
        ),
        (*lists, w_in, species_emb, w_out),
    )
    far_pack = sds((channels // 2, channels), f32)
    *sent, near, far = call(
        functools.partial(tiles_kernel, orders, tables, homes), "tiles",
        tuple(sds((len(home) * block, channels), f32) for home in homes) + (far_pack,) * 2,
        (rows, *weights, y, *blocks, cot_own, cot_near, cot_far),
        [pltpu.VMEM((2, sublanes, sources), f32)], 32,
    )
    back_gy = [link.swap(value, "gy") for link, value in zip(far_links, (far, near))]
    came = [link.swap(value, "gx") for link, value in zip(gx_links, sent[1:])]
    own, y = call(
        functools.partial(add_kernel, len(sent)), "add", (gx_pack,) * 2, (sent[0], *came)
    )
    back = [own, gy_links[0].swap(y, "gy")]
    pos, feat = call(
        functools.partial(sum_kernel, len(back)), "sums",
        (sds(by_axis.shape, f32), sds(features.shape, f32)),
        (*back, *back_gy),
    )
    return jnp.transpose(pos, (0, 2, 1, 3)), feat


def solution(mesh):
    split = [P("gx", "gy")] * 7 + [P()] * 3
    return jax.shard_map(
        functools.partial(local, mesh.shape["gx"], mesh.shape["gy"]),
        mesh=mesh,
        in_specs=tuple(split),
        out_specs=(P("gx", "gy"), P("gx", "gy")),
        check_vma=False,
    )
```

```python
import functools
import math

import jax
import jax.numpy as jnp
from jax import lax
from jax.experimental import pallas as pl
from jax.experimental.pallas import tpu as pltpu
from jax.sharding import PartitionSpec as P

domain_side = 5.0
cutoff = 12.0
soften = 0.25
reach = 2
sublanes = 8
degree = (0, 1, 1, 1, 2, 2, 2, 2, 2)
megabyte = 1024 * 1024
f32 = jnp.float32
bf16 = jnp.bfloat16


class Link:
    def __init__(self, step, bit, peers):
        self.step, self.bit, self.peers = step, bit, peers

    def delta(self, i):
        return self.step * (1 - 2 * ((i >> self.bit) & 1))

    def swap(self, value, axis):
        n = self.peers
        return lax.ppermute(value, axis, [(i, (i + self.delta(i)) % n) for i in range(n)])


def links_of(peers):
    assert peers % 4 == 0, peers
    steps = [(1, 0), (-1, 0), (2, 1)] + ([(-2, 1)] if peers > 4 else [])
    return [Link(step, bit, peers) for step, bit in steps]


def gx_spots_of(links):
    spots = [(0, None, 0)]
    for table, link in enumerate(links):
        spots.append((table + 1, link, 1))
        if link.peers == 4 and abs(link.step) == 2:
            spots.append((table + 1, link, -1))
    return spots


def pieces(x, count):
    out = []
    for _ in range(count):
        out.append(x.astype(bf16).astype(f32))
        x = x - out[-1]
    return out


def dot(a, b):
    return jnp.dot(a, b, preferred_element_type=f32)


def dot_rows(a, b):
    return lax.dot_general(a, b, (((1,), (1,)), ((), ())), preferred_element_type=f32)


def dot_cols(a, b):
    return lax.dot_general(a, b, (((0,), (0,)), ((), ())), preferred_element_type=f32)


def write_rows(store, gx_spots, at_x, lists, step_y, place, start):
    atoms = pairs = lists[0].shape[4]
    for slot, (table, link, sign) in enumerate(gx_spots):
        step_x = 0 if link is None else sign * link.delta(at_x)
        src, tgt, mask, spec = (ref[0, reach + step_x, reach + step_y] for ref in lists)
        store(0, start + slot * pairs, src + table * atoms)
        store(1, start + slot * pairs, tgt + place * atoms)
        store(2, start + slot * pairs, mask)
        store(3, start + slot * pairs, spec)
        store(4, start + slot * pairs, jnp.full((1, pairs), step_x, jnp.int32))
        store(5, start + slot * pairs, jnp.full((1, pairs), -step_y, jnp.int32))


def pack_kernel(
    gx_spots, gy_links, pos_ref, feat_ref, cot_ref, src_ref, tgt_ref, mask_ref, spec_ref,
    gx_ref, y_ref, gy_ref,
):
    atoms, channels = feat_ref.shape[2:]
    pairs = src_ref.shape[4]
    parts = len(degree)
    zero = jnp.zeros((sublanes, channels), f32)
    for ref in (gx_ref, y_ref):
        ref[0:atoms] = feat_ref[0, 0]
        ref[atoms : atoms + sublanes] = zero
    for m in range(parts):
        gy_ref[m * atoms : (m + 1) * atoms] = cot_ref[0, 0, :, m * channels : (m + 1) * channels]
    gy_ref[parts * atoms :] = zero
    for axis in range(3):
        row = pos_ref[0, axis]
        gx_ref[atoms + axis : atoms + axis + 1, 0:atoms] = row
        y_ref[atoms + axis : atoms + axis + 1, 0:atoms] = row
        gy_ref[parts * atoms + axis : parts * atoms + axis + 1, 0:atoms] = row

    base = atoms + sublanes
    for start in range(base, y_ref.shape[0], sublanes):
        y_ref[start : start + sublanes] = zero

    def store(row, lane, value):
        chunk, lane = divmod(lane, channels)
        at = base + chunk * sublanes + row
        y_ref[at : at + 1, lane : lane + pairs] = value.astype(f32)

    at_x, at_y = lax.axis_index("gx"), lax.axis_index("gy")
    lists = (src_ref, tgt_ref, mask_ref, spec_ref)
    near, other = gy_links[0].delta(at_y), gy_links[1].delta(at_y)
    partner = at_y + near
    to_far = (partner + (partner >> 1)) & 1
    lanes = -(-len(gx_spots) * pairs // channels) * channels
    write_rows(store, gx_spots, at_x, lists, near, 0, 0)
    write_rows(store, gx_spots, at_x, lists, other, to_far, lanes)


def stack_kernel(rows, *refs):
    *refs, _, out_ref = refs
    for at, ref in enumerate(refs):
        out_ref[at * rows : (at + 1) * rows] = ref[0:rows]


def prep_kernel(
    gx_spots, gy_links, src_ref, tgt_ref, mask_ref, spec_ref, in_ref, emb_ref, out_ref,
    early_ref, late_ref, wide_ref, back_ref, first_ref, last_ref,
):
    pairs = src_ref.shape[4]
    at_x, at_y = lax.axis_index("gx"), lax.axis_index("gy")
    lists = (src_ref, tgt_ref, mask_ref, spec_ref)
    for rows_ref, links in ((early_ref, (None,)), (late_ref, (gy_links[2], gy_links[3]))):
        rows_ref[...] = jnp.zeros(rows_ref.shape, jnp.int32)

        def store(row, lane, value, rows_ref=rows_ref):
            rows_ref[row : row + 1, lane : lane + pairs] = value

        for place, link in enumerate(links):
            step_y = 0 if link is None else link.delta(at_y)
            write_rows(store, gx_spots, at_x, lists, step_y, place, place * len(gx_spots) * pairs)
    high, low = pieces(out_ref[...], 2)
    wide_ref[...] = jnp.concatenate([high, high, low], axis=0).T.astype(bf16)
    upper = jnp.concatenate([high, high], axis=1)
    lower = jnp.concatenate([low, jnp.zeros_like(low)], axis=1)
    back_ref[...] = jnp.concatenate([upper, lower], axis=0).astype(bf16)
    orders, hidden = in_ref.shape
    spare = jnp.zeros((sublanes * 2 - emb_ref.shape[0], hidden), f32)
    high, low = pieces(jnp.concatenate([in_ref[...], emb_ref[...], spare], axis=0), 2)
    first_ref[...] = jnp.concatenate([high, high, low], axis=0).T.astype(bf16)
    last_ref[...] = jnp.concatenate([high[0:orders], high[0:orders], low[0:orders]], axis=1).astype(bf16)


def radial_waves(dist, orders):
    order = (lax.broadcasted_iota(jnp.int32, (orders, 1), 0) + 1).astype(f32)
    turn = order * (dist * (1.0 / cutoff))
    whole = jnp.floor(turn + 0.5)
    part = turn - whole
    sign = 1.0 - 2.0 * (whole - 2.0 * jnp.floor(0.5 * whole))
    square = part * part
    sine = jnp.zeros_like(square)
    for k in (11, 9, 7, 5, 3, 1):
        sine = sine * square + (-1.0) ** (k // 2) * math.pi**k / math.factorial(k)
    cosine = jnp.zeros_like(square)
    for k in (12, 10, 8, 6, 4, 2, 0):
        cosine = cosine * square + (-1.0) ** (k // 2) * math.pi**k / math.factorial(k)
    return order, sign * part * sine, sign * cosine


def thrice(x):
    high, low = pieces(x, 2)
    return jnp.concatenate([high, low, high], axis=0).astype(bf16)


def onehot(ids, count):
    return jnp.where(lax.broadcasted_iota(jnp.int32, (count, ids.shape[1]), 0) == ids, 1.0, 0.0)


def slot_grads(rows, cot_refs, columns, weights, orders):
    wide, back, first, last = weights
    slots = rows.shape[1]
    sources = columns[0][1].shape[1]
    channels = columns[0][2].shape[0]
    hidden = last.shape[1] // 3
    parts = len(degree)
    atoms = (cot_refs[0].shape[0] - sublanes) // parts
    targets = atoms * len(cot_refs)

    src_hot = onehot(rows[0:1], sources).astype(bf16)
    tgt_hot = onehot(rows[1:2], targets).astype(bf16)
    mask = rows[2:3].astype(f32)
    offset = rows[4:6].astype(f32) * domain_side

    tgt_pos = [jnp.concatenate(pieces(ref[parts * atoms :, 0:atoms], 3), axis=0) for ref in cot_refs]
    hots = [src_hot[:, lanes] for lanes, _, _ in columns]
    from_src = jnp.concatenate([dot(c[1], hot) for c, hot in zip(columns, hots)], axis=1)
    from_tgt = dot(jnp.concatenate(tgt_pos, axis=1).astype(bf16), tgt_hot)
    from_src = from_src[0:8] + from_src[8:16] + from_src[16:24]
    from_tgt = from_tgt[0:8] + from_tgt[8:16] + from_tgt[16:24]
    rel = [
        from_src[0:1] + offset[0:1] - from_tgt[0:1],
        from_src[1:2] + offset[1:2] - from_tgt[1:2],
        from_src[2:3] - from_tgt[2:3],
    ]
    dist = jnp.sqrt(rel[0] * rel[0] + rel[1] * rel[1] + rel[2] * rel[2] + soften)
    near = 1.0 / dist
    x, y, z = (r * near for r in rel)
    scaled = dist * (1.0 / cutoff)
    room = jnp.where(scaled < 1.0, 1.0 - scaled * scaled, 0.0)
    env = room * room * mask
    d_env = (-4.0 / cutoff) * scaled * room * mask

    order, sine, cosine = radial_waves(dist, orders)
    norm = math.sqrt(2.0 / cutoff)
    basis = norm * near * sine
    d_basis = norm * near * ((math.pi / cutoff) * order * cosine - sine * near)
    species = onehot(rows[3:4], 2 * sublanes)
    before = dot(first, thrice(jnp.concatenate([basis, species], axis=0)))
    gate = 1.0 / (1.0 + jnp.exp(-before))
    act = before * gate
    d_act = gate * (1.0 + before * (1.0 - gate))
    radial = dot(wide, thrice(act))
    gathered = jnp.concatenate(
        [dot(c[2], jnp.concatenate([hot, hot], axis=0)) for c, hot in zip(columns, hots)], axis=1
    )

    root3, root5, root15 = math.sqrt(3.0), math.sqrt(5.0), math.sqrt(15.0)
    shapes = [
        None, root3 * x, root3 * y, root3 * z, root15 * x * y, root15 * y * z,
        0.5 * root5 * (2.0 * z * z - x * x - y * y), root15 * x * z, 0.5 * root15 * (x * x - y * y),
    ]
    twice = lax.broadcasted_iota(jnp.int32, (2 * targets, slots), 0)
    twice = (twice // (2 * atoms)) * atoms + lax.rem(twice, atoms)
    twice = jnp.where(twice == rows[1:2], 1.0, 0.0).astype(bf16)
    d_shapes = [None] * parts
    d_radial = []
    through = None
    for low, high in ((0, 1), (1, 4), (4, 9)):
        l = len(d_radial)
        own = radial[l * channels : (l + 1) * channels]
        with_feats = own * gathered
        total = None
        for m in range(low, high):
            blocks = []
            for ref in cot_refs:
                blocks += pieces(ref[m * atoms : (m + 1) * atoms], 2)
            cot = dot_cols(jnp.concatenate(blocks, axis=0).astype(bf16), twice)
            if m:
                d_shapes[m] = jnp.sum(with_feats * cot, axis=0, keepdims=True) * env
                cot = cot * shapes[m]
            total = cot if total is None else total + cot
        d_radial.append(total * gathered)
        own = own * total
        through = own if through is None else through + own
    to_env = jnp.sum(through * gathered, axis=0, keepdims=True)
    through = through * env
    d_hidden = dot(back, jnp.concatenate(
        [p.astype(bf16) for p in pieces(jnp.concatenate(d_radial, axis=0), 2)], axis=0
    ))
    d_before = (d_hidden[0:hidden] + d_hidden[hidden:]) * (d_act * env)
    to_basis = dot(last, thrice(d_before))
    d_dist = jnp.sum(to_basis * d_basis, axis=0, keepdims=True) + to_env * d_env

    s = d_shapes
    d_x = root3 * s[1] + root15 * (y * s[4] + z * s[7] + x * s[8]) - root5 * x * s[6]
    d_y = root3 * s[2] + root15 * (x * s[4] + z * s[5] - y * s[8]) - root5 * y * s[6]
    d_z = root3 * s[3] + root15 * (y * s[5] + x * s[7]) + 2.0 * root5 * z * s[6]
    d_dist = d_dist - near * (x * d_x + y * d_y + z * d_z)
    grad = jnp.concatenate(
        [near * d_x + x * d_dist, near * d_y + y * d_dist, near * d_z + z * d_dist,
         jnp.zeros((sublanes - 3, slots), f32)], axis=0,
    )
    grad = jnp.concatenate(pieces(grad, 2), axis=0).astype(bf16)
    pos_tgt = dot_rows(grad, tgt_hot)
    through = [p.astype(bf16) for p in pieces(through, 2)]
    sums = []
    for (lanes, _, _), hot in zip(columns, hots):
        pos_src = dot_rows(grad[:, lanes], hot)
        feat_src = dot_rows(hot, through[0][:, lanes]) + dot_rows(hot, through[1][:, lanes])
        sums.append((pos_src[0:8] + pos_src[8:16], feat_src))
    return sums, -(pos_tgt[0:8] + pos_tgt[8:16])


def all_rows(rows_ref, y_ref, block, late):
    own = rows_ref[...]
    count = (y_ref.shape[0] - block) // (2 * sublanes)
    start = block + late * count * sublanes
    chunks = [y_ref[start + at * sublanes : start + (at + 1) * sublanes] for at in range(count)]
    rows = jnp.concatenate([own, jnp.concatenate(chunks, axis=1).astype(jnp.int32)], axis=1)
    return rows, (slice(0, own.shape[1]), slice(own.shape[1], None))


def early_kernel(orders, tables, rows_ref, *refs):
    refs = list(refs)
    weights = [refs.pop(0)[...] for _ in range(4)]
    y_ref = refs.pop(0)
    block_refs = [refs.pop(0) for _ in range(1 + max(ref for column in tables for ref, _ in column))]
    cot_ref = refs.pop(0)
    *outs, place = refs
    atoms = (cot_ref.shape[0] - sublanes) // len(degree)
    block = atoms + sublanes
    rows, lanes = all_rows(rows_ref, y_ref, block, 0)
    columns = []
    for at, column in enumerate(tables):
        views = [block_refs[ref].at[start * block : (start + 1) * block] for ref, start in column]
        for table, ref in enumerate(views):
            place[at, :, table * atoms : (table + 1) * atoms] = ref[atoms:, 0:atoms]
        src_pos = jnp.concatenate(pieces(place[at], 3), axis=0).astype(bf16)
        feats = pieces(jnp.concatenate([ref[0:atoms] for ref in views], axis=0), 2)
        feats = jnp.concatenate(feats, axis=0).T.astype(bf16)
        outs[4 * at][...] = src_pos
        outs[4 * at + 1][...] = feats
        columns.append((lanes[at], src_pos, feats))
    sums, pos_tgt = slot_grads(rows, [cot_ref], columns, weights, orders)
    for at, (pos, feat) in enumerate(sums):
        outs[4 * at + 2][...] = pos
        outs[4 * at + 3][...] = feat
    outs[2][:, 0:atoms] = sums[0][0][:, 0:atoms] + pos_tgt


def late_kernel(orders, homes, rows_ref, *refs):
    refs = list(refs)
    weights = [refs.pop(0)[...] for _ in range(4)]
    y_ref = refs.pop(0)
    held = [refs.pop(0) for _ in range(8)]
    cot_refs = [refs.pop(0) for _ in range(2)]
    *outs, near_ref, far_ref = refs
    atoms = (cot_refs[0].shape[0] - sublanes) // len(degree)
    block = atoms + sublanes
    rows, lanes = all_rows(rows_ref, y_ref, block, 1)
    columns = [(lanes[at], held[4 * at][...], held[4 * at + 1][...]) for at in range(2)]
    sums, pos_tgt = slot_grads(rows, cot_refs, columns, weights, orders)
    sums = [
        (pos + held[4 * at + 2][...], feat + held[4 * at + 3][...])
        for at, (pos, feat) in enumerate(sums)
    ]
    for ref, home in zip(outs, homes):
        for at, (column, table) in enumerate(home):
            pos, feat = sums[column]
            part = slice(table * atoms, (table + 1) * atoms)
            ref[at * block : at * block + atoms] = feat[part]
            ref[at * block + atoms : (at + 1) * block] = jnp.zeros((sublanes, ref.shape[1]), f32)
            ref[at * block + atoms : (at + 1) * block, 0:atoms] = pos[:, part]
    for at, ref in enumerate((near_ref, far_ref)):
        ref[...] = jnp.zeros(ref.shape, f32)
        ref[0:sublanes, 0:atoms] = pos_tgt[:, at * atoms : (at + 1) * atoms]


def add_kernel(count, *refs):
    total = refs[0][...]
    for ref in refs[1:count]:
        total = total + ref[...]
    rows = total.shape[0] // len(refs[count:])
    for at, ref in enumerate(refs[count:]):
        ref[...] = total[at * rows : (at + 1) * rows]


def sum_kernel(gx_count, *refs):
    gx_refs, gy_refs = refs[:gx_count], refs[gx_count:-2]
    pos_ref, feat_ref = refs[-2:]
    atoms = pos_ref.shape[3]
    feat = gx_refs[0][...]
    for ref in gx_refs[1:]:
        feat = feat + ref[...]
    pos = feat[atoms : atoms + 3, 0:atoms]
    for ref in gy_refs:
        pos = pos + ref[0:3, 0:atoms]
    for axis in range(3):
        pos_ref[0, axis] = pos[axis : axis + 1]
    feat_ref[0, 0] = feat[0:atoms]


vmem = pl.BlockSpec(memory_space=pltpu.VMEM)


def call(kernel, name, out_shape, operands, scratch=(), room=4, us=None):
    return pl.pallas_call(
        kernel,
        out_shape=out_shape,
        in_specs=[vmem] * len(operands),
        out_specs=(vmem,) * len(out_shape),
        scratch_shapes=list(scratch),
        compiler_params=pltpu.CompilerParams(vmem_limit_bytes=room and room * megabyte),
        name=name,
        cost_estimate=us and pl.CostEstimate(
            flops=int(us * 1e9), bytes_accessed=0, transcendentals=0
        ),
    )(*operands)


def local(
    gx_size, gy_size, positions, features, cotangent, nbr_src, nbr_tgt, pair_mask, pair_species,
    w_in, species_emb, w_out,
):
    atoms, channels = features.shape[2:]
    steps, _, pairs = nbr_src.shape[2:]
    orders, hidden = w_in.shape
    slots = steps * pairs
    gx_links, gy_links = links_of(gx_size), links_of(gy_size)
    gx_spots = gx_spots_of(gx_links)
    sources = (len(gx_links) + 1) * atoms
    block = atoms + sublanes
    sds = jax.ShapeDtypeStruct

    by_axis = jnp.transpose(positions, (0, 2, 1, 3))
    lists = [jnp.transpose(x, (0, 2, 3, 1, 4)) for x in (nbr_src, nbr_tgt, pair_mask, pair_species)]
    gx_pack = sds((block, channels), f32)
    y_pack = sds((block + 2 * -(-slots // channels) * sublanes, channels), f32)
    gy_pack = sds((len(degree) * atoms + sublanes, channels), f32)
    own, y_own, cot_own = call(
        functools.partial(pack_kernel, gx_spots, gy_links), "pack", (gx_pack, y_pack, gy_pack),
        (by_axis, features, cotangent, *lists), room=None,
    )
    far_links = (gy_links[3], gy_links[2])
    y = gy_links[0].swap(y_own, "gy")
    tables = tuple(
        ((at, 0),) + tuple((2 + l, at) for l in range(len(gx_links))) for at in range(2)
    )
    homes = tuple(((0, table), (1, table)) for table in range(len(gx_links) + 1))

    early_rows, late_rows, *weights = call(
        functools.partial(prep_kernel, gx_spots, gy_links),
        "prepare",
        (
            *(sds((sublanes, -(-n * slots // channels) * channels), jnp.int32) for n in (1, 2)),
            sds((w_out.shape[1], 3 * hidden), bf16),
            sds((2 * hidden, 2 * w_out.shape[1]), bf16),
            sds((hidden, 3 * (orders + 2 * sublanes)), bf16),
            sds((orders, 3 * hidden), bf16),
        ),
        (*lists, w_in, species_emb, w_out), us=3,
    )
    late_cot = lax.optimization_barrier((cot_own, weights[-1]))[0]
    cot_far, cot_near = (link.swap(late_cot, "gy") for link in far_links)
    (two,) = call(
        functools.partial(stack_kernel, block), "stack", (sds((2 * block, channels), f32),),
        (own, y, weights[-1]), us=2,
    )
    blocks = [own, y] + [link.swap(two, "gx") for link in gx_links]
    column = (
        sds((3 * sublanes, sources), bf16), sds((channels, 2 * sources), bf16),
        sds((sublanes, sources), f32), sds((sources, channels), f32),
    )
    held = call(
        functools.partial(early_kernel, orders, tables), "early_tiles", column * 2,
        (early_rows, *weights, y, *blocks, cot_own), [pltpu.VMEM((2, sublanes, sources), f32)], 24,
    )
    far_pack = sds((channels // 2, channels), f32)
    *sent, near, far = call(
        functools.partial(late_kernel, orders, homes), "late_tiles",
        tuple(sds((len(home) * block, channels), f32) for home in homes) + (far_pack,) * 2,
        (late_rows, *weights, y, *held, cot_near, cot_far), room=24,
    )
    back_gy = [link.swap(value, "gy") for link, value in zip(far_links, (far, near))]
    came = [link.swap(value, "gx") for link, value in zip(gx_links, sent[1:])]
    own, y = call(
        functools.partial(add_kernel, len(sent)), "add", (gx_pack,) * 2, (sent[0], *came)
    )
    back = [own, gy_links[0].swap(y, "gy")]
    pos, feat = call(
        functools.partial(sum_kernel, len(back)), "sums",
        (sds(by_axis.shape, f32), sds(features.shape, f32)),
        (*back, *back_gy),
    )
    return jnp.transpose(pos, (0, 2, 1, 3)), feat


def solution(mesh):
    split = [P("gx", "gy")] * 7 + [P()] * 3
    return jax.shard_map(
        functools.partial(local, mesh.shape["gx"], mesh.shape["gy"]),
        mesh=mesh,
        in_specs=tuple(split),
        out_specs=(P("gx", "gy"), P("gx", "gy")),
        check_vma=False,
    )
```

```python
import functools
import math

import jax
import jax.numpy as jnp
from jax import lax
from jax.experimental import pallas as pl
from jax.experimental.pallas import tpu as pltpu
from jax.sharding import PartitionSpec as P

domain_side = 5.0
cutoff = 12.0
soften = 0.25
reach = 2
sublanes = 8
degree = (0, 1, 1, 1, 2, 2, 2, 2, 2)
megabyte = 1024 * 1024
f32 = jnp.float32
bf16 = jnp.bfloat16


class Link:
    def __init__(self, step, bit, peers):
        self.step, self.bit, self.peers = step, bit, peers

    def delta(self, i):
        return self.step * (1 - 2 * ((i >> self.bit) & 1))

    def swap(self, value, axis):
        n = self.peers
        return lax.ppermute(value, axis, [(i, (i + self.delta(i)) % n) for i in range(n)])


def links_of(peers):
    assert peers % 4 == 0, peers
    steps = [(1, 0), (-1, 0), (2, 1)] + ([(-2, 1)] if peers > 4 else [])
    return [Link(step, bit, peers) for step, bit in steps]


def gx_spots_of(links):
    spots = [(0, None, 0)]
    for table, link in enumerate(links):
        spots.append((table + 1, link, 1))
        if link.peers == 4 and abs(link.step) == 2:
            spots.append((table + 1, link, -1))
    return spots


def pieces(x, count):
    out = []
    for _ in range(count):
        out.append(x.astype(bf16).astype(f32))
        x = x - out[-1]
    return out


def dot(a, b):
    return jnp.dot(a, b, preferred_element_type=f32)


def dot_rows(a, b):
    return lax.dot_general(a, b, (((1,), (1,)), ((), ())), preferred_element_type=f32)


def dot_cols(a, b):
    return lax.dot_general(a, b, (((0,), (0,)), ((), ())), preferred_element_type=f32)


def write_rows(store, gx_spots, at_x, lists, step_y, place, start, first_source=0):
    atoms = pairs = lists[0].shape[4]
    for slot, (table, link, sign) in enumerate(gx_spots):
        step_x = 0 if link is None else sign * link.delta(at_x)
        src, tgt, mask, spec = (ref[0, reach + step_x, reach + step_y] for ref in lists)
        store(0, start + slot * pairs, src + (first_source + table * atoms))
        store(1, start + slot * pairs, tgt + place * atoms)
        store(2, start + slot * pairs, mask)
        store(3, start + slot * pairs, spec)
        store(4, start + slot * pairs, jnp.full((1, pairs), step_x, jnp.int32))
        store(5, start + slot * pairs, jnp.full((1, pairs), -step_y, jnp.int32))


def pack_kernel(
    gx_spots, gy_links, pos_ref, feat_ref, cot_ref, src_ref, tgt_ref, mask_ref, spec_ref,
    gx_ref, y_ref, gy_ref,
):
    atoms, channels = feat_ref.shape[2:]
    pairs = src_ref.shape[4]
    parts = len(degree)
    zero = jnp.zeros((sublanes, channels), f32)
    for ref in (gx_ref, y_ref):
        ref[0:atoms] = feat_ref[0, 0]
        ref[atoms : atoms + sublanes] = zero
    for m in range(parts):
        gy_ref[m * atoms : (m + 1) * atoms] = cot_ref[0, 0, :, m * channels : (m + 1) * channels]
    gy_ref[parts * atoms :] = zero
    for axis in range(3):
        row = pos_ref[0, axis]
        gx_ref[atoms + axis : atoms + axis + 1, 0:atoms] = row
        y_ref[atoms + axis : atoms + axis + 1, 0:atoms] = row
        gy_ref[parts * atoms + axis : parts * atoms + axis + 1, 0:atoms] = row

    block = atoms + sublanes
    for start in range(block, y_ref.shape[0], sublanes):
        y_ref[start : start + sublanes] = zero

    def store(row, lane, value):
        chunk, lane = divmod(lane, channels)
        at = block + chunk * sublanes + row
        y_ref[at : at + 1, lane : lane + pairs] = value.astype(f32)

    at_x, at_y = lax.axis_index("gx"), lax.axis_index("gy")
    lists = (src_ref, tgt_ref, mask_ref, spec_ref)
    near, other = gy_links[0].delta(at_y), gy_links[1].delta(at_y)
    partner = at_y + near
    to_far = (partner + (partner >> 1)) & 1
    sources = (1 + max(table for table, _, _ in gx_spots)) * atoms
    slots = len(gx_spots) * pairs
    lane = 0
    for own, step_y, place in ((1, near, 0), (2, other, to_far)):
        base, chunks = partner_chunks(own * slots, slots, channels)
        start = lane + own * slots - base
        write_rows(store, gx_spots, at_x, lists, step_y, place, start, sources)
        lane += chunks * channels


def stack_kernel(rows, *refs):
    *refs, _, out_ref = refs
    for at, ref in enumerate(refs):
        out_ref[at * rows : (at + 1) * rows] = ref[0:rows]


def prep_kernel(
    gx_spots, gy_links, src_ref, tgt_ref, mask_ref, spec_ref, in_ref, emb_ref, out_ref,
    early_ref, late_ref, wide_ref, back_ref, first_ref, last_ref,
):
    pairs = src_ref.shape[4]
    at_x, at_y = lax.axis_index("gx"), lax.axis_index("gy")
    lists = (src_ref, tgt_ref, mask_ref, spec_ref)
    for rows_ref, links in ((early_ref, (None,)), (late_ref, (gy_links[2], gy_links[3]))):
        rows_ref[...] = jnp.zeros(rows_ref.shape, jnp.int32)

        def store(row, lane, value, rows_ref=rows_ref):
            rows_ref[row : row + 1, lane : lane + pairs] = value

        for place, link in enumerate(links):
            step_y = 0 if link is None else link.delta(at_y)
            write_rows(store, gx_spots, at_x, lists, step_y, place, place * len(gx_spots) * pairs)
    high, low = pieces(out_ref[...], 2)
    wide_ref[...] = jnp.concatenate([high, high, low], axis=0).T.astype(bf16)
    upper = jnp.concatenate([high, high], axis=1)
    lower = jnp.concatenate([low, jnp.zeros_like(low)], axis=1)
    back_ref[...] = jnp.concatenate([upper, lower], axis=0).astype(bf16)
    orders, hidden = in_ref.shape
    spare = jnp.zeros((sublanes * 2 - emb_ref.shape[0], hidden), f32)
    high, low = pieces(jnp.concatenate([in_ref[...], emb_ref[...], spare], axis=0), 2)
    first_ref[...] = jnp.concatenate([high, high, low], axis=0).T.astype(bf16)
    last_ref[...] = jnp.concatenate([high[0:orders], high[0:orders], low[0:orders]], axis=1).astype(bf16)


def radial_waves(dist, orders):
    order = (lax.broadcasted_iota(jnp.int32, (orders, 1), 0) + 1).astype(f32)
    turn = order * (dist * (1.0 / cutoff))
    whole = jnp.floor(turn + 0.5)
    part = turn - whole
    sign = 1.0 - 2.0 * (whole - 2.0 * jnp.floor(0.5 * whole))
    square = part * part
    sine = jnp.zeros_like(square)
    for k in (11, 9, 7, 5, 3, 1):
        sine = sine * square + (-1.0) ** (k // 2) * math.pi**k / math.factorial(k)
    cosine = jnp.zeros_like(square)
    for k in (12, 10, 8, 6, 4, 2, 0):
        cosine = cosine * square + (-1.0) ** (k // 2) * math.pi**k / math.factorial(k)
    return order, sign * part * sine, sign * cosine


def thrice(x):
    high, low = pieces(x, 2)
    return jnp.concatenate([high, low, high], axis=0).astype(bf16)


def onehot(ids, count):
    return jnp.where(lax.broadcasted_iota(jnp.int32, (count, ids.shape[1]), 0) == ids, 1.0, 0.0)


def slot_grads(rows, cot_refs, src_pos, feats, weights, orders):
    wide, back, first, last = weights
    slots = rows.shape[1]
    sources = src_pos.shape[1]
    channels = feats.shape[0]
    hidden = last.shape[1] // 3
    parts = len(degree)
    atoms = (cot_refs[0].shape[0] - sublanes) // parts
    targets = atoms * len(cot_refs)

    src_hot = onehot(rows[0:1], sources).astype(bf16)
    tgt_hot = onehot(rows[1:2], targets).astype(bf16)
    mask = rows[2:3].astype(f32)
    offset = rows[4:6].astype(f32) * domain_side

    tgt_pos = [jnp.concatenate(pieces(ref[parts * atoms :, 0:atoms], 3), axis=0) for ref in cot_refs]
    from_src = dot(src_pos, src_hot)
    from_tgt = dot(jnp.concatenate(tgt_pos, axis=1).astype(bf16), tgt_hot)
    from_src = from_src[0:8] + from_src[8:16] + from_src[16:24]
    from_tgt = from_tgt[0:8] + from_tgt[8:16] + from_tgt[16:24]
    rel = [
        from_src[0:1] + offset[0:1] - from_tgt[0:1],
        from_src[1:2] + offset[1:2] - from_tgt[1:2],
        from_src[2:3] - from_tgt[2:3],
    ]
    dist = jnp.sqrt(rel[0] * rel[0] + rel[1] * rel[1] + rel[2] * rel[2] + soften)
    near = 1.0 / dist
    x, y, z = (r * near for r in rel)
    scaled = dist * (1.0 / cutoff)
    room = jnp.where(scaled < 1.0, 1.0 - scaled * scaled, 0.0)
    env = room * room * mask
    d_env = (-4.0 / cutoff) * scaled * room * mask

    order, sine, cosine = radial_waves(dist, orders)
    norm = math.sqrt(2.0 / cutoff)
    basis = norm * near * sine
    d_basis = norm * near * ((math.pi / cutoff) * order * cosine - sine * near)
    species = onehot(rows[3:4], 2 * sublanes)
    before = dot(first, thrice(jnp.concatenate([basis, species], axis=0)))
    gate = 1.0 / (1.0 + jnp.exp(-before))
    act = before * gate
    d_act = gate * (1.0 + before * (1.0 - gate))
    radial = dot(wide, thrice(act))
    gathered = dot(feats, jnp.concatenate([src_hot, src_hot], axis=0))

    root3, root5, root15 = math.sqrt(3.0), math.sqrt(5.0), math.sqrt(15.0)
    shapes = [
        None, root3 * x, root3 * y, root3 * z, root15 * x * y, root15 * y * z,
        0.5 * root5 * (2.0 * z * z - x * x - y * y), root15 * x * z, 0.5 * root15 * (x * x - y * y),
    ]
    twice = lax.broadcasted_iota(jnp.int32, (2 * targets, slots), 0)
    twice = (twice // (2 * atoms)) * atoms + lax.rem(twice, atoms)
    twice = jnp.where(twice == rows[1:2], 1.0, 0.0).astype(bf16)
    d_shapes = [None] * parts
    d_radial = []
    through = None
    for low, high in ((0, 1), (1, 4), (4, 9)):
        l = len(d_radial)
        own = radial[l * channels : (l + 1) * channels]
        with_feats = own * gathered
        total = None
        for m in range(low, high):
            blocks = []
            for ref in cot_refs:
                blocks += pieces(ref[m * atoms : (m + 1) * atoms], 2)
            cot = dot_cols(jnp.concatenate(blocks, axis=0).astype(bf16), twice)
            if m:
                d_shapes[m] = jnp.sum(with_feats * cot, axis=0, keepdims=True) * env
                cot = cot * shapes[m]
            total = cot if total is None else total + cot
        d_radial.append(total * gathered)
        own = own * total
        through = own if through is None else through + own
    to_env = jnp.sum(through * gathered, axis=0, keepdims=True)
    through = through * env
    d_hidden = dot(back, jnp.concatenate(
        [p.astype(bf16) for p in pieces(jnp.concatenate(d_radial, axis=0), 2)], axis=0
    ))
    d_before = (d_hidden[0:hidden] + d_hidden[hidden:]) * (d_act * env)
    to_basis = dot(last, thrice(d_before))
    d_dist = jnp.sum(to_basis * d_basis, axis=0, keepdims=True) + to_env * d_env

    s = d_shapes
    d_x = root3 * s[1] + root15 * (y * s[4] + z * s[7] + x * s[8]) - root5 * x * s[6]
    d_y = root3 * s[2] + root15 * (x * s[4] + z * s[5] - y * s[8]) - root5 * y * s[6]
    d_z = root3 * s[3] + root15 * (y * s[5] + x * s[7]) + 2.0 * root5 * z * s[6]
    d_dist = d_dist - near * (x * d_x + y * d_y + z * d_z)
    grad = jnp.concatenate(
        [near * d_x + x * d_dist, near * d_y + y * d_dist, near * d_z + z * d_dist,
         jnp.zeros((sublanes - 3, slots), f32)], axis=0,
    )
    grad = jnp.concatenate(pieces(grad, 2), axis=0).astype(bf16)
    pos_src = dot_rows(grad, src_hot)
    pos_tgt = dot_rows(grad, tgt_hot)
    feat_src = sum(dot_rows(src_hot, p.astype(bf16)) for p in pieces(through, 2))
    return pos_src[0:8] + pos_src[8:16], -(pos_tgt[0:8] + pos_tgt[8:16]), feat_src


def partner_chunks(first, slots, lanes):
    base = first // lanes * lanes
    return base, -(-(first + slots - base) // lanes)


def all_rows(rows_ref, y_ref, start, chunks):
    own = rows_ref[...]
    parts = [y_ref[start + at * sublanes : start + (at + 1) * sublanes] for at in range(chunks)]
    theirs = jnp.concatenate(parts, axis=1).astype(jnp.int32)
    base = own.shape[1] - theirs.shape[1]
    if base:
        theirs = jnp.concatenate([jnp.zeros((sublanes, base), jnp.int32), theirs], axis=1)
    return own + theirs


def early_kernel(orders, tables, start, chunks, rows_ref, *refs):
    refs = list(refs)
    weights = [refs.pop(0)[...] for _ in range(4)]
    y_ref = refs.pop(0)
    block_refs = [refs.pop(0) for _ in range(1 + max(ref for ref, _ in tables))]
    cot_ref, src_pos_ref, feats_ref, pos_ref, feat_ref, place = refs
    atoms = (cot_ref.shape[0] - sublanes) // len(degree)
    block = atoms + sublanes
    views = [block_refs[ref].at[at * block : (at + 1) * block] for ref, at in tables]
    for table, ref in enumerate(views):
        place[:, table * atoms : (table + 1) * atoms] = ref[atoms:, 0:atoms]
    src_pos_ref[...] = jnp.concatenate(pieces(place[...], 3), axis=0).astype(bf16)
    feats = jnp.concatenate([ref[0:atoms] for ref in views], axis=0).T
    feats_ref[...] = jnp.concatenate(pieces(feats, 2), axis=1).astype(bf16)
    rows = all_rows(rows_ref, y_ref, start, chunks)
    pos, pos_tgt, feat = slot_grads(
        rows, [cot_ref], src_pos_ref[...], feats_ref[...], weights, orders
    )
    feat_ref[...] = feat
    pos_ref[...] = pos
    pos_ref[:, 0:atoms] = pos[:, 0:atoms] + pos_tgt


def late_kernel(orders, homes, start, chunks, rows_ref, *refs):
    refs = list(refs)
    weights = [refs.pop(0)[...] for _ in range(4)]
    y_ref, src_pos_ref, feats_ref, held_pos, held_feat = (refs.pop(0) for _ in range(5))
    cot_refs = [refs.pop(0) for _ in range(2)]
    *outs, near_ref, far_ref = refs
    atoms = (cot_refs[0].shape[0] - sublanes) // len(degree)
    block = atoms + sublanes
    rows = all_rows(rows_ref, y_ref, start, chunks)
    pos, pos_tgt, feat = slot_grads(
        rows, cot_refs, src_pos_ref[...], feats_ref[...], weights, orders
    )
    pos = pos + held_pos[...]
    feat = feat + held_feat[...]
    for ref, home in zip(outs, homes):
        for at, table in enumerate(home):
            part = slice(table * atoms, (table + 1) * atoms)
            ref[at * block : at * block + atoms] = feat[part]
            ref[at * block + atoms : (at + 1) * block] = jnp.zeros((sublanes, ref.shape[1]), f32)
            ref[at * block + atoms : (at + 1) * block, 0:atoms] = pos[:, part]
    for at, ref in enumerate((near_ref, far_ref)):
        ref[...] = jnp.zeros(ref.shape, f32)
        ref[0:sublanes, 0:atoms] = pos_tgt[:, at * atoms : (at + 1) * atoms]


def add_kernel(count, *refs):
    total = refs[0][...]
    for ref in refs[1:count]:
        total = total + ref[...]
    rows = total.shape[0] // len(refs[count:])
    for at, ref in enumerate(refs[count:]):
        ref[...] = total[at * rows : (at + 1) * rows]


def sum_kernel(gx_count, *refs):
    gx_refs, gy_refs = refs[:gx_count], refs[gx_count:-2]
    pos_ref, feat_ref = refs[-2:]
    atoms = pos_ref.shape[3]
    feat = gx_refs[0][...]
    for ref in gx_refs[1:]:
        feat = feat + ref[...]
    pos = feat[atoms : atoms + 3, 0:atoms]
    for ref in gy_refs:
        pos = pos + ref[0:3, 0:atoms]
    for axis in range(3):
        pos_ref[0, axis] = pos[axis : axis + 1]
    feat_ref[0, 0] = feat[0:atoms]


vmem = pl.BlockSpec(memory_space=pltpu.VMEM)


def call(kernel, name, out_shape, operands, scratch=(), room=4, us=None):
    return pl.pallas_call(
        kernel,
        out_shape=out_shape,
        in_specs=[vmem] * len(operands),
        out_specs=(vmem,) * len(out_shape),
        scratch_shapes=list(scratch),
        compiler_params=pltpu.CompilerParams(vmem_limit_bytes=room and room * megabyte),
        name=name,
        cost_estimate=us and pl.CostEstimate(
            flops=int(us * 1e9), bytes_accessed=0, transcendentals=0
        ),
    )(*operands)


def local(
    gx_size, gy_size, positions, features, cotangent, nbr_src, nbr_tgt, pair_mask, pair_species,
    w_in, species_emb, w_out,
):
    atoms, channels = features.shape[2:]
    steps, _, pairs = nbr_src.shape[2:]
    orders, hidden = w_in.shape
    slots = steps * pairs
    gx_links, gy_links = links_of(gx_size), links_of(gy_size)
    gx_spots = gx_spots_of(gx_links)
    sources = (len(gx_links) + 1) * atoms
    block = atoms + sublanes
    sds = jax.ShapeDtypeStruct

    by_axis = jnp.transpose(positions, (0, 2, 1, 3))
    lists = [jnp.transpose(x, (0, 2, 3, 1, 4)) for x in (nbr_src, nbr_tgt, pair_mask, pair_species)]
    gx_pack = sds((block, channels), f32)
    chunks = [partner_chunks(own * slots, slots, channels)[1] for own in (1, 2)]
    y_pack = sds((block + sum(chunks) * sublanes, channels), f32)
    gy_pack = sds((len(degree) * atoms + sublanes, channels), f32)
    own, y_own, cot_own = call(
        functools.partial(pack_kernel, gx_spots, gy_links), "pack", (gx_pack, y_pack, gy_pack),
        (by_axis, features, cotangent, *lists), room=None,
    )
    far_links = (gy_links[3], gy_links[2])
    y = gy_links[0].swap(y_own, "gy")
    many = len(gx_links) + 1
    tables = [(at, 0) if not l else (1 + l, at) for at in range(2) for l in range(many)]
    if gx_size == 4:
        homes = ((0, many, 3, many + 3), (1, many + 1, 2, many + 2))
    else:
        homes = tuple((table, many + table) for table in range(many))
    early_rows, late_rows, *weights = call(
        functools.partial(prep_kernel, gx_spots, gy_links),
        "prepare",
        (
            *(sds((sublanes, -(-n * slots // channels) * channels), jnp.int32) for n in (2, 3)),
            sds((w_out.shape[1], 3 * hidden), bf16),
            sds((2 * hidden, 2 * w_out.shape[1]), bf16),
            sds((hidden, 3 * (orders + 2 * sublanes)), bf16),
            sds((orders, 3 * hidden), bf16),
        ),
        (*lists, w_in, species_emb, w_out), us=3,
    )
    late_cot = lax.optimization_barrier((cot_own, weights[-1]))[0]
    cot_far, cot_near = (link.swap(late_cot, "gy") for link in far_links)
    (two,) = call(
        functools.partial(stack_kernel, block), "stack", (sds((2 * block, channels), f32),),
        (own, y, weights[-1]), us=2,
    )
    blocks = [own, y] + [link.swap(two, "gx") for link in gx_links]
    table = (
        sds((3 * sublanes, 2 * sources), bf16), sds((channels, 4 * sources), bf16),
        sds((sublanes, 2 * sources), f32), sds((2 * sources, channels), f32),
    )
    held = call(
        functools.partial(early_kernel, orders, tables, block, chunks[0]), "early_tiles", table,
        (early_rows, *weights, y, *blocks, cot_own),
        [pltpu.VMEM((sublanes, 2 * sources), f32)], 24,
    )
    far_pack = sds((channels // 2, channels), f32)
    *sent, near, far = call(
        functools.partial(late_kernel, orders, homes, block + chunks[0] * sublanes, chunks[1]),
        "late_tiles",
        tuple(sds((len(home) * block, channels), f32) for home in homes) + (far_pack,) * 2,
        (late_rows, *weights, y, *held, cot_near, cot_far), room=24,
    )
    back_gy = [link.swap(value, "gy") for link, value in zip(far_links, (far, near))]
    if gx_size == 4:
        came = gx_links[0].swap(sent[1], "gx")
        near_chip, far_chip = call(
            functools.partial(add_kernel, 2), "add", (sds((2 * block, channels), f32),) * 2,
            (sent[0], came),
        )
        sent, came = [near_chip], [gx_links[2].swap(far_chip, "gx")]
    else:
        came = [link.swap(value, "gx") for link, value in zip(gx_links, sent[1:])]
    own, y = call(
        functools.partial(add_kernel, 1 + len(came)), "add", (gx_pack,) * 2, (sent[0], *came)
    )
    back = [own, gy_links[0].swap(y, "gy")]
    pos, feat = call(
        functools.partial(sum_kernel, len(back)), "sums",
        (sds(by_axis.shape, f32), sds(features.shape, f32)),
        (*back, *back_gy),
    )
    return jnp.transpose(pos, (0, 2, 1, 3)), feat


def solution(mesh):
    split = [P("gx", "gy")] * 7 + [P()] * 3
    return jax.shard_map(
        functools.partial(local, mesh.shape["gx"], mesh.shape["gy"]),
        mesh=mesh,
        in_specs=tuple(split),
        out_specs=(P("gx", "gy"), P("gx", "gy")),
        check_vma=False,
    )
```

```python
import functools
import math

import jax
import jax.numpy as jnp
from jax import lax
from jax.experimental import pallas as pl
from jax.experimental.pallas import tpu as pltpu
from jax.sharding import PartitionSpec as P

domain_side = 5.0
cutoff = 12.0
soften = 0.25
reach = 2
sublanes = 8
degree = (0, 1, 1, 1, 2, 2, 2, 2, 2)
megabyte = 1024 * 1024
f32 = jnp.float32
bf16 = jnp.bfloat16


class Link:
    def __init__(self, step, bit, peers):
        self.step, self.bit, self.peers = step, bit, peers

    def delta(self, i):
        return self.step * (1 - 2 * ((i >> self.bit) & 1))

    def swap(self, value, axis):
        n = self.peers
        return lax.ppermute(value, axis, [(i, (i + self.delta(i)) % n) for i in range(n)])


def links_of(peers):
    assert peers % 4 == 0, peers
    steps = [(1, 0), (-1, 0), (2, 1)] + ([(-2, 1)] if peers > 4 else [])
    return [Link(step, bit, peers) for step, bit in steps]


def gx_spots_of(links):
    spots = [(0, None, 0)]
    for table, link in enumerate(links):
        spots.append((table + 1, link, 1))
        if link.peers == 4 and abs(link.step) == 2:
            spots.append((table + 1, link, -1))
    return spots


def pieces(x, count):
    out = []
    for _ in range(count):
        out.append(x.astype(bf16).astype(f32))
        x = x - out[-1]
    return out


def dot(a, b):
    return jnp.dot(a, b, preferred_element_type=f32)


def dot_rows(a, b):
    return lax.dot_general(a, b, (((1,), (1,)), ((), ())), preferred_element_type=f32)


def dot_cols(a, b):
    return lax.dot_general(a, b, (((0,), (0,)), ((), ())), preferred_element_type=f32)


def write_rows(store, gx_spots, at_x, lists, step_y, place, start, first_source=0):
    atoms = pairs = lists[0].shape[4]
    for slot, (table, link, sign) in enumerate(gx_spots):
        step_x = 0 if link is None else sign * link.delta(at_x)
        src, tgt, mask, spec = (ref[0, reach + step_x, reach + step_y] for ref in lists)
        store(0, start + slot * pairs, src + (first_source + table * atoms))
        store(1, start + slot * pairs, tgt + place * atoms)
        store(2, start + slot * pairs, mask)
        store(3, start + slot * pairs, spec)
        store(4, start + slot * pairs, jnp.full((1, pairs), step_x, jnp.int32))
        store(5, start + slot * pairs, jnp.full((1, pairs), -step_y, jnp.int32))


def pack_kernel(
    gx_spots, gy_links, pos_ref, feat_ref, cot_ref, src_ref, tgt_ref, mask_ref, spec_ref,
    gx_ref, y_ref, gy_ref,
):
    atoms, channels = feat_ref.shape[2:]
    pairs = src_ref.shape[4]
    parts = len(degree)
    zero = jnp.zeros((sublanes, channels), f32)
    for ref in (gx_ref, y_ref):
        ref[0:atoms] = feat_ref[0, 0]
        ref[atoms : atoms + sublanes] = zero
    for m in range(parts):
        gy_ref[m * atoms : (m + 1) * atoms] = cot_ref[0, 0, :, m * channels : (m + 1) * channels]
    gy_ref[parts * atoms :] = zero
    for axis in range(3):
        row = pos_ref[0, axis]
        gx_ref[atoms + axis : atoms + axis + 1, 0:atoms] = row
        y_ref[atoms + axis : atoms + axis + 1, 0:atoms] = row
        gy_ref[parts * atoms + axis : parts * atoms + axis + 1, 0:atoms] = row

    block = atoms + sublanes
    for start in range(block, y_ref.shape[0], sublanes):
        y_ref[start : start + sublanes] = zero

    def store(row, lane, value):
        chunk, lane = divmod(lane, channels)
        at = block + chunk * sublanes + row
        y_ref[at : at + 1, lane : lane + pairs] = value.astype(f32)

    at_x, at_y = lax.axis_index("gx"), lax.axis_index("gy")
    lists = (src_ref, tgt_ref, mask_ref, spec_ref)
    near, other = gy_links[0].delta(at_y), gy_links[1].delta(at_y)
    partner = at_y + near
    to_far = (partner + (partner >> 1)) & 1
    sources = (1 + max(table for table, _, _ in gx_spots)) * atoms
    slots = len(gx_spots) * pairs
    lane = 0
    for own, step_y, place in ((1, near, 0), (2, other, to_far)):
        base, chunks = partner_chunks(own * slots, slots, channels)
        start = lane + own * slots - base
        write_rows(store, gx_spots, at_x, lists, step_y, place, start, sources)
        lane += chunks * channels


def stack_kernel(rows, *refs):
    *refs, _, out_ref = refs
    for at, ref in enumerate(refs):
        out_ref[at * rows : (at + 1) * rows] = ref[0:rows]


def prep_kernel(
    gx_spots, gy_links, src_ref, tgt_ref, mask_ref, spec_ref, in_ref, emb_ref, out_ref,
    early_ref, late_ref, wide_ref, back_ref, first_ref, last_ref,
):
    pairs = src_ref.shape[4]
    at_x, at_y = lax.axis_index("gx"), lax.axis_index("gy")
    lists = (src_ref, tgt_ref, mask_ref, spec_ref)
    for rows_ref, links in ((early_ref, (None,)), (late_ref, (gy_links[2], gy_links[3]))):
        rows_ref[...] = jnp.zeros(rows_ref.shape, jnp.int32)

        def store(row, lane, value, rows_ref=rows_ref):
            rows_ref[row : row + 1, lane : lane + pairs] = value

        for place, link in enumerate(links):
            step_y = 0 if link is None else link.delta(at_y)
            write_rows(store, gx_spots, at_x, lists, step_y, place, place * len(gx_spots) * pairs)
    high, low = pieces(out_ref[...], 2)
    wide_ref[...] = jnp.concatenate([high, high, low], axis=0).T.astype(bf16)
    upper = jnp.concatenate([high, high], axis=1)
    lower = jnp.concatenate([low, jnp.zeros_like(low)], axis=1)
    back_ref[...] = jnp.concatenate([upper, lower], axis=0).astype(bf16)
    orders, hidden = in_ref.shape
    spare = jnp.zeros((sublanes * 2 - emb_ref.shape[0], hidden), f32)
    high, low = pieces(jnp.concatenate([in_ref[...], emb_ref[...], spare], axis=0), 2)
    first_ref[...] = jnp.concatenate([high, high, low], axis=0).T.astype(bf16)
    last_ref[...] = jnp.concatenate([high[0:orders], high[0:orders], low[0:orders]], axis=1).astype(bf16)


def radial_waves(dist, orders):
    order = (lax.broadcasted_iota(jnp.int32, (orders, 1), 0) + 1).astype(f32)
    turn = order * (dist * (1.0 / cutoff))
    whole = jnp.floor(turn + 0.5)
    part = turn - whole
    sign = 1.0 - 2.0 * (whole - 2.0 * jnp.floor(0.5 * whole))
    square = part * part
    sine = jnp.zeros_like(square)
    for k in (11, 9, 7, 5, 3, 1):
        sine = sine * square + (-1.0) ** (k // 2) * math.pi**k / math.factorial(k)
    cosine = jnp.zeros_like(square)
    for k in (12, 10, 8, 6, 4, 2, 0):
        cosine = cosine * square + (-1.0) ** (k // 2) * math.pi**k / math.factorial(k)
    return order, sign * part * sine, sign * cosine


def thrice(x):
    high, low = pieces(x, 2)
    return jnp.concatenate([high, low, high], axis=0).astype(bf16)


def lane_ids(rows, count):
    return lax.broadcasted_iota(jnp.int32, (rows, count), 1)


def onehot(ids, count):
    return jnp.where(lax.broadcasted_iota(jnp.int32, (count, ids.shape[1]), 0) == ids, 1.0, 0.0)


def slot_grads(rows, cot_refs, src_pos, feats, weights, orders):
    wide, back, first, last = weights
    slots = rows.shape[1]
    sources = src_pos.shape[1]
    channels = feats.shape[0] // 2
    hidden = last.shape[1] // 3
    parts = len(degree)
    atoms = (cot_refs[0].shape[0] - sublanes) // parts
    targets = atoms * len(cot_refs)

    src_hot = onehot(rows[0:1], sources).astype(bf16)
    tgt_hot = onehot(rows[1:2], targets).astype(bf16)
    mask = rows[2:3].astype(f32)
    offset = rows[4:6].astype(f32) * domain_side

    tgt_pos = [jnp.concatenate(pieces(ref[parts * atoms :, 0:atoms], 3), axis=0) for ref in cot_refs]
    gathered = dot(jnp.concatenate([feats, src_pos], axis=0), src_hot)
    from_src = gathered[2 * channels :]
    gathered = gathered[0:channels] + gathered[channels : 2 * channels]
    from_tgt = dot(jnp.concatenate(tgt_pos, axis=1).astype(bf16), tgt_hot)
    from_src = from_src[0:8] + from_src[8:16] + from_src[16:24]
    from_tgt = from_tgt[0:8] + from_tgt[8:16] + from_tgt[16:24]
    rel = [
        from_src[0:1] + offset[0:1] - from_tgt[0:1],
        from_src[1:2] + offset[1:2] - from_tgt[1:2],
        from_src[2:3] - from_tgt[2:3],
    ]
    dist = jnp.sqrt(rel[0] * rel[0] + rel[1] * rel[1] + rel[2] * rel[2] + soften)
    near = 1.0 / dist
    x, y, z = (r * near for r in rel)
    scaled = dist * (1.0 / cutoff)
    room = jnp.where(scaled < 1.0, 1.0 - scaled * scaled, 0.0)
    env = room * room * mask
    d_env = (-4.0 / cutoff) * scaled * room * mask

    order, sine, cosine = radial_waves(dist, orders)
    norm = math.sqrt(2.0 / cutoff)
    basis = norm * near * sine
    d_basis = norm * near * ((math.pi / cutoff) * order * cosine - sine * near)
    species = onehot(rows[3:4], 2 * sublanes)
    before = dot(first, thrice(jnp.concatenate([basis, species], axis=0)))
    gate = 1.0 / (1.0 + jnp.exp(-before))
    act = before * gate
    d_act = gate * (1.0 + before * (1.0 - gate))
    radial = dot(wide, thrice(act))
    root3, root5, root15 = math.sqrt(3.0), math.sqrt(5.0), math.sqrt(15.0)
    shapes = [
        None, root3 * x, root3 * y, root3 * z, root15 * x * y, root15 * y * z,
        0.5 * root5 * (2.0 * z * z - x * x - y * y), root15 * x * z, 0.5 * root15 * (x * x - y * y),
    ]
    twice = lax.broadcasted_iota(jnp.int32, (2 * targets, slots), 0)
    twice = (twice // (2 * atoms)) * atoms + lax.rem(twice, atoms)
    twice = jnp.where(twice == rows[1:2], 1.0, 0.0).astype(bf16)
    blocks = []
    for ref in cot_refs:
        block = [ref[m * atoms : (m + 1) * atoms] for m in range(parts)]
        blocks += pieces(jnp.concatenate(block, axis=1), 2)
    cots = dot_cols(jnp.concatenate(blocks, axis=0).astype(bf16), twice)
    d_shapes = [None] * parts
    d_radial = []
    through = None
    for low, high in ((0, 1), (1, 4), (4, 9)):
        l = len(d_radial)
        own = radial[l * channels : (l + 1) * channels]
        with_feats = own * gathered
        total = None
        for m in range(low, high):
            cot = cots[m * channels : (m + 1) * channels]
            if m:
                d_shapes[m] = jnp.sum(with_feats * cot, axis=0, keepdims=True) * env
                cot = cot * shapes[m]
            total = cot if total is None else total + cot
        d_radial.append(total * gathered)
        own = own * total
        through = own if through is None else through + own
    to_env = jnp.sum(through * gathered, axis=0, keepdims=True)
    through = through * env
    d_hidden = dot(back, jnp.concatenate(
        [p.astype(bf16) for p in pieces(jnp.concatenate(d_radial, axis=0), 2)], axis=0
    ))
    d_before = (d_hidden[0:hidden] + d_hidden[hidden:]) * (d_act * env)
    to_basis = dot(last, thrice(d_before))
    d_dist = jnp.sum(to_basis * d_basis, axis=0, keepdims=True) + to_env * d_env

    s = d_shapes
    d_x = root3 * s[1] + root15 * (y * s[4] + z * s[7] + x * s[8]) - root5 * x * s[6]
    d_y = root3 * s[2] + root15 * (x * s[4] + z * s[5] - y * s[8]) - root5 * y * s[6]
    d_z = root3 * s[3] + root15 * (y * s[5] + x * s[7]) + 2.0 * root5 * z * s[6]
    d_dist = d_dist - near * (x * d_x + y * d_y + z * d_z)
    grad = jnp.concatenate(
        [near * d_x + x * d_dist, near * d_y + y * d_dist, near * d_z + z * d_dist,
         jnp.zeros((sublanes - 3, slots), f32)], axis=0,
    )
    grad = jnp.concatenate(pieces(grad, 2), axis=0).astype(bf16)
    ids = rows.T
    src_home = jnp.where(lane_ids(slots, sources) == ids[:, 0:1], 1.0, 0.0).astype(bf16)
    tgt_home = jnp.where(lane_ids(slots, targets) == ids[:, 1:2], 1.0, 0.0).astype(bf16)
    pos_tgt = dot(grad, tgt_home)
    through = [p.astype(bf16) for p in pieces(through, 2)]
    home = dot(jnp.concatenate([*through, grad], axis=0), src_home)
    feat_src = (home[0:channels] + home[channels : 2 * channels]).T
    pos_src = home[2 * channels :]
    return pos_src[0:8] + pos_src[8:16], -(pos_tgt[0:8] + pos_tgt[8:16]), feat_src


def partner_chunks(first, slots, lanes):
    base = first // lanes * lanes
    return base, -(-(first + slots - base) // lanes)


def all_rows(rows_ref, y_ref, start, chunks):
    own = rows_ref[...]
    parts = [y_ref[start + at * sublanes : start + (at + 1) * sublanes] for at in range(chunks)]
    theirs = jnp.concatenate(parts, axis=1).astype(jnp.int32)
    base = own.shape[1] - theirs.shape[1]
    if base:
        theirs = jnp.concatenate([jnp.zeros((sublanes, base), jnp.int32), theirs], axis=1)
    return own + theirs


def early_kernel(orders, tables, start, chunks, rows_ref, *refs):
    refs = list(refs)
    weights = [refs.pop(0)[...] for _ in range(4)]
    y_ref = refs.pop(0)
    block_refs = [refs.pop(0) for _ in range(1 + max(ref for ref, _ in tables))]
    cot_ref, src_pos_ref, feats_ref, pos_ref, feat_ref, place = refs
    atoms = (cot_ref.shape[0] - sublanes) // len(degree)
    block = atoms + sublanes
    views = [block_refs[ref].at[at * block : (at + 1) * block] for ref, at in tables]
    for table, ref in enumerate(views):
        place[:, table * atoms : (table + 1) * atoms] = ref[atoms:, 0:atoms]
    src_pos_ref[...] = jnp.concatenate(pieces(place[...], 3), axis=0).astype(bf16)
    feats = jnp.concatenate([ref[0:atoms] for ref in views], axis=0).T
    feats_ref[...] = jnp.concatenate(pieces(feats, 2), axis=0).astype(bf16)
    rows = all_rows(rows_ref, y_ref, start, chunks)
    pos, pos_tgt, feat = slot_grads(
        rows, [cot_ref], src_pos_ref[...], feats_ref[...], weights, orders
    )
    feat_ref[...] = feat
    pos_ref[...] = pos
    pos_ref[:, 0:atoms] = pos[:, 0:atoms] + pos_tgt


def late_kernel(orders, homes, start, chunks, rows_ref, *refs):
    refs = list(refs)
    weights = [refs.pop(0)[...] for _ in range(4)]
    y_ref, src_pos_ref, feats_ref, held_pos, held_feat = (refs.pop(0) for _ in range(5))
    cot_refs = [refs.pop(0) for _ in range(2)]
    *outs, near_ref, far_ref = refs
    atoms = (cot_refs[0].shape[0] - sublanes) // len(degree)
    block = atoms + sublanes
    rows = all_rows(rows_ref, y_ref, start, chunks)
    pos, pos_tgt, feat = slot_grads(
        rows, cot_refs, src_pos_ref[...], feats_ref[...], weights, orders
    )
    pos = pos + held_pos[...]
    feat = feat + held_feat[...]
    for ref, home in zip(outs, homes):
        for at, table in enumerate(home):
            part = slice(table * atoms, (table + 1) * atoms)
            ref[at * block : at * block + atoms] = feat[part]
            ref[at * block + atoms : (at + 1) * block] = jnp.zeros((sublanes, ref.shape[1]), f32)
            ref[at * block + atoms : (at + 1) * block, 0:atoms] = pos[:, part]
    for at, ref in enumerate((near_ref, far_ref)):
        ref[...] = jnp.zeros(ref.shape, f32)
        ref[0:sublanes, 0:atoms] = pos_tgt[:, at * atoms : (at + 1) * atoms]


def add_kernel(count, *refs):
    total = refs[0][...]
    for ref in refs[1:count]:
        total = total + ref[...]
    rows = total.shape[0] // len(refs[count:])
    for at, ref in enumerate(refs[count:]):
        ref[...] = total[at * rows : (at + 1) * rows]


def sum_kernel(gx_count, *refs):
    gx_refs, gy_refs = refs[:gx_count], refs[gx_count:-2]
    pos_ref, feat_ref = refs[-2:]
    atoms = pos_ref.shape[3]
    feat = gx_refs[0][...]
    for ref in gx_refs[1:]:
        feat = feat + ref[...]
    pos = feat[atoms : atoms + 3, 0:atoms]
    for ref in gy_refs:
        pos = pos + ref[0:3, 0:atoms]
    for axis in range(3):
        pos_ref[0, axis] = pos[axis : axis + 1]
    feat_ref[0, 0] = feat[0:atoms]


vmem = pl.BlockSpec(memory_space=pltpu.VMEM)


def call(kernel, name, out_shape, operands, scratch=(), room=4, us=None):
    return pl.pallas_call(
        kernel,
        out_shape=out_shape,
        in_specs=[vmem] * len(operands),
        out_specs=(vmem,) * len(out_shape),
        scratch_shapes=list(scratch),
        compiler_params=pltpu.CompilerParams(vmem_limit_bytes=room and room * megabyte),
        name=name,
        cost_estimate=us and pl.CostEstimate(
            flops=int(us * 1e9), bytes_accessed=0, transcendentals=0
        ),
    )(*operands)


def local(
    gx_size, gy_size, positions, features, cotangent, nbr_src, nbr_tgt, pair_mask, pair_species,
    w_in, species_emb, w_out,
):
    atoms, channels = features.shape[2:]
    steps, _, pairs = nbr_src.shape[2:]
    orders, hidden = w_in.shape
    slots = steps * pairs
    gx_links, gy_links = links_of(gx_size), links_of(gy_size)
    gx_spots = gx_spots_of(gx_links)
    sources = (len(gx_links) + 1) * atoms
    block = atoms + sublanes
    sds = jax.ShapeDtypeStruct

    by_axis = jnp.transpose(positions, (0, 2, 1, 3))
    lists = [jnp.transpose(x, (0, 2, 3, 1, 4)) for x in (nbr_src, nbr_tgt, pair_mask, pair_species)]
    gx_pack = sds((block, channels), f32)
    chunks = [partner_chunks(own * slots, slots, channels)[1] for own in (1, 2)]
    y_pack = sds((block + sum(chunks) * sublanes, channels), f32)
    gy_pack = sds((len(degree) * atoms + sublanes, channels), f32)
    own, y_own, cot_own = call(
        functools.partial(pack_kernel, gx_spots, gy_links), "pack", (gx_pack, y_pack, gy_pack),
        (by_axis, features, cotangent, *lists), room=None,
    )
    far_links = (gy_links[3], gy_links[2])
    y = gy_links[0].swap(y_own, "gy")
    many = len(gx_links) + 1
    tables = [(at, 0) if not l else (1 + l, at) for at in range(2) for l in range(many)]
    if gx_size == 4:
        homes = ((0, many, 3, many + 3), (1, many + 1, 2, many + 2))
    else:
        homes = tuple((table, many + table) for table in range(many))
    early_rows, late_rows, *weights = call(
        functools.partial(prep_kernel, gx_spots, gy_links),
        "prepare",
        (
            *(sds((sublanes, -(-n * slots // channels) * channels), jnp.int32) for n in (2, 3)),
            sds((w_out.shape[1], 3 * hidden), bf16),
            sds((2 * hidden, 2 * w_out.shape[1]), bf16),
            sds((hidden, 3 * (orders + 2 * sublanes)), bf16),
            sds((orders, 3 * hidden), bf16),
        ),
        (*lists, w_in, species_emb, w_out), us=3,
    )
    late_cot = lax.optimization_barrier((cot_own, weights[-1]))[0]
    cot_far, cot_near = (link.swap(late_cot, "gy") for link in far_links)
    (two,) = call(
        functools.partial(stack_kernel, block), "stack", (sds((2 * block, channels), f32),),
        (own, y, weights[-1]), us=2,
    )
    blocks = [own, y] + [link.swap(two, "gx") for link in gx_links]
    table = (
        sds((3 * sublanes, 2 * sources), bf16), sds((2 * channels, 2 * sources), bf16),
        sds((sublanes, 2 * sources), f32), sds((2 * sources, channels), f32),
    )
    held = call(
        functools.partial(early_kernel, orders, tables, block, chunks[0]), "early_tiles", table,
        (early_rows, *weights, y, *blocks, cot_own),
        [pltpu.VMEM((sublanes, 2 * sources), f32)], 24,
    )
    far_pack = sds((channels // 2, channels), f32)
    *sent, near, far = call(
        functools.partial(late_kernel, orders, homes, block + chunks[0] * sublanes, chunks[1]),
        "late_tiles",
        tuple(sds((len(home) * block, channels), f32) for home in homes) + (far_pack,) * 2,
        (late_rows, *weights, y, *held, cot_near, cot_far), room=24,
    )
    back_gy = [link.swap(value, "gy") for link, value in zip(far_links, (far, near))]
    if gx_size == 4:
        came = gx_links[0].swap(sent[1], "gx")
        near_chip, far_chip = call(
            functools.partial(add_kernel, 2), "add", (sds((2 * block, channels), f32),) * 2,
            (sent[0], came),
        )
        sent, came = [near_chip], [gx_links[2].swap(far_chip, "gx")]
    else:
        came = [link.swap(value, "gx") for link, value in zip(gx_links, sent[1:])]
    own, y = call(
        functools.partial(add_kernel, 1 + len(came)), "add", (gx_pack,) * 2, (sent[0], *came)
    )
    back = [own, gy_links[0].swap(y, "gy")]
    pos, feat = call(
        functools.partial(sum_kernel, len(back)), "sums",
        (sds(by_axis.shape, f32), sds(features.shape, f32)),
        (*back, *back_gy),
    )
    return jnp.transpose(pos, (0, 2, 1, 3)), feat


def solution(mesh):
    split = [P("gx", "gy")] * 7 + [P()] * 3
    return jax.shard_map(
        functools.partial(local, mesh.shape["gx"], mesh.shape["gy"]),
        mesh=mesh,
        in_specs=tuple(split),
        out_specs=(P("gx", "gy"), P("gx", "gy")),
        check_vma=False,
    )
```

```python
import functools
import math

import jax
import jax.numpy as jnp
from jax import lax
from jax.experimental import pallas as pl
from jax.experimental.pallas import tpu as pltpu
from jax.sharding import PartitionSpec as P

domain_side = 5.0
cutoff = 12.0
soften = 0.25
reach = 2
sublanes = 8
degree = (0, 1, 1, 1, 2, 2, 2, 2, 2)
megabyte = 1024 * 1024
f32 = jnp.float32
bf16 = jnp.bfloat16


class Link:
    def __init__(self, step, bit, peers):
        self.step, self.bit, self.peers = step, bit, peers

    def delta(self, i):
        return self.step * (1 - 2 * ((i >> self.bit) & 1))

    def swap(self, value, axis):
        n = self.peers
        return lax.ppermute(value, axis, [(i, (i + self.delta(i)) % n) for i in range(n)])


def links_of(peers):
    assert peers % 4 == 0, peers
    steps = [(1, 0), (-1, 0), (2, 1)] + ([(-2, 1)] if peers > 4 else [])
    return [Link(step, bit, peers) for step, bit in steps]


def gx_spots_of(links):
    spots = [(0, None, 0)]
    for table, link in enumerate(links):
        spots.append((table + 1, link, 1))
        if link.peers == 4 and abs(link.step) == 2:
            spots.append((table + 1, link, -1))
    return spots


def pieces(x, count):
    out = []
    for _ in range(count):
        out.append(x.astype(bf16).astype(f32))
        x = x - out[-1]
    return out


def dot(a, b):
    return jnp.dot(a, b, preferred_element_type=f32)


def dot_rows(a, b):
    return lax.dot_general(a, b, (((1,), (1,)), ((), ())), preferred_element_type=f32)


def dot_cols(a, b):
    return lax.dot_general(a, b, (((0,), (0,)), ((), ())), preferred_element_type=f32)


def write_rows(store, gx_spots, at_x, lists, step_y, place, start, first_source=0):
    atoms = pairs = lists[0].shape[4]
    for slot, (table, link, sign) in enumerate(gx_spots):
        step_x = 0 if link is None else sign * link.delta(at_x)
        src, tgt, mask, spec = (ref[0, reach + step_x, reach + step_y] for ref in lists)
        store(0, start + slot * pairs, src + (first_source + table * atoms))
        store(1, start + slot * pairs, tgt + place * atoms)
        store(2, start + slot * pairs, mask)
        store(3, start + slot * pairs, spec)
        store(4, start + slot * pairs, jnp.full((1, pairs), step_x, jnp.int32))
        store(5, start + slot * pairs, jnp.full((1, pairs), -step_y, jnp.int32))


def pack_kernel(
    gx_spots, gy_links, pos_ref, feat_ref, cot_ref, src_ref, tgt_ref, mask_ref, spec_ref,
    gx_ref, y_ref, gy_ref,
):
    atoms, channels = feat_ref.shape[2:]
    pairs = src_ref.shape[4]
    parts = len(degree)
    zero = jnp.zeros((sublanes, channels), f32)
    for ref in (gx_ref, y_ref):
        ref[0:atoms] = feat_ref[0, 0]
        ref[atoms : atoms + sublanes] = zero
    for m in range(parts):
        gy_ref[m * atoms : (m + 1) * atoms] = cot_ref[0, 0, :, m * channels : (m + 1) * channels]
    gy_ref[parts * atoms :] = zero
    for axis in range(3):
        row = pos_ref[0, axis]
        gx_ref[atoms + axis : atoms + axis + 1, 0:atoms] = row
        y_ref[atoms + axis : atoms + axis + 1, 0:atoms] = row
        gy_ref[parts * atoms + axis : parts * atoms + axis + 1, 0:atoms] = row

    block = atoms + sublanes
    for start in range(block, y_ref.shape[0], sublanes):
        y_ref[start : start + sublanes] = zero

    def store(row, lane, value):
        chunk, lane = divmod(lane, channels)
        at = block + chunk * sublanes + row
        y_ref[at : at + 1, lane : lane + pairs] = value.astype(f32)

    at_x, at_y = lax.axis_index("gx"), lax.axis_index("gy")
    lists = (src_ref, tgt_ref, mask_ref, spec_ref)
    near, other = gy_links[0].delta(at_y), gy_links[1].delta(at_y)
    partner = at_y + near
    to_far = (partner + (partner >> 1)) & 1
    sources = (1 + max(table for table, _, _ in gx_spots)) * atoms
    slots = len(gx_spots) * pairs
    lane = 0
    for own, step_y, place in ((1, near, 0), (2, other, to_far)):
        base, chunks = partner_chunks(own * slots, slots, channels)
        start = lane + own * slots - base
        write_rows(store, gx_spots, at_x, lists, step_y, place, start, sources)
        lane += chunks * channels


def stack_kernel(rows, *refs):
    *refs, _, out_ref = refs
    for at, ref in enumerate(refs):
        out_ref[at * rows : (at + 1) * rows] = ref[0:rows]


def prep_kernel(
    gx_spots, gy_links, src_ref, tgt_ref, mask_ref, spec_ref, in_ref, emb_ref, out_ref,
    early_ref, late_ref, wide_ref, back_ref, first_ref, last_ref,
):
    pairs = src_ref.shape[4]
    at_x, at_y = lax.axis_index("gx"), lax.axis_index("gy")
    lists = (src_ref, tgt_ref, mask_ref, spec_ref)
    for rows_ref, links in ((early_ref, (None,)), (late_ref, (gy_links[2], gy_links[3]))):
        rows_ref[...] = jnp.zeros(rows_ref.shape, jnp.int32)

        def store(row, lane, value, rows_ref=rows_ref):
            rows_ref[row : row + 1, lane : lane + pairs] = value

        for place, link in enumerate(links):
            step_y = 0 if link is None else link.delta(at_y)
            write_rows(store, gx_spots, at_x, lists, step_y, place, place * len(gx_spots) * pairs)
    high, low = pieces(out_ref[...], 2)
    wide_ref[...] = jnp.concatenate([high, high, low], axis=0).T.astype(bf16)
    upper = jnp.concatenate([high, high], axis=1)
    lower = jnp.concatenate([low, jnp.zeros_like(low)], axis=1)
    back_ref[...] = jnp.concatenate([upper, lower], axis=0).astype(bf16)
    orders, hidden = in_ref.shape
    spare = jnp.zeros((sublanes * 2 - emb_ref.shape[0], hidden), f32)
    high, low = pieces(jnp.concatenate([in_ref[...], emb_ref[...], spare], axis=0), 2)
    first_ref[...] = jnp.concatenate([high, high, low], axis=0).T.astype(bf16)
    last_ref[...] = jnp.concatenate([high[0:orders], high[0:orders], low[0:orders]], axis=1).astype(bf16)


def radial_waves(dist, orders):
    order = (lax.broadcasted_iota(jnp.int32, (orders, 1), 0) + 1).astype(f32)
    turn = order * (dist * (1.0 / cutoff))
    whole = jnp.floor(turn + 0.5)
    part = turn - whole
    sign = 1.0 - 2.0 * (whole - 2.0 * jnp.floor(0.5 * whole))
    square = part * part
    sine = jnp.zeros_like(square)
    for k in (11, 9, 7, 5, 3, 1):
        sine = sine * square + (-1.0) ** (k // 2) * math.pi**k / math.factorial(k)
    cosine = jnp.zeros_like(square)
    for k in (12, 10, 8, 6, 4, 2, 0):
        cosine = cosine * square + (-1.0) ** (k // 2) * math.pi**k / math.factorial(k)
    return order, sign * part * sine, sign * cosine


def thrice(x):
    high, low = pieces(x, 2)
    return jnp.concatenate([high, low, high], axis=0).astype(bf16)


def lane_ids(rows, count):
    return lax.broadcasted_iota(jnp.int32, (rows, count), 1)


def onehot(ids, count):
    return jnp.where(lax.broadcasted_iota(jnp.int32, (count, ids.shape[1]), 0) == ids, 1.0, 0.0)


def slot_grads(rows, cot_refs, src_pos, feats, weights, orders):
    wide, back, first, last = weights
    slots = rows.shape[1]
    sources = src_pos.shape[1]
    channels = feats.shape[0] // 2
    hidden = last.shape[1] // 3
    parts = len(degree)
    atoms = (cot_refs[0].shape[0] - sublanes) // parts
    targets = atoms * len(cot_refs)

    src_hot = onehot(rows[0:1], sources).astype(bf16)
    tgt_hot = onehot(rows[1:2], targets).astype(bf16)
    mask = rows[2:3].astype(f32)
    offset = rows[4:6].astype(f32) * domain_side

    tgt_pos = [jnp.concatenate(pieces(ref[parts * atoms :, 0:atoms], 3), axis=0) for ref in cot_refs]
    gathered = dot(jnp.concatenate([feats, src_pos], axis=0), src_hot)
    from_src = gathered[2 * channels :]
    gathered = gathered[0:channels] + gathered[channels : 2 * channels]
    from_tgt = dot(jnp.concatenate(tgt_pos, axis=1).astype(bf16), tgt_hot)
    from_src = from_src[0:8] + from_src[8:16] + from_src[16:24]
    from_tgt = from_tgt[0:8] + from_tgt[8:16] + from_tgt[16:24]
    rel = [
        from_src[0:1] + offset[0:1] - from_tgt[0:1],
        from_src[1:2] + offset[1:2] - from_tgt[1:2],
        from_src[2:3] - from_tgt[2:3],
    ]
    dist = jnp.sqrt(rel[0] * rel[0] + rel[1] * rel[1] + rel[2] * rel[2] + soften)
    near = 1.0 / dist
    x, y, z = (r * near for r in rel)
    scaled = dist * (1.0 / cutoff)
    room = jnp.where(scaled < 1.0, 1.0 - scaled * scaled, 0.0)
    env = room * room * mask
    d_env = (-4.0 / cutoff) * scaled * room * mask

    order, sine, cosine = radial_waves(dist, orders)
    norm = math.sqrt(2.0 / cutoff)
    basis = norm * near * sine
    d_basis = norm * near * ((math.pi / cutoff) * order * cosine - sine * near)
    species = onehot(rows[3:4], 2 * sublanes)
    before = dot(first, thrice(jnp.concatenate([basis, species], axis=0)))
    gate = 1.0 / (1.0 + jnp.exp(-before))
    act = before * gate
    d_act = gate * (1.0 + before * (1.0 - gate))
    radial = dot(wide, thrice(act))
    root3, root5, root15 = math.sqrt(3.0), math.sqrt(5.0), math.sqrt(15.0)
    shapes = [
        None, root3 * x, root3 * y, root3 * z, root15 * x * y, root15 * y * z,
        0.5 * root5 * (2.0 * z * z - x * x - y * y), root15 * x * z, 0.5 * root15 * (x * x - y * y),
    ]
    twice = lax.broadcasted_iota(jnp.int32, (2 * targets, slots), 0)
    twice = (twice // (2 * atoms)) * atoms + lax.rem(twice, atoms)
    twice = jnp.where(twice == rows[1:2], 1.0, 0.0).astype(bf16)
    blocks = []
    for ref in cot_refs:
        block = [ref[m * atoms : (m + 1) * atoms] for m in range(parts)]
        blocks += pieces(jnp.concatenate(block, axis=1), 2)
    cots = dot_cols(jnp.concatenate(blocks, axis=0).astype(bf16), twice)
    d_shapes = [None] * parts
    d_radial = []
    through = None
    for low, high in ((0, 1), (1, 4), (4, 9)):
        l = len(d_radial)
        own = radial[l * channels : (l + 1) * channels]
        with_feats = own * gathered
        total = None
        for m in range(low, high):
            cot = cots[m * channels : (m + 1) * channels]
            if m:
                d_shapes[m] = jnp.sum(with_feats * cot, axis=0, keepdims=True) * env
                cot = cot * shapes[m]
            total = cot if total is None else total + cot
        d_radial.append(total * gathered)
        own = own * total
        through = own if through is None else through + own
    to_env = jnp.sum(through * gathered, axis=0, keepdims=True)
    through = through * env
    d_hidden = dot(back, jnp.concatenate(
        [p.astype(bf16) for p in pieces(jnp.concatenate(d_radial, axis=0), 2)], axis=0
    ))
    d_before = (d_hidden[0:hidden] + d_hidden[hidden:]) * (d_act * env)
    to_basis = dot(last, thrice(d_before))
    d_dist = jnp.sum(to_basis * d_basis, axis=0, keepdims=True) + to_env * d_env

    s = d_shapes
    d_x = root3 * s[1] + root15 * (y * s[4] + z * s[7] + x * s[8]) - root5 * x * s[6]
    d_y = root3 * s[2] + root15 * (x * s[4] + z * s[5] - y * s[8]) - root5 * y * s[6]
    d_z = root3 * s[3] + root15 * (y * s[5] + x * s[7]) + 2.0 * root5 * z * s[6]
    d_dist = d_dist - near * (x * d_x + y * d_y + z * d_z)
    grad = jnp.concatenate(
        [near * d_x + x * d_dist, near * d_y + y * d_dist, near * d_z + z * d_dist,
         jnp.zeros((sublanes - 3, slots), f32)], axis=0,
    )
    grad = jnp.concatenate(pieces(grad, 2), axis=0).astype(bf16)
    ids = rows.T
    src_home = jnp.where(lane_ids(slots, sources) == ids[:, 0:1], 1.0, 0.0).astype(bf16)
    tgt_home = jnp.where(lane_ids(slots, targets) == ids[:, 1:2], 1.0, 0.0).astype(bf16)
    pos_tgt = dot(grad, tgt_home)
    through = [p.astype(bf16) for p in pieces(through, 2)]
    home = dot(jnp.concatenate([*through, grad], axis=0), src_home)
    feat_src = (home[0:channels] + home[channels : 2 * channels]).T
    pos_src = home[2 * channels :]
    return pos_src[0:8] + pos_src[8:16], -(pos_tgt[0:8] + pos_tgt[8:16]), feat_src


def partner_chunks(first, slots, lanes):
    base = first // lanes * lanes
    return base, -(-(first + slots - base) // lanes)


def all_rows(rows_ref, y_ref, start, chunks):
    own = rows_ref[...]
    parts = [y_ref[start + at * sublanes : start + (at + 1) * sublanes] for at in range(chunks)]
    theirs = jnp.concatenate(parts, axis=1).astype(jnp.int32)
    base = own.shape[1] - theirs.shape[1]
    if base:
        theirs = jnp.concatenate([jnp.zeros((sublanes, base), jnp.int32), theirs], axis=1)
    return own + theirs


def early_kernel(orders, tables, start, chunks, rows_ref, *refs):
    refs = list(refs)
    weights = [refs.pop(0)[...] for _ in range(4)]
    y_ref = refs.pop(0)
    block_refs = [refs.pop(0) for _ in range(1 + max(ref for ref, _ in tables))]
    cot_ref, src_pos_ref, feats_ref, pos_ref, feat_ref, place = refs
    atoms = (cot_ref.shape[0] - sublanes) // len(degree)
    block = atoms + sublanes
    views = [block_refs[ref].at[at * block : (at + 1) * block] for ref, at in tables]
    for table, ref in enumerate(views):
        place[:, table * atoms : (table + 1) * atoms] = ref[atoms:, 0:atoms]
    src_pos_ref[...] = jnp.concatenate(pieces(place[...], 3), axis=0).astype(bf16)
    feats = jnp.concatenate([ref[0:atoms] for ref in views], axis=0).T
    feats_ref[...] = jnp.concatenate(pieces(feats, 2), axis=0).astype(bf16)
    rows = all_rows(rows_ref, y_ref, start, chunks)
    pos, pos_tgt, feat = slot_grads(
        rows, [cot_ref], src_pos_ref[...], feats_ref[...], weights, orders
    )
    feat_ref[...] = feat
    pos_ref[...] = pos
    pos_ref[:, 0:atoms] = pos[:, 0:atoms] + pos_tgt


def late_kernel(orders, homes, start, chunks, rows_ref, *refs):
    refs = list(refs)
    weights = [refs.pop(0)[...] for _ in range(4)]
    y_ref, src_pos_ref, feats_ref, held_pos, held_feat = (refs.pop(0) for _ in range(5))
    cot_refs = [refs.pop(0) for _ in range(2)]
    *outs, near_ref, far_ref = refs
    atoms = (cot_refs[0].shape[0] - sublanes) // len(degree)
    block = atoms + sublanes
    rows = all_rows(rows_ref, y_ref, start, chunks)
    pos, pos_tgt, feat = slot_grads(
        rows, cot_refs, src_pos_ref[...], feats_ref[...], weights, orders
    )
    pos = pos + held_pos[...]
    feat = feat + held_feat[...]
    for ref, home in zip(outs, homes):
        for at, table in enumerate(home):
            part = slice(table * atoms, (table + 1) * atoms)
            ref[at * block : at * block + atoms] = feat[part]
            ref[at * block + atoms : (at + 1) * block] = jnp.zeros((sublanes, ref.shape[1]), f32)
            ref[at * block + atoms : (at + 1) * block, 0:atoms] = pos[:, part]
    for at, ref in enumerate((near_ref, far_ref)):
        ref[...] = jnp.zeros(ref.shape, f32)
        ref[0:sublanes, 0:atoms] = pos_tgt[:, at * atoms : (at + 1) * atoms]


def add_kernel(count, *refs):
    total = refs[0][...]
    for ref in refs[1:count]:
        total = total + ref[...]
    rows = total.shape[0] // len(refs[count:])
    for at, ref in enumerate(refs[count:]):
        ref[...] = total[at * rows : (at + 1) * rows]


def sum_kernel(gx_count, *refs):
    gx_refs, gy_refs = refs[:gx_count], refs[gx_count:-2]
    pos_ref, feat_ref = refs[-2:]
    atoms = pos_ref.shape[3]
    feat = gx_refs[0][...]
    for ref in gx_refs[1:]:
        feat = feat + ref[...]
    pos = feat[atoms : atoms + 3, 0:atoms]
    for ref in gy_refs:
        pos = pos + ref[0:3, 0:atoms]
    for axis in range(3):
        pos_ref[0, axis] = pos[axis : axis + 1]
    feat_ref[0, 0] = feat[0:atoms]


vmem = pl.BlockSpec(memory_space=pltpu.VMEM)


def call(kernel, name, out_shape, operands, scratch=(), room=4, us=None):
    return pl.pallas_call(
        kernel,
        out_shape=out_shape,
        in_specs=[vmem] * len(operands),
        out_specs=(vmem,) * len(out_shape),
        scratch_shapes=list(scratch),
        compiler_params=pltpu.CompilerParams(vmem_limit_bytes=room and room * megabyte),
        name=name,
        cost_estimate=us and pl.CostEstimate(
            flops=int(us * 1e9), bytes_accessed=0, transcendentals=0
        ),
    )(*operands)


def diagonal(value, gx_link, gy_link):
    n, m = gx_link.peers, gy_link.peers
    pairs = []
    for i in range(n):
        for j in range(m):
            to = ((i + gx_link.delta(i)) % n) * m + (j + gy_link.delta(j)) % m
            pairs.append((i * m + j, to))
    return lax.ppermute(value, ("gx", "gy"), pairs)


def local(
    gx_size, gy_size, positions, features, cotangent, nbr_src, nbr_tgt, pair_mask, pair_species,
    w_in, species_emb, w_out,
):
    atoms, channels = features.shape[2:]
    steps, _, pairs = nbr_src.shape[2:]
    orders, hidden = w_in.shape
    slots = steps * pairs
    gx_links, gy_links = links_of(gx_size), links_of(gy_size)
    gx_spots = gx_spots_of(gx_links)
    sources = (len(gx_links) + 1) * atoms
    block = atoms + sublanes
    sds = jax.ShapeDtypeStruct

    by_axis = jnp.transpose(positions, (0, 2, 1, 3))
    lists = [jnp.transpose(x, (0, 2, 3, 1, 4)) for x in (nbr_src, nbr_tgt, pair_mask, pair_species)]
    gx_pack = sds((block, channels), f32)
    chunks = [partner_chunks(own * slots, slots, channels)[1] for own in (1, 2)]
    y_pack = sds((block + sum(chunks) * sublanes, channels), f32)
    gy_pack = sds((len(degree) * atoms + sublanes, channels), f32)
    own, y_own, cot_own = call(
        functools.partial(pack_kernel, gx_spots, gy_links), "pack", (gx_pack, y_pack, gy_pack),
        (by_axis, features, cotangent, *lists), room=None,
    )
    far_links = (gy_links[3], gy_links[2])
    y = gy_links[0].swap(y_own, "gy")
    many = len(gx_links) + 1
    tables = [(at, 0) if not l else (1 + l, at) for at in range(2) for l in range(many)]
    if gx_size == 4:
        homes = ((0, 3, many, many + 3), (1, 2, many + 1, many + 2))
    else:
        homes = tuple((table, many + table) for table in range(many))
    early_rows, late_rows, *weights = call(
        functools.partial(prep_kernel, gx_spots, gy_links),
        "prepare",
        (
            *(sds((sublanes, -(-n * slots // channels) * channels), jnp.int32) for n in (2, 3)),
            sds((w_out.shape[1], 3 * hidden), bf16),
            sds((2 * hidden, 2 * w_out.shape[1]), bf16),
            sds((hidden, 3 * (orders + 2 * sublanes)), bf16),
            sds((orders, 3 * hidden), bf16),
        ),
        (*lists, w_in, species_emb, w_out), us=3,
    )
    late_cot = lax.optimization_barrier((cot_own, weights[-1]))[0]
    cot_far, cot_near = (link.swap(late_cot, "gy") for link in far_links)
    (two,) = call(
        functools.partial(stack_kernel, block), "stack", (sds((2 * block, channels), f32),),
        (own, y, weights[-1]), us=2,
    )
    blocks = [own, y] + [link.swap(two, "gx") for link in gx_links]
    table = (
        sds((3 * sublanes, 2 * sources), bf16), sds((2 * channels, 2 * sources), bf16),
        sds((sublanes, 2 * sources), f32), sds((2 * sources, channels), f32),
    )
    held = call(
        functools.partial(early_kernel, orders, tables, block, chunks[0]), "early_tiles", table,
        (early_rows, *weights, y, *blocks, cot_own),
        [pltpu.VMEM((sublanes, 2 * sources), f32)], 24,
    )
    far_pack = sds((channels // 2, channels), f32)
    *sent, near, far = call(
        functools.partial(late_kernel, orders, homes, block + chunks[0] * sublanes, chunks[1]),
        "late_tiles",
        tuple(sds((len(home) * block, channels), f32) for home in homes) + (far_pack,) * 2,
        (late_rows, *weights, y, *held, cot_near, cot_far), room=24,
    )
    back_gy = [link.swap(value, "gy") for link, value in zip(far_links, (far, near))]
    if gx_size == 4:
        came = gx_links[0].swap(sent[1], "gx")
        own, x, y, xy = call(
            functools.partial(add_kernel, 2), "add", (gx_pack,) * 4, (sent[0], came)
        )
        back = [
            own, diagonal(xy, gx_links[2], gy_links[0]), gx_links[2].swap(x, "gx"),
            gy_links[0].swap(y, "gy"),
        ]
    else:
        came = [link.swap(value, "gx") for link, value in zip(gx_links, sent[1:])]
        own, y = call(
            functools.partial(add_kernel, len(sent)), "add", (gx_pack,) * 2, (sent[0], *came)
        )
        back = [own, gy_links[0].swap(y, "gy")]
    pos, feat = call(
        functools.partial(sum_kernel, len(back)), "sums",
        (sds(by_axis.shape, f32), sds(features.shape, f32)),
        (*back, *back_gy),
    )
    return jnp.transpose(pos, (0, 2, 1, 3)), feat


def solution(mesh):
    split = [P("gx", "gy")] * 7 + [P()] * 3
    return jax.shard_map(
        functools.partial(local, mesh.shape["gx"], mesh.shape["gy"]),
        mesh=mesh,
        in_specs=tuple(split),
        out_specs=(P("gx", "gy"), P("gx", "gy")),
        check_vma=False,
    )
```

```python
import functools
import math

import jax
import jax.numpy as jnp
from jax import lax
from jax.experimental import pallas as pl
from jax.experimental.pallas import tpu as pltpu
from jax.sharding import PartitionSpec as P

domain_side = 5.0
cutoff = 12.0
soften = 0.25
reach = 2
sublanes = 8
degree = (0, 1, 1, 1, 2, 2, 2, 2, 2)
megabyte = 1024 * 1024
f32 = jnp.float32
bf16 = jnp.bfloat16


class Link:
    def __init__(self, step, bit, peers):
        self.step, self.bit, self.peers = step, bit, peers

    def delta(self, i):
        return self.step * (1 - 2 * ((i >> self.bit) & 1))

    def swap(self, value, axis):
        n = self.peers
        return lax.ppermute(value, axis, [(i, (i + self.delta(i)) % n) for i in range(n)])


def links_of(peers):
    assert peers % 4 == 0, peers
    steps = [(1, 0), (-1, 0), (2, 1)] + ([(-2, 1)] if peers > 4 else [])
    return [Link(step, bit, peers) for step, bit in steps]


def gx_spots_of(links):
    spots = [(0, None, 0)]
    for table, link in enumerate(links):
        spots.append((table + 1, link, 1))
        if link.peers == 4 and abs(link.step) == 2:
            spots.append((table + 1, link, -1))
    return spots


def pieces(x, count):
    out = []
    for _ in range(count):
        out.append(x.astype(bf16).astype(f32))
        x = x - out[-1]
    return out


def dot(a, b):
    return jnp.dot(a, b, preferred_element_type=f32)


def dot_rows(a, b):
    return lax.dot_general(a, b, (((1,), (1,)), ((), ())), preferred_element_type=f32)


def dot_cols(a, b):
    return lax.dot_general(a, b, (((0,), (0,)), ((), ())), preferred_element_type=f32)


def write_rows(store, gx_spots, at_x, lists, step_y, place, start, first_source=0):
    atoms = pairs = lists[0].shape[4]
    for slot, (table, link, sign) in enumerate(gx_spots):
        step_x = 0 if link is None else sign * link.delta(at_x)
        src, tgt, mask, spec = (ref[0, reach + step_x, reach + step_y] for ref in lists)
        store(0, start + slot * pairs, src + (first_source + table * atoms))
        store(1, start + slot * pairs, tgt + place * atoms)
        store(2, start + slot * pairs, mask)
        store(3, start + slot * pairs, spec)
        store(4, start + slot * pairs, jnp.full((1, pairs), step_x, jnp.int32))
        store(5, start + slot * pairs, jnp.full((1, pairs), -step_y, jnp.int32))


def pack_kernel(
    gx_spots, gy_links, pos_ref, feat_ref, cot_ref, src_ref, tgt_ref, mask_ref, spec_ref,
    gx_ref, y_ref, gy_ref,
):
    atoms, channels = feat_ref.shape[2:]
    pairs = src_ref.shape[4]
    parts = len(degree)
    zero = jnp.zeros((sublanes, channels), f32)
    for ref in (gx_ref, y_ref):
        ref[0:atoms] = feat_ref[0, 0]
        ref[atoms : atoms + sublanes] = zero
    for m in range(parts):
        gy_ref[m * atoms : (m + 1) * atoms] = cot_ref[0, 0, :, m * channels : (m + 1) * channels]
    gy_ref[parts * atoms :] = zero
    for axis in range(3):
        row = pos_ref[0, axis]
        gx_ref[atoms + axis : atoms + axis + 1, 0:atoms] = row
        y_ref[atoms + axis : atoms + axis + 1, 0:atoms] = row
        gy_ref[parts * atoms + axis : parts * atoms + axis + 1, 0:atoms] = row

    block = atoms + sublanes
    for start in range(block, y_ref.shape[0], sublanes):
        y_ref[start : start + sublanes] = zero

    def store(row, lane, value):
        chunk, lane = divmod(lane, channels)
        at = block + chunk * sublanes + row
        y_ref[at : at + 1, lane : lane + pairs] = value.astype(f32)

    at_x, at_y = lax.axis_index("gx"), lax.axis_index("gy")
    lists = (src_ref, tgt_ref, mask_ref, spec_ref)
    near, other = gy_links[0].delta(at_y), gy_links[1].delta(at_y)
    partner = at_y + near
    to_far = (partner + (partner >> 1)) & 1
    sources = (1 + max(table for table, _, _ in gx_spots)) * atoms
    slots = len(gx_spots) * pairs
    lane = 0
    for own, step_y, place in ((1, near, 0), (2, other, to_far)):
        base, chunks = partner_chunks(own * slots, slots, channels)
        start = lane + own * slots - base
        write_rows(store, gx_spots, at_x, lists, step_y, place, start, sources)
        lane += chunks * channels


def stack_kernel(rows, *refs):
    *refs, _, out_ref = refs
    for at, ref in enumerate(refs):
        out_ref[at * rows : (at + 1) * rows] = ref[0:rows]


def prep_kernel(
    gx_spots, gy_links, src_ref, tgt_ref, mask_ref, spec_ref, in_ref, emb_ref, out_ref,
    early_ref, late_ref, wide_ref, back_ref, first_ref, last_ref,
):
    pairs = src_ref.shape[4]
    at_x, at_y = lax.axis_index("gx"), lax.axis_index("gy")
    lists = (src_ref, tgt_ref, mask_ref, spec_ref)
    for rows_ref, links in ((early_ref, (None,)), (late_ref, (gy_links[2], gy_links[3]))):
        rows_ref[...] = jnp.zeros(rows_ref.shape, jnp.int32)

        def store(row, lane, value, rows_ref=rows_ref):
            rows_ref[row : row + 1, lane : lane + pairs] = value

        for place, link in enumerate(links):
            step_y = 0 if link is None else link.delta(at_y)
            write_rows(store, gx_spots, at_x, lists, step_y, place, place * len(gx_spots) * pairs)
    high, low = pieces(out_ref[...], 2)
    wide_ref[...] = jnp.concatenate([high, high, low], axis=0).T.astype(bf16)
    upper = jnp.concatenate([high, high], axis=1)
    lower = jnp.concatenate([low, jnp.zeros_like(low)], axis=1)
    back_ref[...] = jnp.concatenate([upper, lower], axis=0).astype(bf16)
    orders, hidden = in_ref.shape
    spare = jnp.zeros((sublanes * 2 - emb_ref.shape[0], hidden), f32)
    high, low = pieces(jnp.concatenate([in_ref[...], emb_ref[...], spare], axis=0), 2)
    first_ref[...] = jnp.concatenate([high, high, low], axis=0).T.astype(bf16)
    last_ref[...] = jnp.concatenate([high[0:orders], high[0:orders], low[0:orders]], axis=1)


def radial_waves(dist, orders):
    order = (lax.broadcasted_iota(jnp.int32, (orders, 1), 0) + 1).astype(f32)
    turn = order * (dist * (1.0 / cutoff))
    whole = jnp.floor(turn + 0.5)
    part = turn - whole
    sign = 1.0 - 2.0 * (whole - 2.0 * jnp.floor(0.5 * whole))
    square = part * part
    sine = jnp.zeros_like(square)
    for k in (11, 9, 7, 5, 3, 1):
        sine = sine * square + (-1.0) ** (k // 2) * math.pi**k / math.factorial(k)
    cosine = jnp.zeros_like(square)
    for k in (12, 10, 8, 6, 4, 2, 0):
        cosine = cosine * square + (-1.0) ** (k // 2) * math.pi**k / math.factorial(k)
    return order, sign * part * sine, sign * cosine


def thrice(x):
    high, low = pieces(x, 2)
    return jnp.concatenate([high, low, high], axis=0).astype(bf16)


def lane_ids(rows, count):
    return lax.broadcasted_iota(jnp.int32, (rows, count), 1)


def onehot(ids, count):
    return jnp.where(lax.broadcasted_iota(jnp.int32, (count, ids.shape[1]), 0) == ids, 1.0, 0.0)


def slot_grads(rows, cot_refs, src_pos, feats, weights, orders):
    wide, back, first, last = weights
    slots = rows.shape[1]
    sources = src_pos.shape[1]
    channels = feats.shape[0] // 2
    hidden = last.shape[1] // 3
    parts = len(degree)
    atoms = (cot_refs[0].shape[0] - sublanes) // parts
    targets = atoms * len(cot_refs)

    src_hot = onehot(rows[0:1], sources).astype(bf16)
    tgt_hot = onehot(rows[1:2], targets).astype(bf16)
    mask = rows[2:3].astype(f32)
    offset = rows[4:6].astype(f32) * domain_side

    tgt_pos = [jnp.concatenate(pieces(ref[parts * atoms :, 0:atoms], 3), axis=0) for ref in cot_refs]
    gathered = dot(jnp.concatenate([feats, src_pos.astype(bf16)], axis=0), src_hot)
    from_src = gathered[2 * channels :]
    gathered = gathered[0:channels] + gathered[channels : 2 * channels]
    from_tgt = dot(jnp.concatenate(tgt_pos, axis=1).astype(bf16), tgt_hot)
    from_src = from_src[0:8] + from_src[8:16] + from_src[16:24]
    from_tgt = from_tgt[0:8] + from_tgt[8:16] + from_tgt[16:24]
    rel = [
        from_src[0:1] + offset[0:1] - from_tgt[0:1],
        from_src[1:2] + offset[1:2] - from_tgt[1:2],
        from_src[2:3] - from_tgt[2:3],
    ]
    dist = jnp.sqrt(rel[0] * rel[0] + rel[1] * rel[1] + rel[2] * rel[2] + soften)
    near = 1.0 / dist
    x, y, z = (r * near for r in rel)
    scaled = dist * (1.0 / cutoff)
    room = jnp.where(scaled < 1.0, 1.0 - scaled * scaled, 0.0)
    env = room * room * mask
    d_env = (-4.0 / cutoff) * scaled * room * mask

    order, sine, cosine = radial_waves(dist, orders)
    norm = math.sqrt(2.0 / cutoff)
    basis = norm * near * sine
    d_basis = norm * near * ((math.pi / cutoff) * order * cosine - sine * near)
    species = onehot(rows[3:4], 2 * sublanes)
    before = dot(first, thrice(jnp.concatenate([basis, species], axis=0)))
    gate = 1.0 / (1.0 + jnp.exp(-before))
    act = before * gate
    d_act = gate * (1.0 + before * (1.0 - gate))
    radial = dot(wide, thrice(act))
    root3, root5, root15 = math.sqrt(3.0), math.sqrt(5.0), math.sqrt(15.0)
    shapes = [
        None, root3 * x, root3 * y, root3 * z, root15 * x * y, root15 * y * z,
        0.5 * root5 * (2.0 * z * z - x * x - y * y), root15 * x * z, 0.5 * root15 * (x * x - y * y),
    ]
    twice = lax.broadcasted_iota(jnp.int32, (2 * targets, slots), 0)
    twice = (twice // (2 * atoms)) * atoms + lax.rem(twice, atoms)
    twice = jnp.where(twice == rows[1:2], 1.0, 0.0).astype(bf16)
    blocks = []
    for ref in cot_refs:
        block = [ref[m * atoms : (m + 1) * atoms] for m in range(parts)]
        blocks += pieces(jnp.concatenate(block, axis=1), 2)
    cots = dot_cols(jnp.concatenate(blocks, axis=0).astype(bf16), twice)
    d_shapes = [None] * parts
    d_radial = []
    through = None
    for low, high in ((0, 1), (1, 4), (4, 9)):
        l = len(d_radial)
        own = radial[l * channels : (l + 1) * channels]
        with_feats = own * gathered
        total = None
        for m in range(low, high):
            cot = cots[m * channels : (m + 1) * channels]
            if m:
                d_shapes[m] = jnp.sum(with_feats * cot, axis=0, keepdims=True) * env
                cot = cot * shapes[m]
            total = cot if total is None else total + cot
        d_radial.append(total * gathered)
        own = own * total
        through = own if through is None else through + own
    to_env = jnp.sum(through * gathered, axis=0, keepdims=True)
    through = through * env
    d_hidden = dot(back, jnp.concatenate(
        [p.astype(bf16) for p in pieces(jnp.concatenate(d_radial, axis=0), 2)], axis=0
    ))
    d_before = (d_hidden[0:hidden] + d_hidden[hidden:]) * (d_act * env)
    to_basis = dot(last.astype(bf16), thrice(d_before))
    d_dist = jnp.sum(to_basis * d_basis, axis=0, keepdims=True) + to_env * d_env

    s = d_shapes
    d_x = root3 * s[1] + root15 * (y * s[4] + z * s[7] + x * s[8]) - root5 * x * s[6]
    d_y = root3 * s[2] + root15 * (x * s[4] + z * s[5] - y * s[8]) - root5 * y * s[6]
    d_z = root3 * s[3] + root15 * (y * s[5] + x * s[7]) + 2.0 * root5 * z * s[6]
    d_dist = d_dist - near * (x * d_x + y * d_y + z * d_z)
    grad = jnp.concatenate(
        [near * d_x + x * d_dist, near * d_y + y * d_dist, near * d_z + z * d_dist,
         jnp.zeros((sublanes - 3, slots), f32)], axis=0,
    )
    grad = jnp.concatenate(pieces(grad, 2), axis=0).astype(bf16)
    ids = rows.T
    src_home = jnp.where(lane_ids(slots, sources) == ids[:, 0:1], 1.0, 0.0).astype(bf16)
    tgt_home = jnp.where(lane_ids(slots, targets) == ids[:, 1:2], 1.0, 0.0).astype(bf16)
    pos_tgt = dot(grad, tgt_home)
    through = [p.astype(bf16) for p in pieces(through, 2)]
    home = dot(jnp.concatenate([*through, grad], axis=0), src_home)
    feat_src = (home[0:channels] + home[channels : 2 * channels]).T
    pos_src = home[2 * channels :]
    return pos_src[0:8] + pos_src[8:16], -(pos_tgt[0:8] + pos_tgt[8:16]), feat_src


def partner_chunks(first, slots, lanes):
    base = first // lanes * lanes
    return base, -(-(first + slots - base) // lanes)


def all_rows(rows_ref, y_ref, start, chunks):
    own = rows_ref[...]
    parts = [y_ref[start + at * sublanes : start + (at + 1) * sublanes] for at in range(chunks)]
    theirs = jnp.concatenate(parts, axis=1).astype(jnp.int32)
    base = own.shape[1] - theirs.shape[1]
    if base:
        theirs = jnp.concatenate([jnp.zeros((sublanes, base), jnp.int32), theirs], axis=1)
    return own + theirs


def early_kernel(orders, tables, start, chunks, rows_ref, *refs):
    refs = list(refs)
    weights = [refs.pop(0)[...] for _ in range(4)]
    y_ref = refs.pop(0)
    block_refs = [refs.pop(0) for _ in range(1 + max(ref for ref, _ in tables))]
    cot_ref, src_pos_ref, feats_ref, pos_ref, feat_ref, place = refs
    atoms = (cot_ref.shape[0] - sublanes) // len(degree)
    block = atoms + sublanes
    views = [block_refs[ref].at[at * block : (at + 1) * block] for ref, at in tables]
    for table, ref in enumerate(views):
        place[:, table * atoms : (table + 1) * atoms] = ref[atoms:, 0:atoms]
    src_pos_ref[...] = jnp.concatenate(pieces(place[...], 3), axis=0)
    feats = jnp.concatenate([ref[0:atoms] for ref in views], axis=0).T
    feats_ref[...] = jnp.concatenate(pieces(feats, 2), axis=0).astype(bf16)
    rows = all_rows(rows_ref, y_ref, start, chunks)
    pos, pos_tgt, feat = slot_grads(
        rows, [cot_ref], src_pos_ref[...], feats_ref[...], weights, orders
    )
    feat_ref[...] = feat
    pos_ref[...] = pos
    pos_ref[:, 0:atoms] = pos[:, 0:atoms] + pos_tgt


def late_kernel(orders, homes, start, chunks, rows_ref, *refs):
    refs = list(refs)
    weights = [refs.pop(0)[...] for _ in range(4)]
    y_ref, src_pos_ref, feats_ref, held_pos, held_feat = (refs.pop(0) for _ in range(5))
    cot_refs = [refs.pop(0) for _ in range(2)]
    *outs, near_ref, far_ref = refs
    atoms = (cot_refs[0].shape[0] - sublanes) // len(degree)
    block = atoms + sublanes
    rows = all_rows(rows_ref, y_ref, start, chunks)
    pos, pos_tgt, feat = slot_grads(
        rows, cot_refs, src_pos_ref[...], feats_ref[...], weights, orders
    )
    pos = pos + held_pos[...]
    feat = feat + held_feat[...]
    for ref, home in zip(outs, homes):
        for at, table in enumerate(home):
            part = slice(table * atoms, (table + 1) * atoms)
            ref[at * block : at * block + atoms] = feat[part]
            ref[at * block + atoms : (at + 1) * block] = jnp.zeros((sublanes, ref.shape[1]), f32)
            ref[at * block + atoms : (at + 1) * block, 0:atoms] = pos[:, part]
    for at, ref in enumerate((near_ref, far_ref)):
        ref[...] = jnp.zeros(ref.shape, f32)
        ref[0:sublanes, 0:atoms] = pos_tgt[:, at * atoms : (at + 1) * atoms]


def add_kernel(count, *refs):
    total = refs[0][...]
    for ref in refs[1:count]:
        total = total + ref[...]
    rows = total.shape[0] // len(refs[count:])
    for at, ref in enumerate(refs[count:]):
        ref[...] = total[at * rows : (at + 1) * rows]


def sum_kernel(gx_count, *refs):
    gx_refs, gy_refs = refs[:gx_count], refs[gx_count:-2]
    pos_ref, feat_ref = refs[-2:]
    atoms = pos_ref.shape[3]
    feat = gx_refs[0][...]
    for ref in gx_refs[1:]:
        feat = feat + ref[...]
    pos = feat[atoms : atoms + 3, 0:atoms]
    for ref in gy_refs:
        pos = pos + ref[0:3, 0:atoms]
    for axis in range(3):
        pos_ref[0, axis] = pos[axis : axis + 1]
    feat_ref[0, 0] = feat[0:atoms]


vmem = pl.BlockSpec(memory_space=pltpu.VMEM)


def call(kernel, name, out_shape, operands, scratch=(), room=4, us=None):
    return pl.pallas_call(
        kernel,
        out_shape=out_shape,
        in_specs=[vmem] * len(operands),
        out_specs=(vmem,) * len(out_shape),
        scratch_shapes=list(scratch),
        compiler_params=pltpu.CompilerParams(vmem_limit_bytes=room and room * megabyte),
        name=name,
        cost_estimate=us and pl.CostEstimate(
            flops=int(us * 1e9), bytes_accessed=0, transcendentals=0
        ),
    )(*operands)


def diagonal(value, gx_link, gy_link):
    n, m = gx_link.peers, gy_link.peers
    pairs = []
    for i in range(n):
        for j in range(m):
            to = ((i + gx_link.delta(i)) % n) * m + (j + gy_link.delta(j)) % m
            pairs.append((i * m + j, to))
    return lax.ppermute(value, ("gx", "gy"), pairs)


def local(
    gx_size, gy_size, positions, features, cotangent, nbr_src, nbr_tgt, pair_mask, pair_species,
    w_in, species_emb, w_out,
):
    atoms, channels = features.shape[2:]
    steps, _, pairs = nbr_src.shape[2:]
    orders, hidden = w_in.shape
    slots = steps * pairs
    gx_links, gy_links = links_of(gx_size), links_of(gy_size)
    gx_spots = gx_spots_of(gx_links)
    sources = (len(gx_links) + 1) * atoms
    block = atoms + sublanes
    sds = jax.ShapeDtypeStruct

    by_axis = jnp.transpose(positions, (0, 2, 1, 3))
    lists = [jnp.transpose(x, (0, 2, 3, 1, 4)) for x in (nbr_src, nbr_tgt, pair_mask, pair_species)]
    gx_pack = sds((block, channels), f32)
    chunks = [partner_chunks(own * slots, slots, channels)[1] for own in (1, 2)]
    y_pack = sds((block + sum(chunks) * sublanes, channels), f32)
    gy_pack = sds((len(degree) * atoms + sublanes, channels), f32)
    own, y_own, cot_own = call(
        functools.partial(pack_kernel, gx_spots, gy_links), "pack", (gx_pack, y_pack, gy_pack),
        (by_axis, features, cotangent, *lists), room=None,
    )
    far_links = (gy_links[3], gy_links[2])
    y = gy_links[0].swap(y_own, "gy")
    many = len(gx_links) + 1
    tables = [(at, 0) if not l else (1 + l, at) for at in range(2) for l in range(many)]
    if gx_size == 4:
        homes = ((0, 3, many, many + 3), (1, 2, many + 1, many + 2))
    else:
        homes = tuple((table, many + table) for table in range(many))
    early_rows, late_rows, *weights = call(
        functools.partial(prep_kernel, gx_spots, gy_links),
        "prepare",
        (
            *(sds((sublanes, -(-n * slots // channels) * channels), jnp.int32) for n in (2, 3)),
            sds((w_out.shape[1], 3 * hidden), bf16),
            sds((2 * hidden, 2 * w_out.shape[1]), bf16),
            sds((hidden, 3 * (orders + 2 * sublanes)), bf16),
            sds((orders, 3 * hidden), f32),
        ),
        (*lists, w_in, species_emb, w_out), us=3,
    )
    late_cot = lax.optimization_barrier((cot_own, weights[-1]))[0]
    cot_far, cot_near = (link.swap(late_cot, "gy") for link in far_links)
    (two,) = call(
        functools.partial(stack_kernel, block), "stack", (sds((2 * block, channels), f32),),
        (own, y, weights[-1]), us=2,
    )
    blocks = [own, y] + [link.swap(two, "gx") for link in gx_links]
    table = (
        sds((3 * sublanes, 2 * sources), f32), sds((2 * channels, 2 * sources), bf16),
        sds((sublanes, 2 * sources), f32), sds((2 * sources, channels), f32),
    )
    held = call(
        functools.partial(early_kernel, orders, tables, block, chunks[0]), "early_tiles", table,
        (early_rows, *weights, y, *blocks, cot_own),
        [pltpu.VMEM((sublanes, 2 * sources), f32)], 24,
    )
    far_pack = sds((channels // 2, channels), f32)
    *sent, near, far = call(
        functools.partial(late_kernel, orders, homes, block + chunks[0] * sublanes, chunks[1]),
        "late_tiles",
        tuple(sds((len(home) * block, channels), f32) for home in homes) + (far_pack,) * 2,
        (late_rows, *weights, y, *held, cot_near, cot_far), room=24,
    )
    back_gy = [link.swap(value, "gy") for link, value in zip(far_links, (far, near))]
    if gx_size == 4:
        came = gx_links[0].swap(sent[1], "gx")
        own, x, y, xy = call(
            functools.partial(add_kernel, 2), "add", (gx_pack,) * 4, (sent[0], came)
        )
        back = [
            own, diagonal(xy, gx_links[2], gy_links[0]), gx_links[2].swap(x, "gx"),
            gy_links[0].swap(y, "gy"),
        ]
    else:
        came = [link.swap(value, "gx") for link, value in zip(gx_links, sent[1:])]
        own, y = call(
            functools.partial(add_kernel, len(sent)), "add", (gx_pack,) * 2, (sent[0], *came)
        )
        back = [own, gy_links[0].swap(y, "gy")]
    pos, feat = call(
        functools.partial(sum_kernel, len(back)), "sums",
        (sds(by_axis.shape, f32), sds(features.shape, f32)),
        (*back, *back_gy),
    )
    return jnp.transpose(pos, (0, 2, 1, 3)), feat


def solution(mesh):
    split = [P("gx", "gy")] * 7 + [P()] * 3
    return jax.shard_map(
        functools.partial(local, mesh.shape["gx"], mesh.shape["gy"]),
        mesh=mesh,
        in_specs=tuple(split),
        out_specs=(P("gx", "gy"), P("gx", "gy")),
        check_vma=False,
    )
```

```python
import functools
import math

import jax
import jax.numpy as jnp
from jax import lax
from jax.experimental import pallas as pl
from jax.experimental.pallas import tpu as pltpu
from jax.sharding import PartitionSpec as P

domain_side = 5.0
cutoff = 12.0
soften = 0.25
reach = 2
sublanes = 8
degree = (0, 1, 1, 1, 2, 2, 2, 2, 2)
megabyte = 1024 * 1024
f32 = jnp.float32
bf16 = jnp.bfloat16


class Link:
    def __init__(self, step, bit, peers):
        self.step, self.bit, self.peers = step, bit, peers

    def delta(self, i):
        return self.step * (1 - 2 * ((i >> self.bit) & 1))

    def swap(self, value, axis):
        n = self.peers
        return lax.ppermute(value, axis, [(i, (i + self.delta(i)) % n) for i in range(n)])


def links_of(peers):
    assert peers % 4 == 0, peers
    steps = [(1, 0), (-1, 0), (2, 1)] + ([(-2, 1)] if peers > 4 else [])
    return [Link(step, bit, peers) for step, bit in steps]


def gx_spots_of(links):
    spots = [(0, None, 0)]
    for table, link in enumerate(links):
        spots.append((table + 1, link, 1))
        if link.peers == 4 and abs(link.step) == 2:
            spots.append((table + 1, link, -1))
    return spots


def pieces(x, count):
    out = []
    for _ in range(count):
        out.append(x.astype(bf16).astype(f32))
        x = x - out[-1]
    return out


def dot(a, b):
    return jnp.dot(a, b, preferred_element_type=f32)


def dot_rows(a, b):
    return lax.dot_general(a, b, (((1,), (1,)), ((), ())), preferred_element_type=f32)


def dot_cols(a, b):
    return lax.dot_general(a, b, (((0,), (0,)), ((), ())), preferred_element_type=f32)


def write_rows(store, gx_spots, at_x, lists, step_y, place, start, first_source=0):
    atoms = pairs = lists[0].shape[4]
    for slot, (table, link, sign) in enumerate(gx_spots):
        step_x = 0 if link is None else sign * link.delta(at_x)
        src, tgt, mask, spec = (ref[0, reach + step_x, reach + step_y] for ref in lists)
        store(0, start + slot * pairs, src + (first_source + table * atoms))
        store(1, start + slot * pairs, tgt + place * atoms)
        store(2, start + slot * pairs, mask)
        store(3, start + slot * pairs, spec)
        store(4, start + slot * pairs, jnp.full((1, pairs), step_x, jnp.int32))
        store(5, start + slot * pairs, jnp.full((1, pairs), -step_y, jnp.int32))


def pack_kernel(
    gx_spots, gy_links, pos_ref, feat_ref, cot_ref, src_ref, tgt_ref, mask_ref, spec_ref,
    gx_ref, y_ref, gy_ref,
):
    atoms, channels = feat_ref.shape[2:]
    pairs = src_ref.shape[4]
    parts = len(degree)
    zero = jnp.zeros((sublanes, channels), f32)
    for ref in (gx_ref, y_ref):
        ref[0:atoms] = feat_ref[0, 0]
        ref[atoms : atoms + sublanes] = zero
    for m in range(parts):
        gy_ref[m * atoms : (m + 1) * atoms] = cot_ref[0, 0, :, m * channels : (m + 1) * channels]
    gy_ref[parts * atoms :] = zero
    for axis in range(3):
        row = pos_ref[0, axis]
        gx_ref[atoms + axis : atoms + axis + 1, 0:atoms] = row
        y_ref[atoms + axis : atoms + axis + 1, 0:atoms] = row
        gy_ref[parts * atoms + axis : parts * atoms + axis + 1, 0:atoms] = row

    block = atoms + sublanes
    for start in range(block, y_ref.shape[0], sublanes):
        y_ref[start : start + sublanes] = zero

    def store(row, lane, value):
        chunk, lane = divmod(lane, channels)
        at = block + chunk * sublanes + row
        y_ref[at : at + 1, lane : lane + pairs] = value.astype(f32)

    at_x, at_y = lax.axis_index("gx"), lax.axis_index("gy")
    lists = (src_ref, tgt_ref, mask_ref, spec_ref)
    near, other = gy_links[0].delta(at_y), gy_links[1].delta(at_y)
    partner = at_y + near
    to_far = (partner + (partner >> 1)) & 1
    sources = (1 + max(table for table, _, _ in gx_spots)) * atoms
    slots = len(gx_spots) * pairs
    lane = 0
    for own, step_y, place in ((1, near, 0), (2, other, to_far)):
        base, chunks = partner_chunks(own * slots, slots, channels)
        start = lane + own * slots - base
        write_rows(store, gx_spots, at_x, lists, step_y, place, start, sources)
        lane += chunks * channels


def stack_kernel(rows, *refs):
    *refs, _, out_ref = refs
    for at, ref in enumerate(refs):
        out_ref[at * rows : (at + 1) * rows] = ref[0:rows]


def prep_kernel(
    gx_spots, gy_links, src_ref, tgt_ref, mask_ref, spec_ref, in_ref, emb_ref, out_ref,
    early_ref, late_ref, wide_ref, back_ref, first_ref, last_ref,
):
    pairs = src_ref.shape[4]
    at_x, at_y = lax.axis_index("gx"), lax.axis_index("gy")
    lists = (src_ref, tgt_ref, mask_ref, spec_ref)
    for rows_ref, links in ((early_ref, (None,)), (late_ref, (gy_links[2], gy_links[3]))):
        rows_ref[...] = jnp.zeros(rows_ref.shape, jnp.int32)

        def store(row, lane, value, rows_ref=rows_ref):
            rows_ref[row : row + 1, lane : lane + pairs] = value

        for place, link in enumerate(links):
            step_y = 0 if link is None else link.delta(at_y)
            write_rows(store, gx_spots, at_x, lists, step_y, place, place * len(gx_spots) * pairs)
    high, low = pieces(out_ref[...], 2)
    wide_ref[...] = jnp.concatenate([high, high, low], axis=0).T.astype(bf16)
    upper = jnp.concatenate([high, high], axis=1)
    lower = jnp.concatenate([low, jnp.zeros_like(low)], axis=1)
    back_ref[...] = jnp.concatenate([upper, lower], axis=0).astype(bf16)
    orders, hidden = in_ref.shape
    spare = jnp.zeros((sublanes * 2 - emb_ref.shape[0], hidden), f32)
    high, low = pieces(jnp.concatenate([in_ref[...], emb_ref[...], spare], axis=0), 2)
    first_ref[...] = jnp.concatenate([high, high, low], axis=0).T.astype(bf16)
    last_ref[...] = jnp.concatenate([high[0:orders], high[0:orders], low[0:orders]], axis=1)


def radial_waves(dist, orders):
    order = (lax.broadcasted_iota(jnp.int32, (orders, 1), 0) + 1).astype(f32)
    turn = order * (dist * (1.0 / cutoff))
    whole = jnp.floor(turn + 0.5)
    part = turn - whole
    sign = 1.0 - 2.0 * (whole - 2.0 * jnp.floor(0.5 * whole))
    square = part * part
    sine = jnp.zeros_like(square)
    for k in (11, 9, 7, 5, 3, 1):
        sine = sine * square + (-1.0) ** (k // 2) * math.pi**k / math.factorial(k)
    cosine = jnp.zeros_like(square)
    for k in (12, 10, 8, 6, 4, 2, 0):
        cosine = cosine * square + (-1.0) ** (k // 2) * math.pi**k / math.factorial(k)
    return order, sign * part * sine, sign * cosine


def thrice(x):
    high, low = pieces(x, 2)
    return jnp.concatenate([high, low, high], axis=0).astype(bf16)


def lane_ids(rows, count):
    return lax.broadcasted_iota(jnp.int32, (rows, count), 1)


def onehot(ids, count):
    return jnp.where(lax.broadcasted_iota(jnp.int32, (count, ids.shape[1]), 0) == ids, 1.0, 0.0)


def slot_grads(rows, cot_refs, src_pos, feats, weights, orders):
    wide, back, first, last = weights
    slots = rows.shape[1]
    sources = src_pos.shape[1]
    channels = feats.shape[0] // 2
    hidden = last.shape[1] // 3
    parts = len(degree)
    atoms = (cot_refs[0].shape[0] - sublanes) // parts
    targets = atoms * len(cot_refs)

    src_hot = onehot(rows[0:1], sources).astype(bf16)
    tgt_hot = onehot(rows[1:2], targets).astype(bf16)
    mask = rows[2:3].astype(f32)
    offset = rows[4:6].astype(f32) * domain_side

    tgt_pos = [jnp.concatenate(pieces(ref[parts * atoms :, 0:atoms], 3), axis=0) for ref in cot_refs]
    gathered = dot(jnp.concatenate([feats, src_pos.astype(bf16)], axis=0), src_hot)
    from_src = gathered[2 * channels :]
    gathered = gathered[0:channels] + gathered[channels : 2 * channels]
    from_tgt = dot(jnp.concatenate(tgt_pos, axis=1).astype(bf16), tgt_hot)
    from_src = from_src[0:8] + from_src[8:16] + from_src[16:24]
    from_tgt = from_tgt[0:8] + from_tgt[8:16] + from_tgt[16:24]
    rel = [
        from_src[0:1] + offset[0:1] - from_tgt[0:1],
        from_src[1:2] + offset[1:2] - from_tgt[1:2],
        from_src[2:3] - from_tgt[2:3],
    ]
    dist = jnp.sqrt(rel[0] * rel[0] + rel[1] * rel[1] + rel[2] * rel[2] + soften)
    near = 1.0 / dist
    x, y, z = (r * near for r in rel)
    scaled = dist * (1.0 / cutoff)
    room = jnp.where(scaled < 1.0, 1.0 - scaled * scaled, 0.0)
    env = room * room * mask
    d_env = (-4.0 / cutoff) * scaled * room * mask

    order, sine, cosine = radial_waves(dist, orders)
    norm = math.sqrt(2.0 / cutoff)
    basis = norm * near * sine
    d_basis = norm * near * ((math.pi / cutoff) * order * cosine - sine * near)
    species = onehot(rows[3:4], 2 * sublanes)
    before = dot(first, thrice(jnp.concatenate([basis, species], axis=0)))
    gate = 1.0 / (1.0 + jnp.exp(-before))
    act = before * gate
    d_act = gate * (1.0 + before * (1.0 - gate))
    radial = dot(wide, thrice(act))
    root3, root5, root15 = math.sqrt(3.0), math.sqrt(5.0), math.sqrt(15.0)
    shapes = [
        None, root3 * x, root3 * y, root3 * z, root15 * x * y, root15 * y * z,
        0.5 * root5 * (2.0 * z * z - x * x - y * y), root15 * x * z, 0.5 * root15 * (x * x - y * y),
    ]
    twice = lax.broadcasted_iota(jnp.int32, (2 * targets, slots), 0)
    twice = (twice // (2 * atoms)) * atoms + lax.rem(twice, atoms)
    twice = jnp.where(twice == rows[1:2], 1.0, 0.0).astype(bf16)
    blocks = []
    for ref in cot_refs:
        block = [ref[m * atoms : (m + 1) * atoms] for m in range(parts)]
        blocks += pieces(jnp.concatenate(block, axis=1), 2)
    cots = dot_cols(jnp.concatenate(blocks, axis=0).astype(bf16), twice)
    d_shapes = [None] * parts
    d_radial = []
    through = None
    for low, high in ((0, 1), (1, 4), (4, 9)):
        l = len(d_radial)
        own = radial[l * channels : (l + 1) * channels]
        with_feats = own * gathered
        total = None
        for m in range(low, high):
            cot = cots[m * channels : (m + 1) * channels]
            if m:
                d_shapes[m] = jnp.sum(with_feats * cot, axis=0, keepdims=True) * env
                cot = cot * shapes[m]
            total = cot if total is None else total + cot
        d_radial.append(total * gathered)
        own = own * total
        through = own if through is None else through + own
    to_env = jnp.sum(through * gathered, axis=0, keepdims=True)
    through = through * env
    d_hidden = dot(back, jnp.concatenate(
        [p.astype(bf16) for p in pieces(jnp.concatenate(d_radial, axis=0), 2)], axis=0
    ))
    d_before = (d_hidden[0:hidden] + d_hidden[hidden:]) * (d_act * env)
    to_basis = dot(last.astype(bf16), thrice(d_before))
    d_dist = jnp.sum(to_basis * d_basis, axis=0, keepdims=True) + to_env * d_env

    s = d_shapes
    d_x = root3 * s[1] + root15 * (y * s[4] + z * s[7] + x * s[8]) - root5 * x * s[6]
    d_y = root3 * s[2] + root15 * (x * s[4] + z * s[5] - y * s[8]) - root5 * y * s[6]
    d_z = root3 * s[3] + root15 * (y * s[5] + x * s[7]) + 2.0 * root5 * z * s[6]
    d_dist = d_dist - near * (x * d_x + y * d_y + z * d_z)
    grad = jnp.concatenate(
        [near * d_x + x * d_dist, near * d_y + y * d_dist, near * d_z + z * d_dist,
         jnp.zeros((sublanes - 3, slots), f32)], axis=0,
    )
    grad = jnp.concatenate(pieces(grad, 2), axis=0).astype(bf16)
    ids = rows.T
    src_home = jnp.where(lane_ids(slots, sources) == ids[:, 0:1], 1.0, 0.0).astype(bf16)
    tgt_home = jnp.where(lane_ids(slots, targets) == ids[:, 1:2], 1.0, 0.0).astype(bf16)
    pos_tgt = dot(grad, tgt_home)
    through = [p.astype(bf16) for p in pieces(through, 2)]
    home = dot(jnp.concatenate([*through, grad], axis=0), src_home)
    feat_src = (home[0:channels] + home[channels : 2 * channels]).T
    pos_src = home[2 * channels :]
    return pos_src[0:8] + pos_src[8:16], -(pos_tgt[0:8] + pos_tgt[8:16]), feat_src


def partner_chunks(first, slots, lanes):
    base = first // lanes * lanes
    return base, -(-(first + slots - base) // lanes)


def all_rows(rows_ref, y_ref, start, chunks):
    own = rows_ref[...]
    parts = [y_ref[start + at * sublanes : start + (at + 1) * sublanes] for at in range(chunks)]
    theirs = jnp.concatenate(parts, axis=1).astype(jnp.int32)
    base = own.shape[1] - theirs.shape[1]
    if base:
        theirs = jnp.concatenate([jnp.zeros((sublanes, base), jnp.int32), theirs], axis=1)
    return own + theirs


def early_kernel(orders, tables, start, chunks, rows_ref, *refs):
    refs = list(refs)
    weights = [refs.pop(0)[...] for _ in range(4)]
    y_ref = refs.pop(0)
    block_refs = [refs.pop(0) for _ in range(1 + max(ref for ref, _ in tables))]
    cot_ref, src_pos_ref, feats_ref, pos_ref, feat_ref, place = refs
    atoms = (cot_ref.shape[0] - sublanes) // len(degree)
    block = atoms + sublanes
    views = [block_refs[ref].at[at * block : (at + 1) * block] for ref, at in tables]
    for table, ref in enumerate(views):
        place[:, table * atoms : (table + 1) * atoms] = ref[atoms:, 0:atoms]
    src_pos_ref[...] = jnp.concatenate(pieces(place[...], 3), axis=0)
    feats = jnp.concatenate([ref[0:atoms] for ref in views], axis=0).T
    feats_ref[...] = jnp.concatenate(pieces(feats, 2), axis=0).astype(bf16)
    rows = all_rows(rows_ref, y_ref, start, chunks)
    pos, pos_tgt, feat = slot_grads(
        rows, [cot_ref], src_pos_ref[...], feats_ref[...], weights, orders
    )
    feat_ref[...] = feat
    pos_ref[...] = pos
    pos_ref[:, 0:atoms] = pos[:, 0:atoms] + pos_tgt


def late_kernel(orders, homes, start, chunks, rows_ref, *refs):
    refs = list(refs)
    weights = [refs.pop(0)[...] for _ in range(4)]
    y_ref, src_pos_ref, feats_ref, held_pos, held_feat = (refs.pop(0) for _ in range(5))
    cot_refs = [refs.pop(0) for _ in range(2)][::-1]
    *outs, near_ref, far_ref = refs
    atoms = (cot_refs[0].shape[0] - sublanes) // len(degree)
    block = atoms + sublanes
    rows = all_rows(rows_ref, y_ref, start, chunks)
    pos, pos_tgt, feat = slot_grads(
        rows, cot_refs, src_pos_ref[...], feats_ref[...], weights, orders
    )
    pos = pos + held_pos[...]
    feat = feat + held_feat[...]
    for ref, home in zip(outs, homes):
        for at, table in enumerate(home):
            part = slice(table * atoms, (table + 1) * atoms)
            ref[at * block : at * block + atoms] = feat[part]
            ref[at * block + atoms : (at + 1) * block] = jnp.zeros((sublanes, ref.shape[1]), f32)
            ref[at * block + atoms : (at + 1) * block, 0:atoms] = pos[:, part]
    for at, ref in enumerate((near_ref, far_ref)):
        ref[...] = jnp.zeros(ref.shape, f32)
        ref[0:sublanes, 0:atoms] = pos_tgt[:, at * atoms : (at + 1) * atoms]


def add_kernel(count, *refs):
    total = refs[0][...]
    for ref in refs[1:count]:
        total = total + ref[...]
    rows = total.shape[0] // len(refs[count:])
    for at, ref in enumerate(refs[count:]):
        ref[...] = total[at * rows : (at + 1) * rows]


def sum_kernel(gx_count, *refs):
    gx_refs, gy_refs = refs[:gx_count], refs[gx_count:-2]
    pos_ref, feat_ref = refs[-2:]
    atoms = pos_ref.shape[3]
    feat = gx_refs[0][...]
    for ref in gx_refs[1:]:
        feat = feat + ref[...]
    pos = feat[atoms : atoms + 3, 0:atoms]
    for ref in gy_refs:
        pos = pos + ref[0:3, 0:atoms]
    for axis in range(3):
        pos_ref[0, axis] = pos[axis : axis + 1]
    feat_ref[0, 0] = feat[0:atoms]


vmem = pl.BlockSpec(memory_space=pltpu.VMEM)


def call(kernel, name, out_shape, operands, scratch=(), room=4, us=None):
    return pl.pallas_call(
        kernel,
        out_shape=out_shape,
        in_specs=[vmem] * len(operands),
        out_specs=(vmem,) * len(out_shape),
        scratch_shapes=list(scratch),
        compiler_params=pltpu.CompilerParams(vmem_limit_bytes=room and room * megabyte),
        name=name,
        cost_estimate=us and pl.CostEstimate(
            flops=int(us * 1e9), bytes_accessed=0, transcendentals=0
        ),
    )(*operands)


def diagonal(value, gx_link, gy_link):
    n, m = gx_link.peers, gy_link.peers
    pairs = []
    for i in range(n):
        for j in range(m):
            to = ((i + gx_link.delta(i)) % n) * m + (j + gy_link.delta(j)) % m
            pairs.append((i * m + j, to))
    return lax.ppermute(value, ("gx", "gy"), pairs)


def local(
    gx_size, gy_size, positions, features, cotangent, nbr_src, nbr_tgt, pair_mask, pair_species,
    w_in, species_emb, w_out,
):
    atoms, channels = features.shape[2:]
    steps, _, pairs = nbr_src.shape[2:]
    orders, hidden = w_in.shape
    slots = steps * pairs
    gx_links, gy_links = links_of(gx_size), links_of(gy_size)
    gx_spots = gx_spots_of(gx_links)
    sources = (len(gx_links) + 1) * atoms
    block = atoms + sublanes
    sds = jax.ShapeDtypeStruct

    by_axis = jnp.transpose(positions, (0, 2, 1, 3))
    lists = [jnp.transpose(x, (0, 2, 3, 1, 4)) for x in (nbr_src, nbr_tgt, pair_mask, pair_species)]
    gx_pack = sds((block, channels), f32)
    chunks = [partner_chunks(own * slots, slots, channels)[1] for own in (1, 2)]
    y_pack = sds((block + sum(chunks) * sublanes, channels), f32)
    gy_pack = sds((len(degree) * atoms + sublanes, channels), f32)
    own, y_own, cot_own = call(
        functools.partial(pack_kernel, gx_spots, gy_links), "pack", (gx_pack, y_pack, gy_pack),
        (by_axis, features, cotangent, *lists), room=None,
    )
    far_links = (gy_links[3], gy_links[2])
    y = gy_links[0].swap(y_own, "gy")
    many = len(gx_links) + 1
    tables = [(at, 0) if not l else (1 + many - l, at) for at in range(2) for l in range(many)]
    if gx_size == 4:
        homes = ((0, 3, many, many + 3), (1, 2, many + 1, many + 2))
    else:
        homes = tuple((table, many + table) for table in range(many))
    early_rows, late_rows, *weights = call(
        functools.partial(prep_kernel, gx_spots, gy_links),
        "prepare",
        (
            *(sds((sublanes, -(-n * slots // channels) * channels), jnp.int32) for n in (2, 3)),
            sds((w_out.shape[1], 3 * hidden), bf16),
            sds((2 * hidden, 2 * w_out.shape[1]), bf16),
            sds((hidden, 3 * (orders + 2 * sublanes)), bf16),
            sds((orders, 3 * hidden), f32),
        ),
        (*lists, w_in, species_emb, w_out), us=3,
    )
    (turn,) = call(
        functools.partial(stack_kernel, orders), "turn", (sds(w_in.shape, f32),), (w_in, w_in), us=3
    )
    late_cot = lax.optimization_barrier((cot_own, turn))[0]
    cot_far, cot_near = (link.swap(late_cot, "gy") for link in far_links)
    (two,) = call(
        functools.partial(stack_kernel, block), "stack", (sds((2 * block, channels), f32),),
        (own, y, turn), us=2,
    )
    blocks = [own, y] + [link.swap(two, "gx") for link in gx_links[::-1]]
    table = (
        sds((3 * sublanes, 2 * sources), f32), sds((2 * channels, 2 * sources), bf16),
        sds((sublanes, 2 * sources), f32), sds((2 * sources, channels), f32),
    )
    held = call(
        functools.partial(early_kernel, orders, tables, block, chunks[0]), "early_tiles", table,
        (early_rows, *weights, y, *blocks, cot_own),
        [pltpu.VMEM((sublanes, 2 * sources), f32)], 24,
    )
    far_pack = sds((channels // 2, channels), f32)
    *sent, near, far = call(
        functools.partial(late_kernel, orders, homes, block + chunks[0] * sublanes, chunks[1]),
        "late_tiles",
        tuple(sds((len(home) * block, channels), f32) for home in homes) + (far_pack,) * 2,
        (late_rows, *weights, y, *held, cot_far, cot_near), room=24,
    )
    back_gy = [link.swap(value, "gy") for link, value in zip(far_links, (far, near))]
    if gx_size == 4:
        came = gx_links[0].swap(sent[1], "gx")
        own, x, y, xy = call(
            functools.partial(add_kernel, 2), "add", (gx_pack,) * 4, (sent[0], came)
        )
        back = [
            own, diagonal(xy, gx_links[2], gy_links[0]), gy_links[0].swap(y, "gy"),
            gx_links[2].swap(x, "gx"),
        ]
    else:
        came = [link.swap(value, "gx") for link, value in zip(gx_links, sent[1:])]
        own, y = call(
            functools.partial(add_kernel, len(sent)), "add", (gx_pack,) * 2, (sent[0], *came)
        )
        back = [own, gy_links[0].swap(y, "gy")]
    pos, feat = call(
        functools.partial(sum_kernel, len(back)), "sums",
        (sds(by_axis.shape, f32), sds(features.shape, f32)),
        (*back, *back_gy),
    )
    return jnp.transpose(pos, (0, 2, 1, 3)), feat


def solution(mesh):
    split = [P("gx", "gy")] * 7 + [P()] * 3
    return jax.shard_map(
        functools.partial(local, mesh.shape["gx"], mesh.shape["gy"]),
        mesh=mesh,
        in_specs=tuple(split),
        out_specs=(P("gx", "gy"), P("gx", "gy")),
        check_vma=False,
    )
```
